32 devices in a mesh: img: 8 (over z, x), ch: 4 (over y, core).
Axes of the slice: x: 2, y: 2, z: 4, core: 2. Of those that a mesh axis runs over, the one named last changes fastest.
Arguments:
- tokens: bfloat16 [32, 576, 1024], P(('img', 'ch')), may hold values from -6 to 6
- features: bfloat16 [32, 1536, 1024], P('img', 'ch'), may hold values from -6 to 6
- sample_of: int32 [32], P(('img', 'ch')), may hold values from 0 to 11, never falling along the last dimension, each value on 1 to 4 neighbouring positions
- cotangent: bfloat16 [32, 576, 1024], P(('img', 'ch')), may hold values from -6 to 6
- ln1_gain: bfloat16 [1024], P(('img', 'ch')), may hold values from 0.5 to 1.5
- ln1_bias: bfloat16 [1024], P(('img', 'ch')), may hold values from -1.75 to 1.75
- w_qkv: bfloat16 [1024, 3072], P(('img', 'ch')), may hold values from -0.1875 to 0.1875
- bias_qv: bfloat16 [2048], P(('img', 'ch')), may hold values from -3 to 3
- w_attn_out: bfloat16 [1024, 1024], P(('img', 'ch')), may hold values from -0.75 to 0.75
- bias_attn_out: bfloat16 [1024], P(('img', 'ch')), may hold values from -3 to 3
- ln2_gain: bfloat16 [1024], P(('img', 'ch')), may hold values from 0.5 to 1.5
- ln2_bias: bfloat16 [1024], P(('img', 'ch')), may hold values from -1.75 to 1.75
- w_fc1: bfloat16 [1024, 4096], P(('img', 'ch')), may hold values from -0.1875 to 0.1875
- bias_fc1: bfloat16 [4096], P(('img', 'ch')), may hold values from -3 to 3
- w_fc2: bfloat16 [4096, 1024], P(('img', 'ch')), may hold values from -0.125 to 0.125
- bias_fc2: bfloat16 [1024], P(('img', 'ch')), may hold values from -3 to 3
- w_proj: bfloat16 [1536, 1024], P(('img', 'ch')), may hold values from -0.3125 to 0.3125
- bias_proj: bfloat16 [1024], P(('img', 'ch')), may hold values from -3 to 3
- w_depth: bfloat16 [9, 1024], P(None, ('img', 'ch')), may hold values from -2 to 2
- bias_depth: bfloat16 [1024], P(('img', 'ch')), may hold values from -3 to 3
- w_gate_in: bfloat16 [1024, 512], P(('img', 'ch')), may hold values from -0.375 to 0.375
- w_gate_out: bfloat16 [512, 1024], P(None, ('img', 'ch')), may hold values from -0.375 to 0.375
Outputs:
- layer_out: bfloat16 [32, 576, 1024], P(('img', 'ch'))
- grad_tokens: bfloat16 [32, 576, 1024], P(('img', 'ch'))
- grad_features: bfloat16 [32, 1536, 1024], P('img', 'ch')
- grad_ln1_gain: float32 [1024], P(('img', 'ch'))
- grad_ln1_bias: float32 [1024], P(('img', 'ch'))
- grad_w_qkv: float32 [1024, 3072], P(('img', 'ch'))
- grad_bias_qv: float32 [2048], P(('img', 'ch'))
- grad_w_attn_out: float32 [1024, 1024], P(('img', 'ch'))
- grad_bias_attn_out: float32 [1024], P(('img', 'ch'))
- grad_ln2_gain: float32 [1024], P(('img', 'ch'))
- grad_ln2_bias: float32 [1024], P(('img', 'ch'))
- grad_w_fc1: float32 [1024, 4096], P(('img', 'ch'))
- grad_bias_fc1: float32 [4096], P(('img', 'ch'))
- grad_w_fc2: float32 [4096, 1024], P(('img', 'ch'))
- grad_bias_fc2: float32 [1024], P(('img', 'ch'))
- grad_w_proj: float32 [1536, 1024], P(('img', 'ch'))
- grad_bias_proj: float32 [1024], P(('img', 'ch'))
- grad_w_depth: float32 [9, 1024], P(None, ('img', 'ch'))
- grad_bias_depth: float32 [1024], P(('img', 'ch'))
- grad_w_gate_in: float32 [1024, 512], P(('img', 'ch'))
- grad_w_gate_out: float32 [512, 1024], P(None, ('img', 'ch'))
- gate_mean: float32 [], replicated
The draws below stay inside these ranges and needn't reach their ends.
Inputs may be any that keep to these rules, and one draw needn't show every extreme that they name: `sample_of`: the images of one sample are consecutive; every sample has 1 to 4 images, and sample numbers never fall along the images.
All inputs are finite; a program needn't handle non-finite values.
Results may differ from the reference program's by a relative error of at most 0.012.
Values may be sent and summed in bfloat16 or wider, within the bound.
No kernel may reach another device: no remote copies, remote signals or barrier semaphores. Data moves between devices by JAX's collectives and lax.ppermute only.
A program may use at most 256 MiB of HBM per device.

```python
import math
import jax
import jax.numpy as jnp
import numpy as np
from jax import lax

D = 1024
HEAD = 64
FF = 4096
CH = 1536
GH = 512
PS = 24
FS = 32
TOK_IMG = 576
IMAGES = 32
SAMPLES = 12


def shard_levels(own_key, dims, pieces, least, high):
    def one(position, shards_of):
        draws = jax.random.uniform(jax.random.fold_in(jax.random.fold_in(own_key, 6), position), (shards_of,), jnp.float32, least / len(pieces), high / len(pieces))
        return jnp.repeat(jnp.exp(draws), dims[position] // shards_of).reshape((-1,) + (1,) * (len(dims) - position - 1))

    loudness = one(*pieces[0])
    for cut in pieces[1:]:
        loudness = loudness * one(*cut)
    return loudness


def profile(amount, total, bound, slope):
    loads = [(1 << 20) // math.isqrt(standing ** slope) + 1 for standing in range(2, amount + 1)]
    surplus, given = total - bound - (amount - 1), [1] * (amount - 1)
    while surplus > 0:
        free = [i for i in range(amount - 1) if given[i] < bound]
        mass, budget = sum([loads[i] for i in free]), surplus
        for i in free:
            addition = min(bound - given[i], max(1, budget * loads[i] // mass), surplus)
            given[i] = given[i] + addition
            surplus = surplus - addition
    return np.array([bound] + given)


def uneven_parts(own_key, amount, total, bound, skew):
    if amount == 2:
        one = jax.random.randint(own_key, (), max(1, total - bound), min(bound, total - 1) + 1)
        return jnp.stack([one, total - one])
    lengths = jnp.asarray(profile(amount, total, bound, skew), jnp.int32)
    twos = (amount - 1) // 2
    giver, sink = lengths[1:1 + 2 * twos:2], lengths[2:2 + 2 * twos:2]
    margin = jnp.minimum(giver - 1, bound - sink)
    passed = jax.random.randint(jax.random.fold_in(own_key, 1), (twos,), 0, 1 << 20) % (margin + 1)
    lengths = lengths.at[1:1 + 2 * twos:2].set(giver - passed).at[2:2 + 2 * twos:2].set(sink + passed)
    return lengths[jax.random.permutation(jax.random.fold_in(own_key, 2), amount)]


def normal_values(own_key, extent, scale, limit, shards=(), held_as=jnp.bfloat16):
    values = scale * jax.random.normal(own_key, extent, jnp.float32)
    if shards:
        values = values * shard_levels(own_key, extent, shards, -0.22, 0.18)
    return jnp.clip(values, -limit, limit).astype(held_as)


def setup_inputs(seed: int = 0) -> dict:
    seeds = jax.random.split(jax.random.key(seed), 23)
    return {
        "tokens": normal_values(seeds[0], (IMAGES, TOK_IMG, D), 1.0, 6.0, ((0, 32),)),
        "features": normal_values(seeds[1], (IMAGES, CH, FS * FS), 1.0, 6.0, ((0, 8), (1, 4))),
        "sample_of": jnp.searchsorted(jnp.cumsum(uneven_parts(seeds[2], SAMPLES, IMAGES, 4, 2)), jnp.arange(IMAGES), side="right").astype(jnp.int32),
        "cotangent": normal_values(seeds[3], (IMAGES, TOK_IMG, D), 1.0, 6.0, ((0, 32),)),
        "ln1_gain": jnp.clip(1.0 + 0.1 * jax.random.normal(seeds[4], (D,), jnp.float32), 0.5, 1.5).astype(jnp.bfloat16),
        "ln1_bias": normal_values(seeds[5], (D,), 0.3, 1.75, ((0, 32),)),
        "w_qkv": normal_values(seeds[6], (D, 3 * D), D ** -0.5, 0.1875, ((0, 32),)),
        "bias_qv": normal_values(seeds[7], (2 * D,), 0.5, 3.0, ((0, 32),)),
        "w_attn_out": normal_values(seeds[8], (D, D), (D // 16) ** -0.5, 0.75, ((0, 32),)),
        "bias_attn_out": normal_values(seeds[9], (D,), 0.5, 3.0, ((0, 32),)),
        "ln2_gain": jnp.clip(1.0 + 0.1 * jax.random.normal(seeds[10], (D,), jnp.float32), 0.5, 1.5).astype(jnp.bfloat16),
        "ln2_bias": normal_values(seeds[11], (D,), 0.3, 1.75, ((0, 32),)),
        "w_fc1": normal_values(seeds[12], (D, FF), D ** -0.5, 0.1875, ((0, 32),)),
        "bias_fc1": normal_values(seeds[13], (FF,), 0.5, 3.0, ((0, 32),)),
        "w_fc2": normal_values(seeds[14], (FF, D), (FF // 2) ** -0.5, 0.125, ((0, 32),)),
        "bias_fc2": normal_values(seeds[15], (D,), 0.5, 3.0, ((0, 32),)),
        "w_proj": normal_values(seeds[16], (CH, D), (CH // 4) ** -0.5, 0.3125, ((0, 32),)),
        "bias_proj": normal_values(seeds[17], (D,), 0.5, 3.0, ((0, 32),)),
        "w_depth": normal_values(seeds[18], (9, D), 9 ** -0.5, 2.0, ((1, 32),)),
        "bias_depth": normal_values(seeds[19], (D,), 0.5, 3.0, ((0, 32),)),
        "w_gate_in": normal_values(seeds[20], (D, GH), (D // 4) ** -0.5, 0.375, ((0, 32),)),
        "w_gate_out": normal_values(seeds[21], (GH, D), (GH // 2) ** -0.5, 0.375, ((1, 32),)),
    }


norm_eps = 1e-05
highest = lax.Precision.HIGHEST

@jax.custom_vjp
def low(v):
    return lax.optimization_barrier(v.astype(jnp.bfloat16)).astype(jnp.float32)

@jax.custom_vjp
def low_back(v):
    return v

def low_keep(v):
    return (low(v), None)

def low_pass(kept, grad):
    return (grad,)

def back_keep(v):
    return (v, None)

def back_low(kept, grad):
    return (low(grad),)
low.defvjp(low_keep, low_pass)
low_back.defvjp(back_keep, back_low)

def layer_norm(inputs, scale_gain, offset_bias):
    centre = lax.optimization_barrier(jnp.mean(inputs, axis=-1, keepdims=True))
    centred = inputs - centre
    spread = lax.optimization_barrier(jnp.mean(centred * centred, axis=-1, keepdims=True))
    return centred * lax.rsqrt(spread + norm_eps) * scale_gain + offset_bias

def pool_table(coarse_side, fine_side):
    coarse_index = jnp.arange(coarse_side)[:, None]
    fine_index = jnp.arange(fine_side)[None, :]
    window_start = coarse_index * fine_side // coarse_side
    window_end = ((coarse_index + 1) * fine_side + coarse_side - 1) // coarse_side
    inside = jnp.logical_and(fine_index >= window_start, fine_index < window_end)
    single = jnp.where(inside, 1.0, 0.0).astype(jnp.float32) / (window_end - window_start).astype(jnp.float32)
    return jnp.kron(single, single)

def depth_filter(projected, kernel, offset_bias):
    count_images = projected.shape[0]
    grid_cells = projected.reshape(count_images, PS, PS, -1)
    padded = jnp.pad(grid_cells, ((0, 0), (1, 1), (1, 1), (0, 0)))
    summed = jnp.zeros_like(grid_cells)
    for tap_row in range(3):
        for tap_col in range(3):
            summed = summed + padded[:, tap_row:tap_row + PS, tap_col:tap_col + PS, :] * kernel[3 * tap_row + tap_col]
    return summed.reshape(count_images, PS * PS, -1) + offset_bias

def gate_of(sample_mean, w_gate_in, w_gate_out):
    hidden_gate = jax.nn.gelu(jnp.dot(sample_mean, w_gate_in, precision=highest), approximate=False)
    return jnp.tanh(jnp.dot(hidden_gate, w_gate_out, precision=highest))

def vit_block(group_tok, params):
    ln1_gain, ln1_bias, w_qkv, bias_qv, w_attn_out, bias_attn_out, ln2_gain, ln2_bias, w_fc1, bias_fc1, w_fc2, bias_fc2 = params
    count_images, length_tok, model_width = group_tok.shape
    heads_count = model_width // HEAD
    head_shape = (count_images, length_tok, heads_count, HEAD)
    normed = low(layer_norm(group_tok, ln1_gain, ln1_bias))
    mixed_qkv = jnp.einsum('kpd,de->kpe', normed, w_qkv, precision=highest)
    query_heads = low(low_back(mixed_qkv[..., :model_width] + bias_qv[:model_width])).reshape(head_shape)
    key_heads = low(low_back(mixed_qkv[..., model_width:2 * model_width])).reshape(head_shape)
    value_heads = low(low_back(mixed_qkv[..., 2 * model_width:] + bias_qv[model_width:])).reshape(head_shape)
    scores = low_back(jnp.einsum('kqhe,kshe->khqs', query_heads, key_heads, precision=highest)) * HEAD ** (-0.5)
    largest = lax.optimization_barrier(jnp.max(scores, axis=-1, keepdims=True))
    lifted = jnp.exp(scores - largest)
    soft_weights = lifted / lax.optimization_barrier(jnp.sum(lifted, axis=-1, keepdims=True))
    attended = jnp.einsum('khqs,kshe->kqhe', low(soft_weights), value_heads, precision=highest)
    attended = low(low_back(attended.reshape(count_images, length_tok, model_width)))
    first_sum = group_tok + low_back(jnp.einsum('kpd,de->kpe', attended, w_attn_out, precision=highest) + bias_attn_out)
    normed2 = low(layer_norm(first_sum, ln2_gain, ln2_bias))
    pre_act = low_back(jnp.einsum('kpd,df->kpf', normed2, w_fc1, precision=highest) + bias_fc1)
    activation = low(jax.nn.gelu(pre_act, approximate=False))
    return first_sum + low_back(jnp.einsum('kpf,fd->kpd', activation, w_fc2, precision=highest) + bias_fc2)

def forward(tokens32, features32, params, sample_of):
    vit_params = params[:12]
    w_proj, bias_proj, w_depth, bias_depth, w_gate_in, w_gate_out = params[12:]
    grouped = tokens32.reshape(IMAGES // 4, 4, TOK_IMG, D)

    def one_group(group_tok):
        return vit_block(group_tok, vit_params)
    second_sum = lax.map(jax.checkpoint(one_group), grouped).reshape(IMAGES, TOK_IMG, D)
    table = pool_table(PS, FS)
    pooled = low(low_back(jnp.einsum('icf,pf->icp', features32, table, precision=highest)))
    projected = low_back(jnp.einsum('icp,cd->ipd', pooled, w_proj, precision=highest) + bias_proj)
    spatial = depth_filter(projected, w_depth, bias_depth)
    row_sums = lax.optimization_barrier(jnp.sum(spatial, axis=1))
    match = (sample_of[:, None] == sample_of[None, :]).astype(jnp.float32)
    counts = lax.optimization_barrier(jnp.sum(match, axis=1, keepdims=True))
    sample_mean = jnp.dot(match, row_sums, precision=highest) / (counts * TOK_IMG)
    gate = gate_of(sample_mean, w_gate_in, w_gate_out)
    layer = second_sum + gate[:, None, :] * spatial
    return (layer, jnp.mean(gate))

def reference(tokens, features, sample_of, cotangent, ln1_gain, ln1_bias, w_qkv, bias_qv, w_attn_out, bias_attn_out, ln2_gain, ln2_bias, w_fc1, bias_fc1, w_fc2, bias_fc2, w_proj, bias_proj, w_depth, bias_depth, w_gate_in, w_gate_out):
    params = tuple((item.astype(jnp.float32) for item in (ln1_gain, ln1_bias, w_qkv, bias_qv, w_attn_out, bias_attn_out, ln2_gain, ln2_bias, w_fc1, bias_fc1, w_fc2, bias_fc2, w_proj, bias_proj, w_depth, bias_depth, w_gate_in, w_gate_out)))

    def wrapped(tok_in, feat_in, param_in):
        return forward(tok_in, feat_in, param_in, sample_of)
    layer, pull_back, gate_mean = jax.vjp(wrapped, tokens.astype(jnp.float32), features.astype(jnp.float32), params, has_aux=True)
    d_tokens, d_features, d_params = pull_back(cotangent.astype(jnp.float32))
    g_ln1_gain, g_ln1_bias, g_qkv, g_bias_qv, g_attn_out, g_bias_attn_out, g_ln2_gain, g_ln2_bias, g_fc1, g_bias_fc1, g_fc2, g_bias_fc2, g_proj, g_bias_proj, g_depth, g_bias_depth, g_gate_in, g_gate_out = d_params
    return (layer.astype(jnp.bfloat16), d_tokens.astype(jnp.bfloat16), d_features.astype(jnp.bfloat16), g_ln1_gain, g_ln1_bias, g_qkv, g_bias_qv, g_attn_out, g_bias_attn_out, g_ln2_gain, g_ln2_bias, g_fc1, g_bias_fc1, g_fc2, g_bias_fc2, g_proj, g_bias_proj, g_depth, g_bias_depth, g_gate_in, g_gate_out, gate_mean)
```

```python
import jax
import jax.numpy as jnp
from jax import lax
from jax.experimental import pallas as pl
from jax.experimental.pallas import tpu as pltpu
from jax.sharding import PartitionSpec as P

HEAD = 64
PS = 24
FS = 32


norm_eps = 1e-05
highest = lax.Precision.HIGHEST


AXES = ("img", "ch")


class Grid:
    def __init__(self):
        img, ch = lax.axis_size("img"), lax.axis_size("ch")
        depth = 4 if img % 4 == 0 else 1
        self.n = {"z": depth, "x": img // depth, "y": ch // 2, "c": 2}
        self.stride = {"c": 1, "y": 2, "x": ch, "z": ch * (img // depth)}
        self.total = img * ch
        me = lax.axis_index(AXES)
        self.me = me
        self.pos = {a: lax.rem(lax.div(me, self.stride[a]), self.n[a]) for a in self.n}

    def send(self, v, axis, by):
        n, s = self.n[axis], self.stride[axis]
        pairs = []
        for i in range(self.total):
            a = (i // s) % n
            pairs.append((i, i + ((a + by) % n - a) * s))
        return lax.ppermute(v, AXES, pairs)

    def other(self, axis, by):
        return lax.rem(self.pos[axis] + by, self.n[axis])


def gather_small(grid, v):
    v = v[None]
    for axis in ("c", "y", "x", "z"):
        n = grid.n[axis]
        got = [v] + [grid.send(v, axis, k) for k in range(1, n)]
        ring = jnp.stack(got[::-1] + got[::-1])
        start = lax.rem(2 * n - 1 - grid.pos[axis], n)
        v = lax.dynamic_slice_in_dim(ring, start, n, 0).reshape(n * v.shape[0], v.shape[1])
    return v


def scatter_small(grid, v):
    for axis in ("c", "y", "x", "z")[::-1]:
        n = grid.n[axis]
        t = v.reshape(n, -1, v.shape[1])
        total = lax.dynamic_index_in_dim(t, grid.pos[axis], 0, keepdims=False)
        for k in range(1, n):
            total = total + grid.send(
                lax.dynamic_index_in_dim(t, grid.other(axis, k), 0, keepdims=False), axis, k
            )
        v = total
    return v[0]


def gather_pieces(grid, shard):
    r, width = shard.shape
    h, q = width // 2, width // 4
    c = grid.pos["c"]
    mine = lax.dynamic_slice(shard, (0, c * h), (r, h))
    theirs = lax.dynamic_slice(shard, (0, (1 - c) * h), (r, h))
    got = grid.send(theirs, "c", 1)
    both = jnp.where(
        c == 0, jnp.concatenate([mine, got], 0), jnp.concatenate([got, mine], 0)
    )
    along_z = [both] + [grid.send(both, "z", k) for k in range(1, grid.n["z"])]
    out = []
    for part, (first, second) in enumerate((("x", "y"), ("y", "x"))):
        s0 = jnp.stack([p[:, part * q : (part + 1) * q] for p in along_z])
        r1 = [grid.send(s0, first, k) for k in range(1, grid.n[first])]
        s1 = jnp.concatenate([s0] + r1, 0)
        r2 = [grid.send(s1, second, k) for k in range(1, grid.n[second])]
        out.append((first, second, s0, r1, r2))
    return out


def assemble(grid, cores, r, width):
    nz, nx, ny = grid.n["z"], grid.n["x"], grid.n["y"]
    h, q = width // 2, width // 4
    arrays, plan = [], []
    for core_rel, parts in enumerate(cores):
        for part, (first, second, s0, r1, r2) in enumerate(parts):
            for k1, buf in enumerate([s0] + r1):
                for kz in range(nz):
                    plan.append((len(arrays), kz, core_rel, part, kz, {first: k1, second: 0}))
                arrays.append(buf)
            for k2, buf in enumerate(r2, 1):
                for k1 in range(grid.n[first]):
                    for kz in range(nz):
                        rel = {first: k1, second: k2}
                        plan.append((len(arrays), k1 * nz + kz, core_rel, part, kz, rel))
                arrays.append(buf)

    def body(place, *refs):
        ins, out, sem = refs[: len(arrays)], refs[len(arrays)], refs[len(arrays) + 1]
        z, x, y, c = place[0], place[1], place[2], place[3]
        copies = []
        for i, j, core_rel, part, kz, rel in plan:
            zz = lax.rem(z - kz + nz, nz)
            xx = lax.rem(x - rel["x"] + nx, nx)
            yy = lax.rem(y - rel["y"] + ny, ny)
            col = lax.rem(c + core_rel, 2) * h + part * q
            if q % 128 == 0:
                col = pl.multiple_of(col, 128)
            copies.append(
                pltpu.make_async_copy(ins[i].at[j], out.at[zz, xx, yy, :, pl.ds(col, q)], sem)
            )
            copies[-1].start()
        for copy in copies:
            copy.wait()

    place = jnp.stack([grid.pos[a] for a in ("z", "x", "y", "c")]).astype(jnp.int32)
    whole = pl.pallas_call(
        body,
        out_shape=jax.ShapeDtypeStruct((nz, nx, ny, 2 * r, width), jnp.bfloat16),
        in_specs=[pl.BlockSpec(memory_space=pltpu.SMEM)]
        + [pl.BlockSpec(memory_space=pltpu.HBM)] * len(arrays),
        out_specs=pl.BlockSpec(memory_space=pltpu.VMEM),
        scratch_shapes=[pltpu.SemaphoreType.DMA],
        compiler_params=pltpu.CompilerParams(
            vmem_limit_bytes=nz * nx * ny * (2 * r + 16) * width * 2 + (4 << 20)
        ),
        cost_estimate=pl.CostEstimate(
            flops=0, bytes_accessed=nz * nx * ny * 2 * r * width * 4, transcendentals=0
        ),
        name="assemble",
    )(place, *arrays)
    return whole.reshape(nz * nx * ny * 2 * r, width)


def gather(grid, shard):
    own = gather_pieces(grid, shard)

    def over(buf):
        return grid.send(buf, "c", 1)

    away = [
        (first, second, over(s0), [over(b) for b in r1], [over(b) for b in r2])
        for first, second, s0, r1, r2 in own
    ]
    return assemble(grid, [own, away], *shard.shape)


def scatter(grid, mine, theirs, r):
    nz, nx, ny = grid.n["z"], grid.n["x"], grid.n["y"]
    f32 = jnp.float32
    h = mine.shape[1]
    q = h // 2
    got = grid.send(theirs, "c", 1)
    shape = (nz, nx, ny, 2 * r, h)
    base = mine.reshape(shape).astype(f32) + got.reshape(shape).astype(f32)
    parts = []
    for part, (first, second) in enumerate((("y", "x"), ("x", "y"))):
        total = base[..., part * q : (part + 1) * q]
        for axis, dim in ((first, {"x": 1, "y": 2}[first]), (second, 1)):
            t = total
            total = lax.dynamic_index_in_dim(t, grid.pos[axis], dim, keepdims=False)
            for k in range(1, grid.n[axis]):
                piece = lax.dynamic_index_in_dim(t, grid.other(axis, k), dim, keepdims=False)
                total = total + grid.send(piece.astype(jnp.bfloat16), axis, k).astype(f32)
        parts.append(total)
    t = jnp.concatenate(parts, -1)
    total = lax.dynamic_index_in_dim(t, grid.pos["z"], 0, keepdims=False)
    for k in range(1, nz):
        piece = lax.dynamic_index_in_dim(t, grid.other("z", k), 0, keepdims=False)
        total = total + grid.send(piece.astype(jnp.bfloat16), "z", k).astype(f32)
    c = grid.pos["c"]
    own = lax.dynamic_slice(total, (c * r, 0), (r, h))
    away = lax.dynamic_slice(total, ((1 - c) * r, 0), (r, h))
    back = grid.send(away, "c", 1)
    return jnp.where(
        c == 0, jnp.concatenate([own, back], 1), jnp.concatenate([back, own], 1)
    )


def weight_grad(grid, left, right):
    h = right.shape[1] // 2
    c = grid.pos["c"]

    def half(which):
        cols = lax.dynamic_slice(right, (0, which * h), (right.shape[0], h))
        return lax.dot_general(
            left, cols, (((0,), (0,)), ((), ())), preferred_element_type=jnp.float32
        ).astype(jnp.bfloat16)

    theirs = half(1 - c)
    return scatter(grid, half(c), theirs, left.shape[1] // grid.total)


def neighbours(grid, v, reach):
    out = [v]
    for offset in range(1, reach + 1):
        for by in (offset, -offset):
            pairs = [(i, i + by) for i in range(grid.total) if 0 <= i + by < grid.total]
            out.append(lax.ppermute(v, AXES, pairs))
    return out


def layer_norm(inputs, scale_gain, offset_bias):
    centre = jnp.mean(inputs, axis=-1, keepdims=True)
    centred = inputs - centre
    spread = jnp.mean(centred * centred, axis=-1, keepdims=True)
    return centred * lax.rsqrt(spread + norm_eps) * scale_gain + offset_bias


def pool_table(coarse_side, fine_side):
    coarse_index = jnp.arange(coarse_side)[:, None]
    fine_index = jnp.arange(fine_side)[None, :]
    window_start = coarse_index * fine_side // coarse_side
    window_end = ((coarse_index + 1) * fine_side + coarse_side - 1) // coarse_side
    inside = jnp.logical_and(fine_index >= window_start, fine_index < window_end)
    single = jnp.where(inside, 1.0, 0.0).astype(jnp.float32) / (window_end - window_start).astype(
        jnp.float32
    )
    return jnp.kron(single, single)


def depth_filter(projected, kernel, offset_bias):
    count_images = projected.shape[0]
    grid_cells = projected.reshape(count_images, PS, PS, -1)
    padded = jnp.pad(grid_cells, ((0, 0), (1, 1), (1, 1), (0, 0)))
    summed = jnp.zeros_like(grid_cells)
    for tap_row in range(3):
        for tap_col in range(3):
            summed = (
                summed
                + padded[:, tap_row : tap_row + PS, tap_col : tap_col + PS, :]
                * kernel[3 * tap_row + tap_col]
            )
    return summed.reshape(count_images, PS * PS, -1) + offset_bias


def gelu_exact(inputs):
    return jax.nn.gelu(inputs, approximate=False)


def attend(items):
    query_heads, key_heads, value_heads = items
    scores = jnp.einsum(
        "qhe,she->hqs", query_heads, key_heads, preferred_element_type=jnp.float32
    ) * HEAD ** (-0.5)
    largest = jnp.max(scores, axis=-1, keepdims=True)
    lifted = jnp.exp(scores - largest)
    summed = jnp.sum(lifted, axis=-1, keepdims=True)
    soft_weights = (lifted / summed).astype(jnp.bfloat16)
    attended = jnp.einsum(
        "hqs,she->qhe", soft_weights, value_heads, preferred_element_type=jnp.float32
    )
    return (attended.astype(jnp.bfloat16), largest + jnp.log(summed))


def attend_back(items):
    query_heads, key_heads, value_heads, log_total, d_attended = items
    scores = jnp.einsum(
        "qhe,she->hqs", query_heads, key_heads, preferred_element_type=jnp.float32
    ) * HEAD ** (-0.5)
    soft_full = jnp.exp(scores - log_total)
    soft_weights = soft_full.astype(jnp.bfloat16)
    d_value_heads = jnp.einsum(
        "hqs,qhe->she", soft_weights, d_attended, preferred_element_type=jnp.float32
    ).astype(jnp.bfloat16)
    d_soft = jnp.einsum("qhe,she->hqs", d_attended, value_heads, preferred_element_type=jnp.float32)
    inner = jnp.sum(soft_full * d_soft, axis=-1, keepdims=True)
    d_scores = (soft_full * (d_soft - inner) * HEAD ** (-0.5)).astype(jnp.bfloat16)
    d_query_heads = jnp.einsum(
        "hqs,she->qhe", d_scores, key_heads, preferred_element_type=jnp.float32
    ).astype(jnp.bfloat16)
    d_key_heads = jnp.einsum(
        "hqs,qhe->she", d_scores, query_heads, preferred_element_type=jnp.float32
    ).astype(jnp.bfloat16)
    return (d_query_heads, d_key_heads, d_value_heads)


def token_sum(values_in):
    return jnp.sum(values_in.astype(jnp.float32), axis=(0, 1))


def shards(
    tokens,
    features,
    sample_of,
    cotangent,
    ln1_gain,
    ln1_bias,
    w_qkv,
    bias_qv,
    w_attn_out,
    bias_attn_out,
    ln2_gain,
    ln2_bias,
    w_fc1,
    bias_fc1,
    w_fc2,
    bias_fc2,
    w_proj,
    bias_proj,
    w_depth,
    bias_depth,
    w_gate_in,
    w_gate_out,
):
    grid = Grid()
    rows = ln1_gain.shape[0]
    vectors = (
        ("ln1_gain", ln1_gain),
        ("ln1_bias", ln1_bias),
        ("bias_qv", bias_qv),
        ("bias_out", bias_attn_out),
        ("ln2_gain", ln2_gain),
        ("ln2_bias", ln2_bias),
        ("bias_fc1", bias_fc1),
        ("bias_fc2", bias_fc2),
        ("bias_proj", bias_proj),
        ("bias_depth", bias_depth),
        ("depth", w_depth.T.reshape(-1)),
    )
    every = gather_small(grid, jnp.concatenate([v for _, v in vectors])).astype(jnp.float32)
    full, spans, at = {}, {}, 0
    for name, v in vectors:
        spans[name] = (at, at + v.shape[0])
        full[name] = every[:, at : at + v.shape[0]].reshape(-1)
        at += v.shape[0]
    full_ln1_gain, full_ln1_bias, bias_pair = full["ln1_gain"], full["ln1_bias"], full["bias_qv"]
    full_bias_out, full_ln2_gain, full_ln2_bias = full["bias_out"], full["ln2_gain"], full["ln2_bias"]
    full_bias_fc1, full_bias_fc2 = full["bias_fc1"], full["bias_fc2"]
    full_bias_proj, full_bias_depth = full["bias_proj"], full["bias_depth"]
    full_depth = full["depth"].reshape(-1, 9).T
    full_qkv = gather(grid, w_qkv)
    full_proj = gather(grid, w_proj)
    mixed_w = gather(grid, jnp.concatenate([w_attn_out, w_gate_in, w_gate_out.T], 1))
    model_width = tokens.shape[2]
    gate_hidden = w_gate_in.shape[1]
    full_attn_out = mixed_w[:, :model_width]
    full_gate_in = mixed_w[:, model_width : model_width + gate_hidden].astype(jnp.float32)
    full_gate_out = mixed_w[:, model_width + gate_hidden :].astype(jnp.float32).T
    full_fc1 = gather(grid, w_fc1)
    full_fc2 = gather(grid, w_fc2)
    count_images = tokens.shape[0]
    length_tok = tokens.shape[1]
    heads_count = model_width // HEAD
    head_shape = (count_images, length_tok, heads_count, HEAD)
    reach = (3 + count_images - 1) // count_images
    inputs32 = tokens.astype(jnp.float32)
    normed1 = layer_norm(
        inputs32, full_ln1_gain, full_ln1_bias
    ).astype(jnp.bfloat16)
    mixed_qkv = jnp.einsum("kpd,de->kpe", normed1, full_qkv, preferred_element_type=jnp.float32)
    query_heads = (
        (mixed_qkv[..., :model_width] + bias_pair[:model_width])
        .astype(jnp.bfloat16)
        .reshape(head_shape)
    )
    key_heads = (
        mixed_qkv[..., model_width : 2 * model_width].astype(jnp.bfloat16).reshape(head_shape)
    )
    value_heads = (
        (mixed_qkv[..., 2 * model_width :] + bias_pair[model_width:])
        .astype(jnp.bfloat16)
        .reshape(head_shape)
    )
    attended, log_total = lax.map(attend, (query_heads, key_heads, value_heads))
    attended = attended.reshape(count_images, length_tok, model_width)
    first_sum = (
        inputs32
        + jnp.einsum("kpd,de->kpe", attended, full_attn_out, preferred_element_type=jnp.float32)
        + full_bias_out
    )
    normed2 = layer_norm(
        first_sum, full_ln2_gain, full_ln2_bias
    ).astype(jnp.bfloat16)
    pre_act = jnp.einsum(
        "kpd,df->kpf", normed2, full_fc1, preferred_element_type=jnp.float32
    ) + full_bias_fc1
    activation = gelu_exact(pre_act).astype(jnp.bfloat16)
    second_sum = (
        first_sum
        + jnp.einsum("kpf,fd->kpd", activation, full_fc2, preferred_element_type=jnp.float32)
        + full_bias_fc2
    )
    pool_weights = pool_table(PS, FS).T.astype(jnp.bfloat16)
    local_pooled = jnp.einsum(
        "kcf,fp->kcp", features, pool_weights, preferred_element_type=jnp.float32
    ).astype(jnp.bfloat16)
    pooled = lax.all_to_all(local_pooled, "ch", split_axis=0, concat_axis=1, tiled=True)
    projected = jnp.einsum(
        "kcp,cd->kpd", pooled, full_proj, preferred_element_type=jnp.float32
    ) + full_bias_proj
    spatial = depth_filter(
        projected, full_depth, full_bias_depth
    )
    row_sums = jnp.sum(spatial, axis=1)
    ids_plus = sample_of.astype(jnp.float32) + 1.0
    carried = jnp.concatenate([row_sums, jnp.broadcast_to(ids_plus[:, None], (count_images, 128))], 1)
    near = jnp.concatenate(neighbours(grid, carried, reach), axis=0)
    all_sums, all_ids = near[:, :model_width], near[:, model_width]
    match = (ids_plus[:, None] == all_ids[None, :]).astype(jnp.float32)
    counts = jnp.sum(match, axis=1, keepdims=True)
    sample_mean = jnp.dot(match, all_sums, precision=highest) / (counts * length_tok)
    hidden = jnp.dot(sample_mean, full_gate_in, precision=highest)
    gate_act, act_back = jax.vjp(gelu_exact, hidden)
    gate_values = jnp.tanh(jnp.dot(gate_act, full_gate_out, precision=highest))
    layer_out = (second_sum + gate_values[:, None, :] * spatial).astype(jnp.bfloat16)
    d_output = cotangent.astype(jnp.float32)
    d_gate = jnp.sum(d_output * spatial, axis=1)
    d_pre_gate = d_gate * (1.0 - gate_values * gate_values)
    d_hidden = act_back(jnp.dot(d_pre_gate, full_gate_out.T, precision=highest))[0]
    d_mean = jnp.dot(d_hidden, full_gate_in.T, precision=highest)
    gate_sum = jnp.broadcast_to(jnp.sum(gate_values), (128,))
    factors = gather_small(
        grid, jnp.concatenate([sample_mean[0], d_pre_gate[0], d_hidden[0], gate_act[0], gate_sum])
    )
    own_cols = grid.me * rows
    g_gate_in = lax.dot_general(
        lax.dynamic_slice(factors, (0, own_cols), (grid.total, rows)),
        factors[:, 2 * model_width : 2 * model_width + gate_hidden],
        (((0,), (0,)), ((), ())),
        precision=highest,
    )
    g_gate_out = lax.dot_general(
        factors[:, 2 * model_width + gate_hidden : 2 * model_width + 2 * gate_hidden],
        lax.dynamic_slice(factors, (0, model_width + own_cols), (grid.total, rows)),
        (((0,), (0,)), ((), ())),
        precision=highest,
    )
    gate_mean = jnp.sum(factors[:, -1]) / (grid.total * model_width)
    all_dmean = jnp.concatenate(neighbours(grid, d_mean, reach), axis=0)
    d_rows = jnp.dot(match, all_dmean, precision=highest) / (counts * length_tok)
    d_spatial = d_output * gate_values[:, None, :] + d_rows[:, None, :]
    depth_primal, depth_back = jax.vjp(
        depth_filter, projected, full_depth, full_bias_depth
    )
    d_projected, d_depth, d_bias_depth = depth_back(d_spatial)
    d_projected = d_projected.astype(jnp.bfloat16)
    d_bias_proj = token_sum(d_projected)
    g_proj = weight_grad(grid, pooled[0].T, d_projected[0])
    d_pooled = jnp.einsum(
        "kpd,cd->kcp", d_projected, full_proj, preferred_element_type=jnp.float32
    ).astype(jnp.bfloat16)
    d_local = lax.all_to_all(d_pooled, "ch", split_axis=1, concat_axis=0, tiled=True)
    grad_features = jnp.einsum(
        "kcp,fp->kcf", d_local, pool_weights, preferred_element_type=jnp.float32
    ).astype(jnp.bfloat16)
    d_bias_fc2 = jnp.sum(d_output, axis=(0, 1))
    g_fc2 = weight_grad(grid, activation[0], cotangent[0])
    d_activation = jnp.einsum(
        "kpd,fd->kpf", cotangent, full_fc2, preferred_element_type=jnp.float32
    )
    gelu_primal, gelu_back = jax.vjp(gelu_exact, pre_act)
    d_pre = gelu_back(d_activation)[0].astype(jnp.bfloat16)
    d_bias_fc1 = token_sum(d_pre)
    g_fc1 = weight_grad(grid, normed2[0], d_pre[0])
    d_normed2 = jnp.einsum("kpf,df->kpd", d_pre, full_fc1, preferred_element_type=jnp.float32)
    norm_primal, norm_two_back = jax.vjp(
        layer_norm, first_sum, full_ln2_gain, full_ln2_bias
    )
    d_first_norm, d_ln2_gain, d_ln2_bias = norm_two_back(d_normed2)
    d_first = d_output + d_first_norm
    d_branch = d_first.astype(jnp.bfloat16)
    d_bias_out = token_sum(d_branch)
    g_attn_out = weight_grad(grid, attended[0], d_branch[0])
    d_attended = (
        jnp.einsum("kpe,de->kpd", d_branch, full_attn_out, preferred_element_type=jnp.float32)
        .astype(jnp.bfloat16)
        .reshape(head_shape)
    )
    d_query_heads, d_key_heads, d_value_heads = lax.map(
        attend_back, (query_heads, key_heads, value_heads, log_total, d_attended)
    )
    flat_shape = (count_images, length_tok, model_width)
    d_query_flat = d_query_heads.reshape(flat_shape)
    d_value_flat = d_value_heads.reshape(flat_shape)
    d_bias_qv = jnp.concatenate([token_sum(d_query_flat), token_sum(d_value_flat)])
    d_mixed = jnp.concatenate(
        [d_query_flat, d_key_heads.reshape(flat_shape), d_value_flat], axis=-1
    )
    g_qkv = weight_grad(grid, normed1[0], d_mixed[0])
    d_normed1 = jnp.einsum("kpe,de->kpd", d_mixed, full_qkv, preferred_element_type=jnp.float32)
    norm_one_primal, norm_one_back = jax.vjp(
        layer_norm, inputs32, full_ln1_gain, full_ln1_bias
    )
    d_input_norm, d_ln1_gain, d_ln1_bias = norm_one_back(d_normed1)
    grad_tokens = (d_first + d_input_norm).astype(jnp.bfloat16)
    sums = {
        "ln1_gain": d_ln1_gain,
        "ln1_bias": d_ln1_bias,
        "bias_qv": d_bias_qv,
        "bias_out": d_bias_out,
        "ln2_gain": d_ln2_gain,
        "ln2_bias": d_ln2_bias,
        "bias_fc1": d_bias_fc1,
        "bias_fc2": d_bias_fc2,
        "bias_proj": d_bias_proj,
        "bias_depth": d_bias_depth,
        "depth": d_depth.T.reshape(-1),
    }
    summed = scatter_small(
        grid, jnp.concatenate([sums[name].reshape(grid.total, -1) for name, _ in vectors], 1)
    )
    g = {name: summed[spans[name][0] : spans[name][1]] for name, _ in vectors}
    return (
        layer_out,
        grad_tokens,
        grad_features,
        g["ln1_gain"],
        g["ln1_bias"],
        g_qkv,
        g["bias_qv"],
        g_attn_out,
        g["bias_out"],
        g["ln2_gain"],
        g["ln2_bias"],
        g_fc1,
        g["bias_fc1"],
        g_fc2,
        g["bias_fc2"],
        g_proj,
        g["bias_proj"],
        g["depth"].reshape(rows, 9).T,
        g["bias_depth"],
        g_gate_in,
        g_gate_out,
        gate_mean,
    )


def solution(mesh):
    return jax.shard_map(
        shards,
        mesh=mesh,
        in_specs=(
            P(("img", "ch"), None, None),
            P("img", "ch", None),
            P(("img", "ch")),
            P(("img", "ch"), None, None),
            P(("img", "ch")),
            P(("img", "ch")),
            P(("img", "ch"), None),
            P(("img", "ch")),
            P(("img", "ch"), None),
            P(("img", "ch")),
            P(("img", "ch")),
            P(("img", "ch")),
            P(("img", "ch"), None),
            P(("img", "ch")),
            P(("img", "ch"), None),
            P(("img", "ch")),
            P(("img", "ch"), None),
            P(("img", "ch")),
            P(None, ("img", "ch")),
            P(("img", "ch")),
            P(("img", "ch"), None),
            P(None, ("img", "ch")),
        ),
        out_specs=(
            P(("img", "ch"), None, None),
            P(("img", "ch"), None, None),
            P("img", "ch", None),
            P(("img", "ch")),
            P(("img", "ch")),
            P(("img", "ch"), None),
            P(("img", "ch")),
            P(("img", "ch"), None),
            P(("img", "ch")),
            P(("img", "ch")),
            P(("img", "ch")),
            P(("img", "ch"), None),
            P(("img", "ch")),
            P(("img", "ch"), None),
            P(("img", "ch")),
            P(("img", "ch"), None),
            P(("img", "ch")),
            P(None, ("img", "ch")),
            P(("img", "ch")),
            P(("img", "ch"), None),
            P(None, ("img", "ch")),
            P(),
        ),
        check_vma=False,
    )
```

```python
import functools
import math

import jax
import numpy as np
import jax.numpy as jnp
from jax import lax
from jax.experimental import pallas as pl
from jax.experimental.pallas import tpu as pltpu
from jax.sharding import PartitionSpec as P

HEAD = 64
PS = 24
FS = 32
REACH = 3
LN1_GAIN, LN1_BIAS, BIAS_OUT, LN2_GAIN, LN2_BIAS, BIAS_FC2, BIAS_PROJ, BIAS_DEPTH, DEPTH = range(9)
LINES = DEPTH + 9

norm_eps = 1e-05
highest = lax.Precision.HIGHEST
f32, bf16 = jnp.float32, jnp.bfloat16
AXES = ("img", "ch")
NN = (((1,), (0,)), ((), ()))
NT = (((1,), (1,)), ((), ()))
TN = (((0,), (0,)), ((), ()))


class Grid:
    def __init__(self):
        img, ch = lax.axis_size("img"), lax.axis_size("ch")
        depth = 4 if img % 4 == 0 else 1
        self.n = {"z": depth, "x": img // depth, "y": ch // 2, "c": 2}
        self.stride = {"c": 1, "y": 2, "x": ch, "z": ch * (img // depth)}
        self.total = img * ch
        me = lax.axis_index(AXES)
        self.me = me
        self.pos = {a: lax.rem(lax.div(me, self.stride[a]), self.n[a]) for a in self.n}

    def send(self, v, axis, by):
        n, s = self.n[axis], self.stride[axis]
        pairs = []
        for i in range(self.total):
            a = (i // s) % n
            pairs.append((i, i + ((a + by) % n - a) * s))
        return lax.ppermute(v, AXES, pairs)

    def other(self, axis, by):
        return lax.rem(self.pos[axis] + by, self.n[axis])


class GatherSmall:
    def __init__(self, grid, v):
        self.grid, self.v, self.left = grid, v[None], ["c", "y", "x", "z"]

    def next(self):
        axis = self.left.pop(0)
        n, v = self.grid.n[axis], self.v
        got = [v] + [self.grid.send(v, axis, k) for k in range(1, n)]
        ring = jnp.stack(got[::-1] + got[::-1])
        start = lax.rem(2 * n - 1 - self.grid.pos[axis], n)
        v = lax.dynamic_slice_in_dim(ring, start, n, 0)
        self.v = v.reshape(n * v.shape[1], v.shape[2])
        return self.v


class ScatterSmall:
    def __init__(self, grid, v):
        self.grid, self.v, self.left = grid, v, ["z", "x", "y", "c"]

    def next(self):
        axis = self.left.pop(0)
        g, n = self.grid, self.grid.n[axis]
        t = self.v.reshape(n, -1, self.v.shape[1])
        total = lax.dynamic_index_in_dim(t, g.pos[axis], 0, keepdims=False)
        for k in range(1, n):
            away = lax.dynamic_index_in_dim(t, g.other(axis, k), 0, keepdims=False)
            total = total + g.send(away, axis, k)
        self.v = total
        return self.v


def assemble(grid, cores, r, width):
    nz, nx, ny = grid.n["z"], grid.n["x"], grid.n["y"]
    q = width // 2
    arrays, plan = [], []
    for core_rel, parts in enumerate(cores):
        for part, (first, second, s0, r1, r2) in enumerate(parts):
            for k1, buf in enumerate([s0] + r1):
                for kz in range(nz):
                    plan.append((len(arrays), kz, core_rel, part, kz, {first: k1, second: 0}))
                arrays.append(buf)
            for k2, buf in enumerate(r2, 1):
                for k1 in range(grid.n[first]):
                    for kz in range(nz):
                        rel = {first: k1, second: k2}
                        plan.append((len(arrays), k1 * nz + kz, core_rel, part, kz, rel))
                arrays.append(buf)

    def body(place, *refs):
        ins, out, sem = refs[: len(arrays)], refs[len(arrays)], refs[len(arrays) + 1]
        z, x, y, c = place[0], place[1], place[2], place[3]
        copies = []
        for i, j, core_rel, part, kz, rel in plan:
            zz = lax.rem(z - kz + nz, nz)
            xx = lax.rem(x - rel["x"] + nx, nx)
            yy = lax.rem(y - rel["y"] + ny, ny)
            cc = lax.rem(c + core_rel, 2)
            copies.append(
                pltpu.make_async_copy(
                    ins[i].at[j], out.at[zz, xx, yy, cc, :, pl.ds(part * q, q)], sem
                )
            )
            copies[-1].start()
        for copy in copies:
            copy.wait()

    place = jnp.stack([grid.pos[a] for a in ("z", "x", "y", "c")]).astype(jnp.int32)
    rows = nz * nx * ny * 2 * r
    whole = pl.pallas_call(
        body,
        out_shape=jax.ShapeDtypeStruct((nz, nx, ny, 2, r, width), bf16),
        in_specs=[pl.BlockSpec(memory_space=pltpu.SMEM)]
        + [pl.BlockSpec(memory_space=pltpu.HBM)] * len(arrays),
        out_specs=pl.BlockSpec(memory_space=pltpu.VMEM),
        scratch_shapes=[pltpu.SemaphoreType.DMA],
        compiler_params=pltpu.CompilerParams(
            vmem_limit_bytes=nz * nx * ny * 2 * (r + 8) * width * 2 + (4 << 20)
        ),
        cost_estimate=pl.CostEstimate(
            flops=0, bytes_accessed=rows * width * 4, transcendentals=0
        ),
        name="assemble",
    )(place, *arrays)
    return whole.reshape(rows, width)


def after(value, done):
    return lax.optimization_barrier((value, done))[0]


class Gather:
    def __init__(self, grid, shard):
        self.grid, self.shard = grid, shard
        self.q = shard.shape[1] // 2

    def along_z(self):
        g = self.grid
        self.z = [self.shard] + [g.send(self.shard, "z", k) for k in range(1, g.n["z"])]

    def first(self):
        self.s0 = [
            jnp.stack([p[:, i * self.q : (i + 1) * self.q] for p in self.z]) for i in range(2)
        ]
        self.r1 = [self.every(self.s0[i], "xy"[i]) for i in range(2)]

    def second(self):
        self.r2 = [
            self.every(jnp.concatenate([self.s0[i]] + self.r1[i], 0), "yx"[i]) for i in range(2)
        ]
        self.c0 = [self.over(s) for s in self.s0]
        self.c1 = [[self.over(b) for b in r] for r in self.r1]

    def cross(self):
        self.c2 = [[self.over(b) for b in r] for r in self.r2]

    def every(self, v, axis):
        return [self.grid.send(v, axis, k) for k in range(1, self.grid.n[axis])]

    def over(self, v):
        return self.grid.send(v, "c", 1)


    def state(self):
        return {k: v for k, v in vars(self).items() if k not in ("grid", "q", "rows")}

    def set_state(self, state):
        for k, v in state.items():
            setattr(self, k, v)

    def whole(self):
        own = [("xy"[i], "yx"[i], self.s0[i], self.r1[i], self.r2[i]) for i in range(2)]
        away = [("xy"[i], "yx"[i], self.c0[i], self.c1[i], self.c2[i]) for i in range(2)]
        return assemble(self.grid, [own, away], *self.shard.shape)


def wgrad_body(n, r2, pos_ref, l0, l1, r0, r1, *outs):
    nx, ny = n
    o = dot(l0[...], r0[...], TN) + dot(l1[...], r1[...], TN)
    h = o.shape[1]
    q = h // 2
    o = o.reshape(nx, ny, r2, h)
    keep_a, keep_b = outs[0], outs[1]
    away_a, away_b = outs[2:2 + ny - 1], outs[2 + ny - 1:]
    for y in range(ny):
        @pl.when(pos_ref[1] == y)
        def _(y=y):
            keep_a[0] = o[:, y, :, :q].astype(bf16)
            for k in range(1, ny):
                away_a[k - 1][0] = o[:, (y + k) % ny, :, :q].astype(bf16)
    for x in range(nx):
        @pl.when(pos_ref[0] == x)
        def _(x=x):
            keep_b[0] = o[x, :, :, q:].astype(bf16)
            for k in range(1, nx):
                away_b[k - 1][0] = o[(x + k) % nx, :, :, q:].astype(bf16)

def wgrad(place, n, left, left_peer, right, right_peer):
    nz, nx, ny = n
    t, rows = left.shape
    h = right_peer.shape[1]
    q = h // 2
    r2 = rows // (nz * nx * ny)
    part = pl.BlockSpec((t, rows // nz), lambda i, p: (0, i))
    a = jax.ShapeDtypeStruct((nz, nx, r2, q), bf16)
    b = jax.ShapeDtypeStruct((nz, ny, r2, q), bf16)
    sa = pl.BlockSpec((1, nx, r2, q), lambda i, p: (i, 0, 0, 0))
    sb = pl.BlockSpec((1, ny, r2, q), lambda i, p: (i, 0, 0, 0))
    return pl.pallas_call(
        functools.partial(wgrad_body, (nx, ny), r2),
        grid_spec=pltpu.PrefetchScalarGridSpec(
            num_scalar_prefetch=1, grid=(nz,),
            in_specs=[part, part, pl.BlockSpec((t, h), lambda i, p: (0, p[2])), pl.BlockSpec((t, h), lambda i, p: (0, 0))],
            out_specs=[sa, sb] + [sa] * (ny - 1) + [sb] * (nx - 1)),
        out_shape=[a, b] + [a] * (ny - 1) + [b] * (nx - 1),
        compiler_params=pltpu.CompilerParams(vmem_limit_bytes=56 << 20),
        name="weight_grad",
    )(place, left, left_peer, right, right_peer)


class Scatter:
    def __init__(self, grid, left, left_peer, right, right_peer):
        self.grid, self.rows = grid, left.shape[1] // grid.total
        n = grid.n
        place = jnp.stack([grid.pos[a] for a in ("x", "y", "c")]).astype(jnp.int32)
        sums = wgrad(place, (n["z"], n["x"], n["y"]), left, left_peer, right, right_peer)
        self.keep = list(sums[:2])
        self.away = [list(sums[2 : 1 + n["y"]]), list(sums[1 + n["y"] :])]

    state, set_state = Gather.state, Gather.set_state

    def first(self):
        self.got = [
            [self.grid.send(v, "yx"[i], k) for k, v in enumerate(self.away[i], 1)] for i in range(2)
        ]
        del self.away

    def total(self, i, at):
        terms = [
            lax.dynamic_index_in_dim(t, at, 1, keepdims=False).astype(f32)
            for t in [self.keep[i]] + self.got[i]
        ]
        return functools.reduce(jnp.add, terms)

    def second(self):
        g = self.grid
        self.more = []
        for i, axis in enumerate("xy"):
            self.more.append(
                [
                    g.send(self.total(i, g.other(axis, k)).astype(bf16), axis, k)
                    for k in range(1, g.n[axis])
                ]
            )

    def along_z(self):
        g = self.grid
        halves = []
        for i, axis in enumerate("xy"):
            terms = [self.total(i, g.pos[axis])] + [t.astype(f32) for t in self.more[i]]
            halves.append(functools.reduce(jnp.add, terms))

        def at(z):
            return [lax.dynamic_index_in_dim(t, z, 0, keepdims=False) for t in halves]

        self.kept = [jnp.concatenate(at(g.pos["z"]), 1)]
        for k in range(1, g.n["z"]):
            away = jnp.concatenate([t.astype(bf16) for t in at(g.other("z", k))], 1)
            self.kept.append(g.send(away, "z", k))
        del self.keep, self.got, self.more

    def last(self):
        total = functools.reduce(jnp.add, [t.astype(f32) for t in self.kept])
        r, c = self.rows, self.grid.pos["c"]
        self.own = lax.dynamic_slice_in_dim(total, c * r, r, 0)
        self.back = self.grid.send(lax.dynamic_slice_in_dim(total, (1 - c) * r, r, 0), "c", 1)
        del self.kept

    def result(self):
        pair = (self.own, self.back)
        return jnp.where(
            self.grid.pos["c"] == 0, jnp.concatenate(pair, 1), jnp.concatenate(pair[::-1], 1)
        )


def neighbours(grid, v, reach):
    out = [v]
    for offset in range(1, reach + 1):
        for by in (offset, -offset):
            pairs = [(i, i + by) for i in range(grid.total) if 0 <= i + by < grid.total]
            out.append(lax.ppermute(v, AXES, pairs))
    return out


def layer_norm(inputs, scale_gain, offset_bias):
    centre = jnp.mean(inputs, axis=-1, keepdims=True)
    centred = inputs - centre
    spread = jnp.mean(centred * centred, axis=-1, keepdims=True)
    return centred * lax.rsqrt(spread + norm_eps) * scale_gain + offset_bias


def dot(a, b, dims=NN):
    return lax.dot_general(a, b, dims, preferred_element_type=f32)

def attend_body(q_ref, k_ref, v_ref, o_ref, lse_ref):
    t = q_ref.shape[0]
    first = lax.broadcasted_iota(jnp.int32, (t, 2 * HEAD), 1) < HEAD
    q, k, v = q_ref[...], k_ref[...], v_ref[...]
    out, totals = [], []
    for side in range(2):
        keep = first if side == 0 else jnp.logical_not(first)
        s = dot(q, jnp.where(keep, k, jnp.zeros_like(k)), NT)
        top = jnp.max(s, axis=-1, keepdims=True)
        p = jnp.exp((s - top) * HEAD ** -0.5)
        total = jnp.sum(p, axis=-1, keepdims=True)
        o = dot((p * (1.0 / total)).astype(bf16), jnp.where(keep, v, jnp.zeros_like(v)))
        out.append(o)
        totals.append(top * HEAD ** -0.5 + jnp.log(total))
    o_ref[...] = (out[0] + out[1]).astype(bf16)
    lse_ref[...] = jnp.where(first, totals[0], totals[1])

def attend(qkv):
    t, width = qkv.shape
    n = width // 3 // (2 * HEAD)
    spec = lambda off: pl.BlockSpec((t, 2 * HEAD), lambda i, off=off: (0, off * n + i))
    return pl.pallas_call(
        attend_body, grid=(n,),
        in_specs=[spec(0), spec(1), spec(2)],
        out_specs=[spec(0), spec(0)],
        out_shape=[jax.ShapeDtypeStruct((t, width // 3), bf16), jax.ShapeDtypeStruct((t, width // 3), f32)],
        compiler_params=pltpu.CompilerParams(vmem_limit_bytes=48 << 20),
        cost_estimate=pl.CostEstimate(flops=4 * t * t * width // 3, bytes_accessed=t * width * 4, transcendentals=t * t * 16),
        name="attend",
    )(qkv, qkv, qkv)

def attend_back_body(q_ref, k_ref, v_ref, do_ref, lse_ref, dq_ref, dk_ref, dv_ref):
    t = q_ref.shape[0]
    first = lax.broadcasted_iota(jnp.int32, (t, 2 * HEAD), 1) < HEAD
    q, k, v, do = q_ref[...], k_ref[...], v_ref[...], do_ref[...]
    zero = jnp.zeros_like(k)
    dq = dk = dv = None
    for side in range(2):
        keep = first if side == 0 else jnp.logical_not(first)
        km, vm = jnp.where(keep, k, zero), jnp.where(keep, v, zero)
        qm, dom = jnp.where(keep, q, zero), jnp.where(keep, do, zero)
        lse = lse_ref[:, side * HEAD:side * HEAD + 1]
        p = jnp.exp(dot(q, km, NT) * HEAD ** -0.5 - lse)
        dp = dot(do, vm, NT)
        inner = jnp.sum(p * dp, axis=-1, keepdims=True)
        ds = (p * ((dp - inner) * HEAD ** -0.5)).astype(bf16)
        dq_ = dot(ds, km)
        dv_ = dot(dom, p.astype(bf16), TN)
        dk_ = dot(qm, ds, TN)
        dq = dq_ if dq is None else dq + dq_
        dv = dv_ if dv is None else dv + dv_
        dk = dk_ if dk is None else dk + dk_
    dq_ref[...] = dq.astype(bf16)
    dk_ref[...] = dk.T.astype(bf16)
    dv_ref[...] = dv.T.astype(bf16)

def attend_back(qkv, d_attended, lse):
    t, width = qkv.shape
    n = width // 3 // (2 * HEAD)
    spec = lambda off: pl.BlockSpec((t, 2 * HEAD), lambda i, off=off: (0, off * n + i))
    shape = jax.ShapeDtypeStruct((t, width // 3), bf16)
    return pl.pallas_call(
        attend_back_body, grid=(n,),
        in_specs=[spec(0), spec(1), spec(2), spec(0), spec(0)],
        out_specs=[spec(0)] * 3,
        out_shape=[shape] * 3,
        compiler_params=pltpu.CompilerParams(vmem_limit_bytes=48 << 20),
        cost_estimate=pl.CostEstimate(flops=10 * t * t * width // 3, bytes_accessed=t * width * 8, transcendentals=t * t * 16),
        name="attend_back",
    )(qkv, qkv, qkv, d_attended, lse)

def gelu_parts(v):
    e = jnp.exp(-0.5 * v * v)
    t = 1.0 / (1.0 + (0.3275911 * 0.5 ** 0.5) * jnp.abs(v))
    poly = t * (0.127414796 + t * (-0.142248368 + t * (0.7107068705 + t * (-0.7265760135 + t * 0.5307027145))))
    tail = poly * e
    phi = jnp.where(v < 0, tail, 1.0 - tail)
    return v * phi, phi + v * (e * (2.0 * math.pi) ** -0.5)

def mlp_in_body(n_ref, w_ref, b_ref, act_ref, slope_ref):
    v = dot(n_ref[...], w_ref[...]) + b_ref[...]
    act, slope = gelu_parts(v)
    act_ref[...] = act.astype(bf16)
    slope_ref[...] = slope.astype(bf16)

def mlp_in(normed, w, bias, block=512):
    t, d = normed.shape
    ff = w.shape[1]
    out = pl.BlockSpec((t, block), lambda i: (0, i))
    shape = jax.ShapeDtypeStruct((t, ff), bf16)
    return pl.pallas_call(
        mlp_in_body, grid=(ff // block,),
        in_specs=[pl.BlockSpec((t, d), lambda i: (0, 0)), pl.BlockSpec((d, block), lambda i: (0, i)), pl.BlockSpec((1, block), lambda i: (0, i))],
        out_specs=[out, out], out_shape=[shape, shape],
        compiler_params=pltpu.CompilerParams(vmem_limit_bytes=48 << 20),
        cost_estimate=pl.CostEstimate(flops=2 * t * d * ff, bytes_accessed=d * ff * 2 + t * ff * 4, transcendentals=t * ff),
        name="mlp_in",
    )(normed, w, bias.reshape(1, -1))

def mlp_back_body(dy_ref, slope_ref, w1_ref, w2_ref, dpre_ref, db_ref, dn_ref):
    g = dot(dy_ref[...], w2_ref[...], NT) * slope_ref[...].astype(f32)
    low = g.astype(bf16)
    dpre_ref[...] = low
    db_ref[...] = jnp.sum(low.astype(f32), axis=0, keepdims=True)
    dn = dot(low, w1_ref[...], NT)
    @pl.when(pl.program_id(0) == 0)
    def _(): dn_ref[...] = dn
    @pl.when(pl.program_id(0) > 0)
    def _(): dn_ref[...] += dn

def mlp_back(dy, slope, w1, w2, block=512):
    t, d = dy.shape
    ff = w1.shape[1]
    whole = pl.BlockSpec((t, d), lambda i: (0, 0))
    part = pl.BlockSpec((t, block), lambda i: (0, i))
    return pl.pallas_call(
        mlp_back_body, grid=(ff // block,),
        in_specs=[whole, part, pl.BlockSpec((d, block), lambda i: (0, i)), pl.BlockSpec((block, d), lambda i: (i, 0))],
        out_specs=[part, pl.BlockSpec((1, block), lambda i: (0, i)), whole],
        out_shape=[jax.ShapeDtypeStruct((t, ff), bf16), jax.ShapeDtypeStruct((1, ff), f32), jax.ShapeDtypeStruct((t, d), f32)],
        compiler_params=pltpu.CompilerParams(vmem_limit_bytes=48 << 20),
        cost_estimate=pl.CostEstimate(flops=4 * t * d * ff, bytes_accessed=d * ff * 4 + t * ff * 4, transcendentals=0),
        name="mlp_back",
    )(dy, slope, w1, w2)

def side_steps(x, side):
    n = x.shape[0]
    b = lax.rem(lax.broadcasted_iota(jnp.int32, x.shape, 0), side)
    before = jnp.where(b == 0, 0.0, pltpu.roll(x, 1, 0))
    after = jnp.where(b == side - 1, 0.0, pltpu.roll(x, n - 1, 0))
    return before, after

def up(x, by):
    return jnp.concatenate([jnp.zeros((by, x.shape[1]), x.dtype), x[:-by]], 0)

def down(x, by):
    return jnp.concatenate([x[by:], jnp.zeros((by, x.shape[1]), x.dtype)], 0)

def adapter_body(n_pieces, side, pos_ref, *refs):
    pieces, (w_ref, table_ref, dy_ref, proj_ref, spat_ref, rows_ref, dg_ref, dys_ref) = refs[:n_pieces], refs[n_pieces:]
    x = table_ref[BIAS_PROJ : BIAS_PROJ + 1]
    for k in range(n_pieces):
        x = x + dot(pieces[k][...], w_ref[lax.rem(pos_ref[0] - k + n_pieces, n_pieces)])
    proj_ref[...] = x
    before, after = side_steps(x, side)
    w = table_ref[DEPTH : DEPTH + 9]
    y = [before * w[3 * s:3 * s + 1] + x * w[3 * s + 1:3 * s + 2] + after * w[3 * s + 2:3 * s + 3] for s in range(3)]
    spatial = up(y[0], side) + y[1] + down(y[2], side) + table_ref[BIAS_DEPTH : BIAS_DEPTH + 1]
    spat_ref[...] = spatial
    rows_ref[...] = jnp.sum(spatial, axis=0, keepdims=True)
    dy = dy_ref[...].astype(f32)
    dg_ref[...] = jnp.sum(dy * spatial, axis=0, keepdims=True)
    dys_ref[...] = jnp.sum(dy, axis=0, keepdims=True)

def adapter(pos, pieces, w_proj, table, dy, side=PS, block=256):
    t, d = dy.shape
    n, width = len(pieces), pieces[0].shape[1]
    whole = pl.BlockSpec((t, width), lambda i: (0, 0))
    part = pl.BlockSpec((t, block), lambda i: (0, i))
    row = pl.BlockSpec((1, block), lambda i: (0, i))
    big, line = jax.ShapeDtypeStruct((t, d), f32), jax.ShapeDtypeStruct((1, d), f32)
    return pl.pallas_call(
        functools.partial(adapter_body, n, side), grid=(d // block,),
        in_specs=[pl.BlockSpec(memory_space=pltpu.SMEM)] + [whole] * n + [pl.BlockSpec((n, width, block), lambda i: (0, 0, i)), pl.BlockSpec((table.shape[0], block), lambda i: (0, i)), part],
        out_specs=[part, part, row, row, row], out_shape=[big, big, line, line, line],
        compiler_params=pltpu.CompilerParams(vmem_limit_bytes=48 << 20),
        cost_estimate=pl.CostEstimate(flops=2 * t * d * n * width, bytes_accessed=t * d * 16, transcendentals=0),
        name="adapter",
    )(pos.reshape(1).astype(jnp.int32), *pieces, w_proj.reshape(n, width, d), table, dy)

def adapter_back_body(side, n_near, dy_ref, proj_ref, gate_ref, share_ref, *refs):
    near, (table_ref, dp_ref, dwd_ref, dbd_ref, dbp_ref) = refs[:n_near], refs[n_near:]
    d_rows = share_ref[0:1, :1] * near[0][...]
    for i in range(1, n_near):
        d_rows = d_rows + share_ref[i:i + 1, :1] * near[i][...]
    ds = dy_ref[...].astype(f32) * gate_ref[...] + d_rows
    dbd_ref[...] = jnp.sum(ds, axis=0, keepdims=True)
    before, after = side_steps(ds, side)
    w = table_ref[DEPTH : DEPTH + 9]
    y = [after * w[3 * s:3 * s + 1] + ds * w[3 * s + 1:3 * s + 2] + before * w[3 * s + 2:3 * s + 3] for s in range(3)]
    low = (down(y[0], side) + y[1] + up(y[2], side)).astype(bf16)
    dp_ref[...] = low
    dbp_ref[...] = jnp.sum(low.astype(f32), axis=0, keepdims=True)
    x = proj_ref[...]
    x_before, x_after = side_steps(x, side)
    for t, c in enumerate((x_before, x, x_after)):
        dwd_ref[t:t + 1] = jnp.sum(ds[side:] * c[:-side], axis=0, keepdims=True)
        dwd_ref[3 + t:4 + t] = jnp.sum(ds * c, axis=0, keepdims=True)
        dwd_ref[6 + t:7 + t] = jnp.sum(ds[:-side] * c[side:], axis=0, keepdims=True)

def adapter_back(dy, projected, gate, share, near, table, side=PS, block=256):
    t, d = dy.shape
    part = pl.BlockSpec((t, block), lambda i: (0, i))
    row = pl.BlockSpec((1, block), lambda i: (0, i))
    nine = pl.BlockSpec((9, block), lambda i: (0, i))
    line = jax.ShapeDtypeStruct((1, d), f32)
    return pl.pallas_call(
        functools.partial(adapter_back_body, side, len(near)), grid=(d // block,),
        in_specs=[part, part, row, pl.BlockSpec((len(near), 128), lambda i: (0, 0))] + [row] * len(near) + [pl.BlockSpec((table.shape[0], block), lambda i: (0, i))], out_specs=[part, nine, row, row],
        out_shape=[jax.ShapeDtypeStruct((t, d), bf16), jax.ShapeDtypeStruct((9, d), f32), line, line],
        compiler_params=pltpu.CompilerParams(vmem_limit_bytes=48 << 20),
        cost_estimate=pl.CostEstimate(flops=60 * t * d, bytes_accessed=t * d * 8, transcendentals=0),
        name="adapter_back",
    )(dy, projected, gate, share, *near, table)

def dot3(x, w, dims=NN):
    a = x.astype(bf16)
    rest = x - a.astype(f32)
    b = rest.astype(bf16)
    c = (rest - b.astype(f32)).astype(bf16)
    return dot(a, w, dims) + dot(b, w, dims) + dot(c, w, dims)


def gate_body(n_near, tokens, *refs):
    near, refs = refs[:n_near], refs[n_near:]
    dg_ref, win_ref, wout_ref, gate_ref, dmean_ref, share_ref, factors_ref = refs
    d = dg_ref.shape[1]
    own = near[0][:, d:]
    match = [(near[i][:, d:] == own).astype(f32) for i in range(n_near)]
    count = functools.reduce(lambda a, b: a + b, match) * tokens
    share = [m / count for m in match]
    for i in range(n_near):
        share_ref[i : i + 1] = share[i]
    mean = share[0][:, :1] * near[0][:, :d]
    for i in range(1, n_near):
        mean = mean + share[i][:, :1] * near[i][:, :d]

    def tall(v):
        return jnp.broadcast_to(v, (8, v.shape[1]))

    win, wout = win_ref[...], wout_ref[...]
    act, slope = gelu_parts(dot3(tall(mean), win))
    gate = jnp.tanh(dot3(act, wout, NT))
    d_pre = dg_ref[...] * (1.0 - gate * gate)
    d_hidden = dot3(d_pre, wout) * slope
    d_mean = dot3(d_hidden, win, NT)
    gate_ref[...] = gate[:1]
    dmean_ref[...] = d_mean[:1]
    parts = (mean, d_pre[:1], d_hidden[:1], act[:1], jnp.zeros((1, 128), f32) + jnp.sum(gate[:1]))
    at = 0
    for v in parts:
        factors_ref[:, at : at + v.shape[1]] = v
        at += v.shape[1]


def gate_step(near, d_gate, mixed_w, d, hidden, tokens):
    n = len(near)

    def line(k):
        return jax.ShapeDtypeStruct((1, k), f32)

    def at(k, i=0):
        return pl.BlockSpec((1, k), lambda j: (0, 0))

    k = 2 * d + 2 * hidden + 128
    return pl.pallas_call(
        functools.partial(gate_body, n, tokens),
        grid=(1,),
        in_specs=[at(d + 128)] * n
        + [at(d)]
        + [pl.BlockSpec((d, hidden), lambda j, b=b: (0, b)) for b in range(2)],
        out_specs=[at(d), at(d), pl.BlockSpec((n, 128), lambda j: (0, 0)), at(k)],
        out_shape=[line(d), line(d), jax.ShapeDtypeStruct((n, 128), f32), line(k)],
        compiler_params=pltpu.CompilerParams(vmem_limit_bytes=32 << 20),
        name="gate",
    )(*near, d_gate, mixed_w, mixed_w)


def pool_table(coarse_side, fine_side):
    coarse, fine = np.arange(coarse_side)[:, None], np.arange(fine_side)[None]
    start = coarse * fine_side // coarse_side
    end = ((coarse + 1) * fine_side + coarse_side - 1) // coarse_side
    single = np.where((fine >= start) & (fine < end), 1.0, 0.0) / (end - start)
    return np.kron(single, single)


def token_sum(values):
    return jnp.sum(values.astype(f32), axis=0)


def shards(
    tokens,
    features,
    sample_of,
    cotangent,
    ln1_gain,
    ln1_bias,
    w_qkv,
    bias_qv,
    w_attn_out,
    bias_attn_out,
    ln2_gain,
    ln2_bias,
    w_fc1,
    bias_fc1,
    w_fc2,
    bias_fc2,
    w_proj,
    bias_proj,
    w_depth,
    bias_depth,
    w_gate_in,
    w_gate_out,
):
    grid = Grid()
    rows = ln1_gain.shape[0]
    total = grid.total
    x, dy = tokens[0], cotangent[0]
    count, d = x.shape
    hidden = w_gate_in.shape[1]

    vectors = [ln1_gain, ln1_bias, bias_attn_out, ln2_gain, ln2_bias, bias_fc2, bias_proj, bias_depth]
    a_small = GatherSmall(
        grid, jnp.concatenate(vectors + [w_depth.reshape(-1), bias_qv, bias_fc1])
    )
    full_qkv = lax.all_gather(w_qkv, AXES, axis=0, tiled=True)
    full_fc2 = lax.all_gather(w_fc2, AXES, axis=0, tiled=True)
    gate_out_rows = dot(jnp.eye(rows, dtype=bf16), w_gate_out, NT).astype(bf16)
    gates = jnp.concatenate([w_gate_in, gate_out_rows], 1)
    held = -(-rows // 16) * 16
    a_mixed = Gather(
        grid,
        jnp.concatenate(
            [jnp.pad(w, ((0, held - rows), (0, 0))) for w in (w_attn_out, gates)] + [w_proj], 0
        ),
    )
    a_fc1 = Gather(grid, w_fc1)

    n_ch = lax.axis_size("ch")
    ch = lax.axis_index("ch")
    n_img, own_ch = features.shape[0], features.shape[1]
    core = grid.pos["c"]

    def along_ch(v, by):
        img = lax.axis_size("img")
        pairs = [
            (i * n_ch + j, i * n_ch + (j + by) % n_ch) for i in range(img) for j in range(n_ch)
        ]
        return lax.ppermute(v, AXES, pairs)

    def peer(v):
        return grid.send(v, "c", 1)

    def peer_half(v):
        h = v.shape[1] // 2
        return grid.send(lax.dynamic_slice(v, (0, (1 - core) * h), (v.shape[0], h)), "c", 1)

    def step(active, *values):
        states, values = lax.optimization_barrier(([a.state() for a in active], values))
        for a, state in zip(active, states):
            a.set_state(state)
        return values

    a_mixed.along_z()
    pool = jnp.asarray(pool_table(PS, FS), bf16)
    pooled_own = dot(pool, features.reshape(n_img * own_ch, -1), NT).astype(bf16)
    pieces = []
    for k in range(n_ch):
        to = lax.rem(ch + k, n_ch)
        piece = lax.dynamic_slice(pooled_own, (0, to * own_ch), (count, own_ch))
        pieces.append(along_ch(piece, k) if k else piece)
    for _ in range(4):
        every = a_small.next()
    every, pieces = step((a_mixed, a_fc1), every, pieces)

    a_mixed.first()
    a_fc1.along_z()
    every = every.astype(f32)
    table = every[:, : LINES * rows].reshape(total, LINES, rows)
    table = table.transpose(1, 0, 2).reshape(LINES, d)
    at = LINES * rows
    full_bias_qv = every[:, at : at + 2 * rows].reshape(-1)
    full_bias_fc1 = every[:, at + 2 * rows :].reshape(1, -1)
    bias_qkv = jnp.concatenate([full_bias_qv[:d], jnp.zeros((d,), f32), full_bias_qv[d:]])
    x32 = x.astype(f32)
    normed1 = layer_norm(x32, table[LN1_GAIN], table[LN1_BIAS]).astype(bf16)
    pooled = jnp.zeros((count, n_ch * own_ch), bf16)
    for k in range(n_ch):
        from_ch = lax.rem(ch - k + n_ch, n_ch)
        pooled = lax.dynamic_update_slice(pooled, pieces[k], (0, from_ch * own_ch))
    dy_far = peer_half(dy)
    normed1, table, full_bias_fc1, bias_qkv, pooled, dy_far = step(
        (a_mixed, a_fc1), normed1, table, full_bias_fc1, bias_qkv, pooled, dy_far
    )

    a_mixed.second()
    a_fc1.first()
    qkv = (dot(normed1, full_qkv) + bias_qkv).astype(bf16)
    attended, log_total = attend(qkv)
    a_mixed.cross()
    normed1_far, pooled_far = peer(normed1), peer(pooled)
    attended, log_total, normed1_far, pooled_far = step(
        (a_mixed, a_fc1), attended, log_total, normed1_far, pooled_far
    )

    a_fc1.second()
    mixed_w = a_mixed.whole().reshape(total, -1, d)
    full_attn_out = mixed_w[:, :rows].reshape(d, d)
    full_gates = mixed_w[:, held : held + rows].reshape(d, 2 * hidden)
    full_proj = mixed_w[:, 2 * held :].reshape(-1, d)
    first_sum = x32 + dot(attended, full_attn_out) + table[BIAS_OUT]
    normed2 = layer_norm(first_sum, table[LN2_GAIN], table[LN2_BIAS]).astype(bf16)
    projected, spatial, row_sums, d_gate, dy_sum = adapter(ch, pieces, full_proj, table, dy)
    ids_plus = sample_of.astype(f32) + 1.0
    carried = jnp.concatenate([row_sums, jnp.broadcast_to(ids_plus[:, None], (1, 128))], 1)
    near = neighbours(grid, carried, REACH)
    attended_far = peer(attended)
    normed2, near, attended_far, full_gates, full_proj, full_attn_out = step(
        (a_fc1,), normed2, near, attended_far, full_gates, full_proj, full_attn_out
    )

    a_fc1.cross()
    gate, d_mean, share, factors = gate_step(near, d_gate, full_gates, d, hidden, count)
    near_dmean = neighbours(grid, d_mean, REACH)
    normed2_far = peer(normed2)
    full_fc1 = a_fc1.whole()
    activation, slope = mlp_in(normed2, full_fc1, full_bias_fc1)
    activation, slope, near_dmean, full_fc1, normed2_far, factors = step(
        (), activation, slope, near_dmean, full_fc1, normed2_far, factors
    )

    activation_far = peer(activation)
    a_factors = GatherSmall(grid, factors[0])
    a_factors.next()
    d_projected, d_depth, d_bias_depth, d_bias_proj = adapter_back(
        dy, projected, gate, share, near_dmean, table
    )
    d_pooled = dot(d_projected, full_proj, NT).astype(bf16)
    activation_far, d_projected, d_pooled, a_factors.v = step(
        (), activation_far, d_projected, d_pooled, a_factors.v
    )

    s_fc2 = Scatter(grid, activation, activation_far, dy, dy_far)
    a_factors.next()
    d_projected_far = peer_half(d_projected)
    back = []
    for k in range(n_ch):
        to = lax.rem(ch + k, n_ch)
        piece = lax.dynamic_slice(d_pooled, (0, to * own_ch), (count, own_ch))
        back.append(along_ch(piece, k) if k else piece)
    slope, d_projected_far, back, a_factors.v = step(
        (s_fc2,), slope, d_projected_far, back, a_factors.v
    )

    s_fc2.first()
    a_factors.next()
    d_pre, d_bias_fc1, d_normed2 = mlp_back(dy, slope, full_fc1, full_fc2)
    s_proj = Scatter(grid, pooled, pooled_far, d_projected, d_projected_far)
    d_pre, d_bias_fc1, d_normed2, full_fc2, back, a_factors.v = step(
        (s_fc2, s_proj), d_pre, d_bias_fc1, d_normed2, full_fc2, back, a_factors.v
    )

    s_fc2.second()
    s_proj.first()
    d_pre_far = peer_half(d_pre)
    _, norm_two_back = jax.vjp(layer_norm, first_sum, table[LN2_GAIN], table[LN2_BIAS])
    d_first_norm, d_ln2_gain, d_ln2_bias = norm_two_back(d_normed2)
    d_first = dy.astype(f32) + d_first_norm
    d_branch = d_first.astype(bf16)
    d_branch_far = peer_half(d_branch)
    d_attended = dot(d_branch, full_attn_out, NT).astype(bf16)
    d_local = jnp.zeros((n_img, count, own_ch), bf16)
    for k in range(n_ch):
        from_ch = lax.rem(ch - k + n_ch, n_ch)
        d_local = lax.dynamic_update_slice(d_local, back[k][None], (from_ch, 0, 0))
    grad_features = jnp.einsum("kpc,pf->kcf", d_local, pool, preferred_element_type=f32).astype(bf16)
    d_attended, d_first, d_pre_far, d_branch_far, grad_features, a_factors.v = step(
        (s_fc2, s_proj), d_attended, d_first, d_pre_far, d_branch_far, grad_features, a_factors.v
    )

    s_fc2.along_z()
    s_proj.second()
    s_fc1 = Scatter(grid, normed2, normed2_far, d_pre, d_pre_far)
    s_attn = Scatter(grid, attended, attended_far, d_branch, d_branch_far)
    (d_attended,) = step((s_fc2, s_proj, s_fc1, s_attn), d_attended)

    s_fc1.first()
    s_attn.first()
    s_proj.along_z()
    d_query, d_key, d_value = attend_back(qkv, d_attended, log_total)
    d_mixed = jnp.concatenate([d_query, d_key, d_value], -1)
    d_mixed, activation, a_factors.v, s_fc2.kept = step(
        (s_fc1, s_attn, s_proj), d_mixed, activation, a_factors.v, s_fc2.kept
    )

    s_fc1.second()
    s_attn.second()
    s_fc2.last()
    d_mixed_far = peer_half(d_mixed)
    second_sum = first_sum + dot(activation, full_fc2) + table[BIAS_FC2]
    layer_out = (second_sum + gate * spatial).astype(bf16)
    d_normed1 = dot(d_mixed, full_qkv, NT)
    d_mixed_far, layer_out, d_normed1, d_mixed = step(
        (s_fc1, s_attn, s_fc2, s_proj), d_mixed_far, layer_out, d_normed1, d_mixed
    )

    s_fc1.along_z()
    s_proj.last()
    a_factors.next()
    s_qkv = Scatter(grid, normed1, normed1_far, d_mixed, d_mixed_far)
    _, norm_one_back = jax.vjp(layer_norm, x32, table[LN1_GAIN], table[LN1_BIAS])
    d_input, d_ln1_gain, d_ln1_bias = norm_one_back(d_normed1)
    grad_tokens = (d_first + d_input).astype(bf16)
    lines = [
        d_ln1_gain,
        d_ln1_bias,
        token_sum(d_branch),
        d_ln2_gain,
        d_ln2_bias,
        dy_sum[0],
        d_bias_proj[0],
        d_bias_depth[0],
    ]
    stacked = jnp.concatenate([jnp.stack(lines), d_depth], 0)
    stacked = stacked.reshape(LINES, total, rows).transpose(1, 0, 2).reshape(total, -1)
    d_bias_qv = jnp.concatenate([token_sum(d_query), token_sum(d_value)])
    s_small = ScatterSmall(
        grid,
        jnp.concatenate([stacked, d_bias_qv.reshape(total, -1), d_bias_fc1.reshape(total, -1)], 1),
    )
    s_small.v, grad_tokens, a_factors.v = step(
        (s_fc1, s_attn, s_qkv, s_fc2, s_proj), s_small.v, grad_tokens, a_factors.v
    )

    s_qkv.first()
    s_attn.along_z()
    s_fc1.last()
    s_small.next()
    g_fc2, g_proj = s_fc2.result(), s_proj.result()
    g_fc2, g_proj, s_small.v = step((s_fc1, s_attn, s_qkv), g_fc2, g_proj, s_small.v)

    s_qkv.second()
    s_attn.last()
    s_small.next()
    s_small.next()
    all_factors = a_factors.v
    g_fc1 = s_fc1.result()
    s_small.v, g_fc1, all_factors = step((s_attn, s_qkv), s_small.v, g_fc1, all_factors)

    s_qkv.along_z()
    summed = s_small.next()[0]
    g_attn_out = s_attn.result()
    own_cols = grid.me * rows
    g_gate_in = lax.dot_general(
        lax.dynamic_slice(all_factors, (0, own_cols), (total, rows)),
        all_factors[:, 2 * d : 2 * d + hidden],
        TN,
        precision=highest,
    )
    g_gate_out = lax.dot_general(
        all_factors[:, 2 * d + hidden : 2 * d + 2 * hidden],
        lax.dynamic_slice(all_factors, (0, d + own_cols), (total, rows)),
        TN,
        precision=highest,
    )
    gate_mean = jnp.sum(all_factors[:, -1]) / (total * d)
    summed, g_gate_in, g_gate_out, gate_mean = step(
        (s_qkv,), summed, g_gate_in, g_gate_out, gate_mean
    )
    s_qkv.last()
    g_qkv = s_qkv.result()

    def owned(i):
        return summed[i * rows : (i + 1) * rows]

    return (
        layer_out[None],
        grad_tokens[None],
        grad_features,
        owned(LN1_GAIN),
        owned(LN1_BIAS),
        g_qkv,
        summed[at : at + 2 * rows],
        g_attn_out,
        owned(BIAS_OUT),
        owned(LN2_GAIN),
        owned(LN2_BIAS),
        g_fc1,
        summed[at + 2 * rows :],
        g_fc2,
        owned(BIAS_FC2),
        g_proj,
        owned(BIAS_PROJ),
        summed[DEPTH * rows : at].reshape(9, rows),
        owned(BIAS_DEPTH),
        g_gate_in,
        g_gate_out,
        gate_mean,
    )


def solution(mesh):
    return jax.shard_map(
        shards,
        mesh=mesh,
        in_specs=(
            P(("img", "ch"), None, None),
            P("img", "ch", None),
            P(("img", "ch")),
            P(("img", "ch"), None, None),
            P(("img", "ch")),
            P(("img", "ch")),
            P(("img", "ch"), None),
            P(("img", "ch")),
            P(("img", "ch"), None),
            P(("img", "ch")),
            P(("img", "ch")),
            P(("img", "ch")),
            P(("img", "ch"), None),
            P(("img", "ch")),
            P(("img", "ch"), None),
            P(("img", "ch")),
            P(("img", "ch"), None),
            P(("img", "ch")),
            P(None, ("img", "ch")),
            P(("img", "ch")),
            P(("img", "ch"), None),
            P(None, ("img", "ch")),
        ),
        out_specs=(
            P(("img", "ch"), None, None),
            P(("img", "ch"), None, None),
            P("img", "ch", None),
            P(("img", "ch")),
            P(("img", "ch")),
            P(("img", "ch"), None),
            P(("img", "ch")),
            P(("img", "ch"), None),
            P(("img", "ch")),
            P(("img", "ch")),
            P(("img", "ch")),
            P(("img", "ch"), None),
            P(("img", "ch")),
            P(("img", "ch"), None),
            P(("img", "ch")),
            P(("img", "ch"), None),
            P(("img", "ch")),
            P(None, ("img", "ch")),
            P(("img", "ch")),
            P(("img", "ch"), None),
            P(None, ("img", "ch")),
            P(),
        ),
        check_vma=False,
    )
```

```python
import functools
import math

import jax
import numpy as np
import jax.numpy as jnp
from jax import lax
from jax.experimental import pallas as pl
from jax.experimental.pallas import tpu as pltpu
from jax.sharding import PartitionSpec as P

HEAD = 64
PS = 24
FS = 32
REACH = 3
LN1_GAIN, LN1_BIAS, BIAS_OUT, LN2_GAIN, LN2_BIAS, BIAS_FC2, BIAS_PROJ, BIAS_DEPTH, DEPTH = range(9)
LINES = DEPTH + 9

norm_eps = 1e-05
highest = lax.Precision.HIGHEST
f32, bf16 = jnp.float32, jnp.bfloat16
AXES = ("img", "ch")
FREE = pl.CostEstimate(flops=0, bytes_accessed=0, transcendentals=0)
NN = (((1,), (0,)), ((), ()))
NT = (((1,), (1,)), ((), ()))
TN = (((0,), (0,)), ((), ()))


class Grid:
    def __init__(self):
        img, ch = lax.axis_size("img"), lax.axis_size("ch")
        depth = 4 if img % 4 == 0 else 1
        self.n = {"z": depth, "x": img // depth, "y": ch // 2, "c": 2}
        self.stride = {"c": 1, "y": 2, "x": ch, "z": ch * (img // depth)}
        self.total = img * ch
        me = lax.axis_index(AXES)
        self.me = me
        self.pos = {a: lax.rem(lax.div(me, self.stride[a]), self.n[a]) for a in self.n}

    def send(self, v, axis, by):
        n, s = self.n[axis], self.stride[axis]
        pairs = []
        for i in range(self.total):
            a = (i // s) % n
            pairs.append((i, i + ((a + by) % n - a) * s))
        return lax.ppermute(v, AXES, pairs)

    def other(self, axis, by):
        return lax.rem(self.pos[axis] + by, self.n[axis])

    def swap(self, v, bit):
        return lax.ppermute(v, AXES, [(i, i ^ bit) for i in range(self.total)])


class GatherSmall:
    def __init__(self, grid, v):
        self.grid, self.v, self.bit = grid, v[None], 1

    def next(self):
        got = self.grid.swap(self.v, self.bit)
        pair = (self.v, got)
        upper = jnp.bitwise_and(self.grid.me, self.bit) != 0
        self.v = jnp.where(upper, jnp.concatenate(pair[::-1], 0), jnp.concatenate(pair, 0))
        self.bit *= 2
        return self.bit < self.grid.total


class ScatterSmall:
    def __init__(self, grid, v):
        self.grid, self.v = grid, v
        bits = [1 << i for i in range(grid.total.bit_length() - 1)]
        stride = grid.stride["z"]
        self.left = [b for b in bits if b >= stride][::-1] + [b for b in bits if b < stride][::-1]
        self.shape = {b: 2 for b in bits}

    def next(self):
        bit = self.left.pop(0)
        del self.shape[bit]
        low = 2 ** sum(b < bit for b in self.shape)
        t = self.v.reshape(-1, 2, low, self.v.shape[1])
        upper = (jnp.bitwise_and(self.grid.me, bit) != 0).astype(jnp.int32)
        mine = lax.dynamic_index_in_dim(t, upper, 1, keepdims=False)
        away = lax.dynamic_index_in_dim(t, 1 - upper, 1, keepdims=False)
        mine, away = (u.reshape(-1, t.shape[3]) for u in (mine, away))
        self.v = mine + self.grid.swap(away, bit)


def after(value, done):
    return lax.optimization_barrier((value, done))[0]


class Gather:
    def __init__(self, grid, params):
        self.grid = grid
        self.width = width = min(p.shape[1] for p in params)
        self.q = width // 2
        self.places, blocks, at = [], [], 0
        for i, p in enumerate(params):
            r = p.shape[0]
            held = -(-r // 16) * 16
            for j in range(p.shape[1] // width):
                block = p[:, j * width : (j + 1) * width]
                blocks.append(jnp.pad(block, ((0, held - r), (0, 0))) if held > r else block)
                self.places.append((i, at, r if r % 8 == 0 else held, j * width))
                at += held
        self.shapes = [p.shape for p in params]
        self.shard = jnp.concatenate(blocks, 0)

    def along_z(self):
        g = self.grid
        self.z = [self.shard] + [g.send(self.shard, "z", k) for k in range(1, g.n["z"])]

    def pack_first(self):
        self.s0 = [
            jnp.stack([p[:, i * self.q : (i + 1) * self.q] for p in self.z]) for i in range(2)
        ]
        del self.z

    def first(self):
        self.r1 = [self.every(self.s0[i], "xy"[i]) for i in range(2)]

    def pack_second(self):
        self.s1 = [jnp.concatenate([self.s0[i]] + self.r1[i], 0) for i in range(2)]
        del self.s0, self.r1

    def second(self):
        self.r2 = [self.every(self.s1[i], "yx"[i]) for i in range(2)]

    def early(self):
        self.c1 = [self.over(s) for s in self.s1]

    def cross(self):
        self.c2 = [[self.over(b) for b in r] for r in self.r2]

    def every(self, v, axis):
        return [self.grid.send(v, axis, k) for k in range(1, self.grid.n[axis])]

    def over(self, v):
        return self.grid.send(v, "c", 1)


    def state(self):
        names = ("shard", "z", "s0", "s1", "r1", "r2", "c1", "c2")
        return {k: v for k, v in vars(self).items() if k in names}

    def set_state(self, state):
        for k, v in state.items():
            setattr(self, k, v)

    def whole(self):
        n, q, place_of = self.grid.n, self.q, self.places
        nz, nx, ny = n["z"], n["x"], n["y"]
        arrays, plan = [], []
        for core_rel, (s1, r2) in enumerate(((self.s1, self.r2), (self.c1, self.c2))):
            for part, (first, second) in enumerate((("x", "y"), ("y", "x"))):
                for k2, buf in enumerate([s1[part]] + r2[part]):
                    for k1 in range(n[first]):
                        for kz in range(nz):
                            rel = {first: k1, second: k2}
                            plan.append((len(arrays), k1 * nz + kz, core_rel, part, kz, rel))
                    arrays.append(buf)
        count = len(self.shapes)
        tall = {param: r for param, _, r, _ in place_of}

        def body(place, *refs):
            ins, outs = refs[: len(arrays)], refs[len(arrays) : len(arrays) + count]
            held, (sems, out_sems) = refs[len(arrays) + count : -2], refs[-2:]
            z, x, y, c = place[0], place[1], place[2], place[3]
            waits = [[] for _ in range(nz)]
            for i, j, core_rel, part, kz, rel in plan:
                zz = lax.rem(z - kz + nz, nz)
                xx = lax.rem(x - rel["x"] + nx, nx)
                yy = lax.rem(y - rel["y"] + ny, ny)
                cc = lax.rem(c + core_rel, 2)
                for param, row, r, col in place_of:
                    copy = pltpu.make_async_copy(
                        ins[i].at[j, pl.ds(row, r)],
                        held[param].at[zz, xx, yy, cc, :, pl.ds(col + part * q, q)],
                        sems.at[kz],
                    )
                    copy.start()
                    waits[kz].append(copy)
            after = []
            for kz in range(nz):
                for copy in waits[kz]:
                    copy.wait()
                zz = lax.rem(z - kz + nz, nz)
                for param in range(count):
                    copy = pltpu.make_async_copy(
                        held[param].at[zz], outs[param].at[zz], out_sems.at[kz]
                    )
                    copy.start()
                    after.append(copy)
            for copy in after:
                copy.wait()

        place = jnp.stack([self.grid.pos[a] for a in ("z", "x", "y", "c")]).astype(jnp.int32)
        devices = nz * nx * ny * 2
        room = sum(devices * (r + 8) * w * 2 for r, w in self.shapes)
        shapes = [(nz, nx, ny, 2, tall[i], w) for i, (_, w) in enumerate(self.shapes)]
        whole = pl.pallas_call(
            body,
            out_shape=[jax.ShapeDtypeStruct(s, bf16) for s in shapes],
            in_specs=[pl.BlockSpec(memory_space=pltpu.SMEM)]
            + [pl.BlockSpec(memory_space=pltpu.HBM)] * len(arrays),
            out_specs=[pl.BlockSpec(memory_space=pltpu.HBM)] * count,
            scratch_shapes=[pltpu.VMEM(s, bf16) for s in shapes]
            + [pltpu.SemaphoreType.DMA((nz,)), pltpu.SemaphoreType.DMA((nz,))],
            compiler_params=pltpu.CompilerParams(vmem_limit_bytes=room + (4 << 20)),
            cost_estimate=FREE,
            name="assemble",
        )(place, *arrays)
        return [
            w[:, :, :, :, :r].reshape(devices * r, width) for w, (r, width) in zip(whole, self.shapes)
        ]


def tail_of(r, q, keep):
    extra = r - keep
    return extra, keep // extra, q * extra // keep


def place_share(ref, value, row, col):
    r, q, keep = value.shape[1] // 2, value.shape[2], ref.shape[2] // 2
    if row or r <= keep:
        ref[0, :, row : row + 2 * r, col : col + q] = value
        return
    extra, count, w = tail_of(r, q, keep)
    for c in range(2):
        ref[0, :, c * keep : (c + 1) * keep, col : col + q] = value[:, c * r : c * r + keep]
        for j in range(count):
            at = c * keep + j * extra
            ref[0, :, at : at + extra, col + q : col + q + w] = value[
                :, c * r + keep : (c + 1) * r, j * w : (j + 1) * w
            ]


def weight_grad_body(grid_n, terms, scratch, pos_ref, *refs):
    nx, ny = grid_n
    outs = refs[4 * len(terms) :]
    keep_a, keep_b = outs[0], outs[1]
    away_a, away_b = outs[2 : 1 + ny], outs[1 + ny :]
    for i, (r2, q, row, col) in enumerate(terms):
        l0, l1, r0, r1 = refs[4 * i : 4 * i + 4]
        o = dot(l0[...], r0[...], TN) + dot(l1[...], r1[...], TN)
        o = o.reshape(nx, ny, r2, 2 * q)

        def split_y(y, o=o, row=row, col=col, q=q):
            place_share(keep_a, o[:, y, :, :q].astype(bf16), row, col)
            for k in range(1, ny):
                place_share(away_a[k - 1], o[:, (y + k) % ny, :, :q].astype(bf16), row, col)

        def split_x(x, o=o, row=row, col=col, q=q):
            place_share(keep_b, o[x, :, :, q:].astype(bf16), row, col)
            for k in range(1, nx):
                place_share(away_b[k - 1], o[(x + k) % nx, :, :, q:].astype(bf16), row, col)

        for y in range(ny):
            pl.when(pos_ref[2] == y)(functools.partial(split_y, y))
        for x in range(nx):
            pl.when(pos_ref[1] == x)(functools.partial(split_x, x))


class Scatter:
    def __init__(self, grid, terms, height, width):
        self.grid = grid
        n = grid.n
        nz, nx, ny = n["z"], n["x"], n["y"]
        self.place = jnp.stack([grid.pos[a] for a in ("z", "x", "y", "c")]).astype(jnp.int32)
        self.height, self.width = height, width
        specs, arrays, shapes = [], [], []
        self.parts = []
        for left, left_far, right, right_far, at, at_far, left_at, rows, half, row, col in terms:
            t, band = left.shape[0], rows // nz
            r2, q = band // (nx * ny), half // 2
            lspec = pl.BlockSpec((t, band), lambda i, p, left_at=left_at: (0, left_at + i))
            specs += [lspec, lspec]
            specs += [pl.BlockSpec((t, half), lambda i, p, at=at: (0, at + p[3]))]
            if at_far is None:
                specs += [pl.BlockSpec((t, half), lambda i, p: (0, 0))]
            else:
                specs += [pl.BlockSpec((t, half), lambda i, p, at=at_far: (0, at + p[3]))]
            arrays += [left, left_far, right, right_far]
            shapes.append((r2, q, row, col))
            self.parts.append((r2 // 2, q, row, col))
        a = jax.ShapeDtypeStruct((nz, nx, height, width), bf16)
        b = jax.ShapeDtypeStruct((nz, ny, height, width), bf16)
        sa = pl.BlockSpec((1, nx, height, width), lambda i, p: (i, 0, 0, 0))
        sb = pl.BlockSpec((1, ny, height, width), lambda i, p: (i, 0, 0, 0))
        sums = pl.pallas_call(
            functools.partial(weight_grad_body, (nx, ny), shapes, None),
            grid_spec=pltpu.PrefetchScalarGridSpec(
                num_scalar_prefetch=1,
                grid=(nz,),
                in_specs=specs,
                out_specs=[sa, sb] + [sa] * (ny - 1) + [sb] * (nx - 1),
            ),
            out_shape=[a, b] + [a] * (ny - 1) + [b] * (nx - 1),
            compiler_params=pltpu.CompilerParams(vmem_limit_bytes=56 << 20),
            cost_estimate=FREE,
            name="weight_grad",
        )(self.place, *arrays)
        self.keep = list(sums[:2])
        self.away = [list(sums[2 : 1 + ny]), list(sums[1 + ny :])]

    def state(self):
        names = ("keep", "away", "got", "more", "sent", "kept", "own", "back")
        return {k: v for k, v in vars(self).items() if k in names}

    def set_state(self, state):
        for k, v in state.items():
            setattr(self, k, v)

    def first(self):
        self.got = [
            [self.grid.send(v, "yx"[i], k) for k, v in enumerate(self.away[i], 1)] for i in range(2)
        ]
        del self.away

    def fold_second(self):
        g, n = self.grid, self.grid.n
        nz, counts = n["z"], (n["x"], n["y"])
        block = (nz, 1, self.height, self.width)
        specs, arrays, plan = [], [], []
        for i in range(2):
            for k in range(1, counts[i]):

                def place(_, p, i=i, k=k):
                    return (0, lax.rem(p[1 + i] + k, counts[i]), 0, 0)

                terms = [self.keep[i]] + self.got[i]
                plan.append(len(terms))
                arrays += terms
                specs += [pl.BlockSpec(block, place)] * len(terms)

        def body(pos, *refs):
            at = 0
            for j, count in enumerate(plan):
                total = refs[at][:, 0].astype(f32)
                for ref in refs[at + 1 : at + count]:
                    total = total + ref[:, 0].astype(f32)
                refs[len(arrays) + j][...] = total.astype(bf16)
                at += count

        shape = jax.ShapeDtypeStruct((nz, self.height, self.width), bf16)
        sent = pl.pallas_call(
            body,
            grid_spec=pltpu.PrefetchScalarGridSpec(
                num_scalar_prefetch=1,
                grid=(1,),
                in_specs=specs,
                out_specs=[pl.BlockSpec(shape.shape, lambda i, p: (0, 0, 0))] * len(plan),
            ),
            out_shape=[shape] * len(plan),
            compiler_params=pltpu.CompilerParams(vmem_limit_bytes=56 << 20),
            cost_estimate=FREE,
            name="fold_second",
        )(self.place, *arrays)
        self.sent = list(sent)

    def second(self):
        g, sent = self.grid, self.sent
        counts = (g.n["x"], g.n["y"])
        at = counts[0] - 1
        del self.sent
        self.more = [
            [g.send(sent[k - 1], "x", k) for k in range(1, counts[0])],
            [g.send(sent[at + k - 1], "y", k) for k in range(1, counts[1])],
        ]

    def fold_z(self):
        g, n = self.grid, self.grid.n
        nz, counts = n["z"], (n["x"], n["y"])
        h, w = self.height, self.width
        specs, arrays, plan = [], [], []
        for i in range(2):
            terms = [self.keep[i]] + self.got[i]
            specs += [
                pl.BlockSpec(
                    (1, 1, h, w), lambda s, p, i=i: (lax.rem(p[0] + s, nz), p[1 + i], 0, 0)
                )
            ] * len(terms)
            specs += [
                pl.BlockSpec((1, h, w), lambda s, p: (lax.rem(p[0] + s, nz), 0, 0))
            ] * len(self.more[i])
            arrays += terms + self.more[i]
            plan.append((len(terms), len(self.more[i])))

        def body(pos, *refs):
            at = 0
            for i, (wide, narrow) in enumerate(plan):
                total = refs[at][0, 0].astype(f32)
                for ref in refs[at + 1 : at + wide]:
                    total = total + ref[0, 0].astype(f32)
                for ref in refs[at + wide : at + wide + narrow]:
                    total = total + ref[0].astype(f32)
                at += wide + narrow
                for k in range(nz):

                    def put(k=k, i=i, total=total):
                        out = refs[len(arrays) + k]
                        out[:, i * w : (i + 1) * w] = total.astype(out.dtype)

                    pl.when(pl.program_id(0) == k)(put)

        sent = pl.pallas_call(
            body,
            grid_spec=pltpu.PrefetchScalarGridSpec(
                num_scalar_prefetch=1,
                grid=(nz,),
                in_specs=specs,
                out_specs=[pl.BlockSpec((h, 2 * w), lambda s, p: (0, 0))] * nz,
            ),
            out_shape=[jax.ShapeDtypeStruct((h, 2 * w), bf16 if k else f32) for k in range(nz)],
            compiler_params=pltpu.CompilerParams(vmem_limit_bytes=56 << 20),
            cost_estimate=FREE,
            name="fold_z",
        )(self.place, *arrays)
        self.sent = list(sent)
        del self.keep, self.got, self.more

    def along_z(self):
        sent = self.sent
        self.kept = [sent[0]] + [self.grid.send(v, "z", k) for k, v in enumerate(sent[1:], 1)]
        del self.sent

    def last(self):
        w = self.width
        shape = jax.ShapeDtypeStruct((self.height // 2, 2 * w), f32)
        rows = sorted({(row, min(r, self.height // 2)) for r, _, row, _ in self.parts})

        def body(pos, *refs):
            own, away = refs[-2], refs[-1]
            total = refs[0][...]
            for ref in refs[1:-2]:
                total = total + ref[...].astype(f32)

            def put(c):
                for row, r in rows:
                    to = slice(row // 2, row // 2 + r)
                    own[to] = total[row + c * r : row + c * r + r]
                    away[to] = total[row + (1 - c) * r : row + (1 - c) * r + r]

            for c in range(2):
                pl.when(pos[3] == c)(functools.partial(put, c))

        self.own, away = pl.pallas_call(
            body,
            in_specs=[pl.BlockSpec(memory_space=pltpu.SMEM)]
            + [pl.BlockSpec(memory_space=pltpu.VMEM)] * len(self.kept),
            out_specs=[pl.BlockSpec(memory_space=pltpu.VMEM)] * 2,
            out_shape=[shape, shape],
            compiler_params=pltpu.CompilerParams(vmem_limit_bytes=56 << 20),
            cost_estimate=FREE,
            name="fold_last",
        )(self.place, *self.kept)
        self.back = self.grid.send(away, "c", 1)
        del self.kept

    def results(self):
        w = self.width

        def body(pos, own, back, *outs):
            def put(c):
                for out, (r, q, row, col) in zip(outs, self.parts):
                    keep = r if row else min(r, self.height // 2)
                    rs = slice(row // 2, row // 2 + keep)
                    for half, ref in ((c, own), (1 - c, back)):
                        for part in range(2):
                            at, from_col = 2 * half * q + part * q, part * w + col
                            out[:keep, at : at + q] = ref[rs, from_col : from_col + q]
                            if keep == r:
                                continue
                            extra, count, wide = tail_of(r, q, keep)
                            for j in range(count):
                                to = at + j * wide
                                out[keep:, to : to + wide] = ref[
                                    j * extra : (j + 1) * extra, from_col + q : from_col + q + wide
                                ]

            for c in range(2):
                pl.when(pos[3] == c)(functools.partial(put, c))

        return pl.pallas_call(
            body,
            in_specs=[pl.BlockSpec(memory_space=pltpu.SMEM)]
            + [pl.BlockSpec(memory_space=pltpu.VMEM)] * 2,
            out_specs=[pl.BlockSpec(memory_space=pltpu.VMEM)] * len(self.parts),
            out_shape=[jax.ShapeDtypeStruct((r, 4 * q), f32) for r, q, _, _ in self.parts],
            compiler_params=pltpu.CompilerParams(vmem_limit_bytes=56 << 20),
            cost_estimate=FREE,
            name="fold_out",
        )(self.place, self.own, self.back)


def neighbours(grid, v, reach):
    out = [v]
    for offset in range(1, reach + 1):
        for by in (offset, -offset):
            pairs = [(i, i + by) for i in range(grid.total) if 0 <= i + by < grid.total]
            out.append(lax.ppermute(v, AXES, pairs))
    return out


def layer_norm(inputs, scale_gain, offset_bias):
    centre = jnp.mean(inputs, axis=-1, keepdims=True)
    centred = inputs - centre
    spread = jnp.mean(centred * centred, axis=-1, keepdims=True)
    return centred * lax.rsqrt(spread + norm_eps) * scale_gain + offset_bias


def dot(a, b, dims=NN):
    return lax.dot_general(a, b, dims, preferred_element_type=f32)

def attend_body(q_ref, k_ref, v_ref, o_ref, lse_ref):
    t = q_ref.shape[0]
    first = lax.broadcasted_iota(jnp.int32, (t, 2 * HEAD), 1) < HEAD
    q, k, v = q_ref[...], k_ref[...], v_ref[...]
    out, totals = [], []
    for side in range(2):
        keep = first if side == 0 else jnp.logical_not(first)
        s = dot(q, jnp.where(keep, k, jnp.zeros_like(k)), NT)
        top = jnp.max(s, axis=-1, keepdims=True)
        p = jnp.exp((s - top) * HEAD ** -0.5)
        total = jnp.sum(p, axis=-1, keepdims=True)
        o = dot((p * (1.0 / total)).astype(bf16), jnp.where(keep, v, jnp.zeros_like(v)))
        out.append(o)
        totals.append(top * HEAD ** -0.5 + jnp.log(total))
    o_ref[...] = (out[0] + out[1]).astype(bf16)
    lse_ref[...] = jnp.where(first, totals[0], totals[1])

def attend(qkv):
    t, width = qkv.shape
    n = width // 3 // (2 * HEAD)
    spec = lambda off: pl.BlockSpec((t, 2 * HEAD), lambda i, off=off: (0, off * n + i))
    return pl.pallas_call(
        attend_body, grid=(n,),
        in_specs=[spec(0), spec(1), spec(2)],
        out_specs=[spec(0), spec(0)],
        out_shape=[jax.ShapeDtypeStruct((t, width // 3), bf16), jax.ShapeDtypeStruct((t, width // 3), f32)],
        compiler_params=pltpu.CompilerParams(vmem_limit_bytes=48 << 20),
        cost_estimate=FREE,
        name="attend",
    )(qkv, qkv, qkv)

def attend_back_body(q_ref, k_ref, v_ref, do_ref, lse_ref, dq_ref, dk_ref, dv_ref):
    t = q_ref.shape[0]
    first = lax.broadcasted_iota(jnp.int32, (t, 2 * HEAD), 1) < HEAD
    q, k, v, do = q_ref[...], k_ref[...], v_ref[...], do_ref[...]
    zero = jnp.zeros_like(k)
    dq = dk = dv = None
    for side in range(2):
        keep = first if side == 0 else jnp.logical_not(first)
        km, vm = jnp.where(keep, k, zero), jnp.where(keep, v, zero)
        qm, dom = jnp.where(keep, q, zero), jnp.where(keep, do, zero)
        lse = lse_ref[:, side * HEAD:side * HEAD + 1]
        p = jnp.exp(dot(q, km, NT) * HEAD ** -0.5 - lse)
        dp = dot(do, vm, NT)
        inner = jnp.sum(p * dp, axis=-1, keepdims=True)
        ds = (p * ((dp - inner) * HEAD ** -0.5)).astype(bf16)
        dq_ = dot(ds, km)
        dv_ = dot(dom, p.astype(bf16), TN)
        dk_ = dot(qm, ds, TN)
        dq = dq_ if dq is None else dq + dq_
        dv = dv_ if dv is None else dv + dv_
        dk = dk_ if dk is None else dk + dk_
    dq_ref[...] = dq.astype(bf16)
    dk_ref[...] = dk.T.astype(bf16)
    dv_ref[...] = dv.T.astype(bf16)

def attend_back(qkv, d_attended, lse):
    t, width = qkv.shape
    n = width // 3 // (2 * HEAD)
    spec = lambda off: pl.BlockSpec((t, 2 * HEAD), lambda i, off=off: (0, off * n + i))
    shape = jax.ShapeDtypeStruct((t, width // 3), bf16)
    return pl.pallas_call(
        attend_back_body, grid=(n,),
        in_specs=[spec(0), spec(1), spec(2), spec(0), spec(0)],
        out_specs=[spec(0)] * 3,
        out_shape=[shape] * 3,
        compiler_params=pltpu.CompilerParams(vmem_limit_bytes=48 << 20),
        cost_estimate=FREE,
        name="attend_back",
    )(qkv, qkv, qkv, d_attended, lse)

def gelu_parts(v):
    e = jnp.exp(-0.5 * v * v)
    t = 1.0 / (1.0 + (0.3275911 * 0.5 ** 0.5) * jnp.abs(v))
    poly = t * (0.127414796 + t * (-0.142248368 + t * (0.7107068705 + t * (-0.7265760135 + t * 0.5307027145))))
    tail = poly * e
    phi = jnp.where(v < 0, tail, 1.0 - tail)
    return v * phi, phi + v * (e * (2.0 * math.pi) ** -0.5)

def mlp_in_body(n_ref, w_ref, b_ref, act_ref, slope_ref):
    v = dot(n_ref[...], w_ref[...]) + b_ref[...]
    act, slope = gelu_parts(v)
    act_ref[...] = act.astype(bf16)
    slope_ref[...] = slope.astype(bf16)

def mlp_in(normed, w, bias, block=512):
    t, d = normed.shape
    ff = w.shape[1]
    out = pl.BlockSpec((t, block), lambda i: (0, i))
    shape = jax.ShapeDtypeStruct((t, ff), bf16)
    return pl.pallas_call(
        mlp_in_body, grid=(ff // block,),
        in_specs=[pl.BlockSpec((t, d), lambda i: (0, 0)), pl.BlockSpec((d, block), lambda i: (0, i)), pl.BlockSpec((1, block), lambda i: (0, i))],
        out_specs=[out, out], out_shape=[shape, shape],
        compiler_params=pltpu.CompilerParams(vmem_limit_bytes=48 << 20),
        cost_estimate=FREE,
        name="mlp_in",
    )(normed, w, bias.reshape(1, -1))

def mlp_back_body(dy_ref, slope_ref, w1_ref, w2_ref, dpre_ref, db_ref, dn_ref):
    g = dot(dy_ref[...], w2_ref[...], NT) * slope_ref[...].astype(f32)
    low = g.astype(bf16)
    dpre_ref[...] = low
    db_ref[...] = jnp.sum(low.astype(f32), axis=0, keepdims=True)
    dn = dot(low, w1_ref[...], NT)
    @pl.when(pl.program_id(0) == 0)
    def _(): dn_ref[...] = dn
    @pl.when(pl.program_id(0) > 0)
    def _(): dn_ref[...] += dn

def mlp_back(dy, slope, w1, w2, block=512):
    t, d = dy.shape
    ff = w1.shape[1]
    whole = pl.BlockSpec((t, d), lambda i: (0, 0))
    part = pl.BlockSpec((t, block), lambda i: (0, i))
    return pl.pallas_call(
        mlp_back_body, grid=(ff // block,),
        in_specs=[whole, part, pl.BlockSpec((d, block), lambda i: (0, i)), pl.BlockSpec((block, d), lambda i: (i, 0))],
        out_specs=[part, pl.BlockSpec((1, block), lambda i: (0, i)), whole],
        out_shape=[jax.ShapeDtypeStruct((t, ff), bf16), jax.ShapeDtypeStruct((1, ff), f32), jax.ShapeDtypeStruct((t, d), f32)],
        compiler_params=pltpu.CompilerParams(vmem_limit_bytes=48 << 20),
        cost_estimate=FREE,
        name="mlp_back",
    )(dy, slope, w1, w2)

def side_steps(x, side):
    n = x.shape[0]
    b = lax.rem(lax.broadcasted_iota(jnp.int32, x.shape, 0), side)
    before = jnp.where(b == 0, 0.0, pltpu.roll(x, 1, 0))
    after = jnp.where(b == side - 1, 0.0, pltpu.roll(x, n - 1, 0))
    return before, after

def up(x, by):
    return jnp.concatenate([jnp.zeros((by, x.shape[1]), x.dtype), x[:-by]], 0)

def down(x, by):
    return jnp.concatenate([x[by:], jnp.zeros((by, x.shape[1]), x.dtype)], 0)

def adapter_body(n_pieces, side, pos_ref, *refs):
    pieces, (w_ref, table_ref, dy_ref, proj_ref, spat_ref, rows_ref, dg_ref, dys_ref) = refs[:n_pieces], refs[n_pieces:]
    x = table_ref[BIAS_PROJ : BIAS_PROJ + 1]
    for k in range(n_pieces):
        x = x + dot(pieces[k][...], w_ref[lax.rem(pos_ref[0] - k + n_pieces, n_pieces)])
    proj_ref[...] = x
    before, after = side_steps(x, side)
    w = table_ref[DEPTH : DEPTH + 9]
    y = [before * w[3 * s:3 * s + 1] + x * w[3 * s + 1:3 * s + 2] + after * w[3 * s + 2:3 * s + 3] for s in range(3)]
    spatial = up(y[0], side) + y[1] + down(y[2], side) + table_ref[BIAS_DEPTH : BIAS_DEPTH + 1]
    spat_ref[...] = spatial
    rows_ref[...] = jnp.sum(spatial, axis=0, keepdims=True)
    dy = dy_ref[...].astype(f32)
    dg_ref[...] = jnp.sum(dy * spatial, axis=0, keepdims=True)
    dys_ref[...] = jnp.sum(dy, axis=0, keepdims=True)

def adapter(pos, pieces, w_proj, table, dy, side=PS, block=256):
    t, d = dy.shape
    n, width = len(pieces), pieces[0].shape[1]
    whole = pl.BlockSpec((t, width), lambda i: (0, 0))
    part = pl.BlockSpec((t, block), lambda i: (0, i))
    row = pl.BlockSpec((1, block), lambda i: (0, i))
    big, line = jax.ShapeDtypeStruct((t, d), f32), jax.ShapeDtypeStruct((1, d), f32)
    return pl.pallas_call(
        functools.partial(adapter_body, n, side), grid=(d // block,),
        in_specs=[pl.BlockSpec(memory_space=pltpu.SMEM)] + [whole] * n + [pl.BlockSpec((n, width, block), lambda i: (0, 0, i)), pl.BlockSpec((table.shape[0], block), lambda i: (0, i)), part],
        out_specs=[part, part, row, row, row], out_shape=[big, big, line, line, line],
        compiler_params=pltpu.CompilerParams(vmem_limit_bytes=48 << 20),
        cost_estimate=FREE,
        name="adapter",
    )(pos.reshape(1).astype(jnp.int32), *pieces, w_proj.reshape(n, width, d), table, dy)

def adapter_back_body(side, dy_ref, proj_ref, gate_ref, dr_ref, table_ref, dp_ref, dwd_ref, dbd_ref, dbp_ref):
    ds = dy_ref[...].astype(f32) * gate_ref[...] + dr_ref[...]
    dbd_ref[...] = jnp.sum(ds, axis=0, keepdims=True)
    before, after = side_steps(ds, side)
    w = table_ref[DEPTH : DEPTH + 9]
    y = [after * w[3 * s:3 * s + 1] + ds * w[3 * s + 1:3 * s + 2] + before * w[3 * s + 2:3 * s + 3] for s in range(3)]
    low = (down(y[0], side) + y[1] + up(y[2], side)).astype(bf16)
    dp_ref[...] = low
    dbp_ref[...] = jnp.sum(low.astype(f32), axis=0, keepdims=True)
    x = proj_ref[...]
    x_before, x_after = side_steps(x, side)
    for t, c in enumerate((x_before, x, x_after)):
        dwd_ref[t:t + 1] = jnp.sum(ds[side:] * c[:-side], axis=0, keepdims=True)
        dwd_ref[3 + t:4 + t] = jnp.sum(ds * c, axis=0, keepdims=True)
        dwd_ref[6 + t:7 + t] = jnp.sum(ds[:-side] * c[side:], axis=0, keepdims=True)

def adapter_back(dy, projected, gate, d_rows, table, side=PS, block=256):
    t, d = dy.shape
    part = pl.BlockSpec((t, block), lambda i: (0, i))
    row = pl.BlockSpec((1, block), lambda i: (0, i))
    nine = pl.BlockSpec((9, block), lambda i: (0, i))
    line = jax.ShapeDtypeStruct((1, d), f32)
    return pl.pallas_call(
        functools.partial(adapter_back_body, side), grid=(d // block,),
        in_specs=[part, part, row, row, pl.BlockSpec((table.shape[0], block), lambda i: (0, i))], out_specs=[part, nine, row, row],
        out_shape=[jax.ShapeDtypeStruct((t, d), bf16), jax.ShapeDtypeStruct((9, d), f32), line, line],
        compiler_params=pltpu.CompilerParams(vmem_limit_bytes=48 << 20),
        cost_estimate=FREE,
        name="adapter_back",
    )(dy, projected, gate, d_rows, table)


def rows_call(body, name, t, steps, ins, outs, sums):
    b = t // steps

    def spec(shape, by_rows):
        if by_rows:
            return pl.BlockSpec((b, shape[1]), lambda i: (i, 0))
        return pl.BlockSpec(shape, lambda i: (0, 0))

    out_specs = [pl.BlockSpec((b, w), lambda i: (i, 0)) for w, _ in outs]
    shapes = [jax.ShapeDtypeStruct((t, w), dt) for w, dt in outs]
    if sums:
        out_specs.append(pl.BlockSpec(sums, lambda i: (0, 0)))
        shapes.append(jax.ShapeDtypeStruct(sums, f32))
    return pl.pallas_call(
        body,
        grid=(steps,),
        in_specs=[spec(a.shape, by_rows) for a, by_rows in ins],
        out_specs=out_specs,
        out_shape=shapes,
        compiler_params=pltpu.CompilerParams(vmem_limit_bytes=48 << 20),
        cost_estimate=FREE,
        name=name,
    )(*[a for a, _ in ins])


def add_sums(ref, values):
    total = jnp.concatenate([jnp.sum(v, axis=0, keepdims=True) for v in values], 0)

    @pl.when(pl.program_id(0) == 0)
    def _():
        ref[...] = total

    @pl.when(pl.program_id(0) > 0)
    def _():
        ref[...] += total


def norm_parts(x):
    centred = x - jnp.mean(x, axis=-1, keepdims=True)
    rstd = lax.rsqrt(jnp.mean(centred * centred, axis=-1, keepdims=True) + norm_eps)
    return centred * rstd, rstd


def norm_back(d_normed, x, gain):
    xhat, rstd = norm_parts(x)
    u = d_normed * gain
    shift = jnp.mean(u, axis=-1, keepdims=True)
    slope = jnp.mean(u * xhat, axis=-1, keepdims=True)
    return (u - shift - xhat * slope) * rstd, d_normed * xhat


def attn_out_norm(attended, w, x, table):
    def body(a_ref, w_ref, x_ref, t_ref, first_ref, n_ref):
        first = x_ref[...].astype(f32) + dot(a_ref[...], w_ref[...]) + t_ref[BIAS_OUT : BIAS_OUT + 1]
        first_ref[...] = first
        xhat, _ = norm_parts(first)
        n_ref[...] = (
            xhat * t_ref[LN2_GAIN : LN2_GAIN + 1] + t_ref[LN2_BIAS : LN2_BIAS + 1]
        ).astype(bf16)

    t, d = x.shape
    ins = [(attended, True), (w, False), (x, True), (table, False)]
    return rows_call(body, "attn_out", t, 4, ins, [(d, f32), (d, bf16)], None)


def norm_two_back(d_normed2, first_sum, dy, table, w):
    def body(dn_ref, x_ref, dy_ref, t_ref, w_ref, first_ref, branch_ref, att_ref, sum_ref):
        dn = dn_ref[...]
        dx, scaled = norm_back(dn, x_ref[...], t_ref[LN2_GAIN : LN2_GAIN + 1])
        first = dy_ref[...].astype(f32) + dx
        low = first.astype(bf16)
        first_ref[...] = first
        branch_ref[...] = low
        att_ref[...] = dot(low, w_ref[...], NT).astype(bf16)
        add_sums(sum_ref, (scaled, dn, low.astype(f32)))

    t, d = dy.shape
    ins = [(d_normed2, True), (first_sum, True), (dy, True), (table, False), (w, False)]
    return rows_call(body, "norm_two", t, 4, ins, [(d, f32), (d, bf16), (d, bf16)], (3, d))


def norm_one_back(parts, w, x, d_first, table):
    def body(q_ref, k_ref, v_ref, w_ref, x_ref, first_ref, t_ref, out_ref, sum_ref):
        d = x_ref.shape[1]
        q, k, v = q_ref[...], k_ref[...], v_ref[...]
        dn = dot(q, w_ref[:, :d], NT) + dot(k, w_ref[:, d : 2 * d], NT) + dot(v, w_ref[:, 2 * d :], NT)
        dx, scaled = norm_back(dn, x_ref[...].astype(f32), t_ref[LN1_GAIN : LN1_GAIN + 1])
        out_ref[...] = (first_ref[...] + dx).astype(bf16)
        add_sums(sum_ref, (scaled, dn, q.astype(f32), v.astype(f32)))

    t, d = x.shape
    ins = [(p, True) for p in parts] + [(w, False), (x, True), (d_first, True), (table, False)]
    return rows_call(body, "norm_one", t, 4, ins, [(d, bf16)], (4, d))


def columns_call(body, name, block, ins, width, dtype):
    t = ins[0][0].shape[0]

    def spec(shape, by_columns):
        if by_columns:
            return pl.BlockSpec((shape[0], block), lambda i: (0, i))
        return pl.BlockSpec(shape, lambda i: (0, 0))

    return pl.pallas_call(
        body,
        grid=(width // block,),
        in_specs=[spec(a.shape, by) for a, by in ins],
        out_specs=pl.BlockSpec((t, block), lambda i: (0, i)),
        out_shape=jax.ShapeDtypeStruct((t, width), dtype),
        compiler_params=pltpu.CompilerParams(vmem_limit_bytes=48 << 20),
        cost_estimate=FREE,
        name=name,
    )(*[a for a, _ in ins])


def project(normed, w, bias):
    def body(n_ref, w_ref, b_ref, out_ref):
        out_ref[...] = (dot(n_ref[...], w_ref[...]) + b_ref[...]).astype(bf16)

    ins = [(normed, False), (w, True), (bias, True)]
    return columns_call(body, "project", 512, ins, w.shape[1], bf16)


def layer_output(activation, w, first_sum, table, gate, spatial):
    def body(a_ref, w_ref, x_ref, t_ref, g_ref, s_ref, out_ref):
        total = x_ref[...] + dot(a_ref[...], w_ref[...]) + t_ref[BIAS_FC2 : BIAS_FC2 + 1]
        out_ref[...] = (total + g_ref[...] * s_ref[...]).astype(bf16)

    ins = [(activation, False), (w, True), (first_sum, True), (table, True), (gate, True), (spatial, True)]
    return columns_call(body, "layer_output", 256, ins, w.shape[1], bf16)


def dot3(x, w, dims=NN):
    a = x.astype(bf16)
    rest = x - a.astype(f32)
    b = rest.astype(bf16)
    c = (rest - b.astype(f32)).astype(bf16)
    return dot(a, w, dims) + dot(b, w, dims) + dot(c, w, dims)


def gate_body(n_near, tokens, d, *refs):
    near, refs = refs[:n_near], refs[n_near:]
    win_ref, wout_ref, gate_ref, drows_ref, pack_ref, sum_ref = refs
    own = near[0][:, 2 * d :]
    match = [(near[i][:, 2 * d :] == own).astype(f32) for i in range(n_near)]
    count = functools.reduce(lambda a, b: a + b, match)[:, :1] * tokens
    rows = d_gates = None
    for i in range(n_near):
        weight = match[i][:, :1]
        row, d_gate = weight * near[i][:, :d], weight * near[i][:, d : 2 * d]
        rows = row if i == 0 else rows + row
        d_gates = d_gate if i == 0 else d_gates + d_gate
    second = lax.broadcasted_iota(jnp.int32, (8, d), 0) == 1
    mean = jnp.broadcast_to(rows / count, (8, d))
    d_gate = jnp.where(second, jnp.broadcast_to(d_gates, (8, d)), jnp.broadcast_to(near[0][:, d : 2 * d], (8, d)))
    win, wout = win_ref[...], wout_ref[...]
    act, slope = gelu_parts(dot3(mean, win))
    gate = jnp.tanh(dot3(act, wout, NT))
    d_pre = d_gate * (1.0 - gate * gate)
    d_hidden = dot3(d_pre, wout) * slope
    d_mean = dot3(d_hidden, win, NT)
    gate_ref[...] = gate[:1]
    drows_ref[...] = d_mean[1:2] / count
    sum_ref[...] = jnp.zeros((1, 128), f32) + jnp.sum(gate[:1])
    at = 0
    for v, order in ((mean, (0, 0, 1)), (d_pre, (0, 0, 1)), (d_hidden, (0, 1, 0)), (act, (0, 1, 0))):
        line = jnp.broadcast_to(v[:1], v.shape)
        high = line.astype(bf16)
        low = (line - high.astype(f32)).astype(bf16)
        place = lax.broadcasted_iota(jnp.int32, v.shape, 0)
        kind = jnp.where(place == 1, order[1], jnp.where(place == 2, order[2], 0))
        pick = jnp.where(kind == 1, low.astype(f32), high.astype(f32))
        pack_ref[:, at : at + v.shape[1]] = jnp.where(place < 3, pick, 0.0).astype(bf16)
        at += v.shape[1]


def gate_step(near, gates, d, hidden, tokens):
    n = len(near)

    def line(k):
        return jax.ShapeDtypeStruct((1, k), f32)

    def at(k):
        return pl.BlockSpec((1, k), lambda j: (0, 0))

    k = 2 * d + 2 * hidden
    return pl.pallas_call(
        functools.partial(gate_body, n, tokens, d),
        grid=(1,),
        in_specs=[at(2 * d + 128)] * n
        + [pl.BlockSpec((d, hidden), lambda j, b=b: (0, b)) for b in range(2)],
        out_specs=[at(d), at(d), pl.BlockSpec((8, k), lambda j: (0, 0)), at(128)],
        out_shape=[line(d), line(d), jax.ShapeDtypeStruct((8, k), bf16), line(128)],
        compiler_params=pltpu.CompilerParams(vmem_limit_bytes=32 << 20),
        cost_estimate=FREE,
        name="gate",
    )(*near, gates, gates)


def pool_table(coarse_side, fine_side):
    coarse, fine = np.arange(coarse_side)[:, None], np.arange(fine_side)[None]
    start = coarse * fine_side // coarse_side
    end = ((coarse + 1) * fine_side + coarse_side - 1) // coarse_side
    single = np.where((fine >= start) & (fine < end), 1.0, 0.0) / (end - start)
    return np.kron(single, single)


def token_sum(values):
    return jnp.sum(values.astype(f32), axis=0)


def shards(
    tokens,
    features,
    sample_of,
    cotangent,
    ln1_gain,
    ln1_bias,
    w_qkv,
    bias_qv,
    w_attn_out,
    bias_attn_out,
    ln2_gain,
    ln2_bias,
    w_fc1,
    bias_fc1,
    w_fc2,
    bias_fc2,
    w_proj,
    bias_proj,
    w_depth,
    bias_depth,
    w_gate_in,
    w_gate_out,
):
    grid = Grid()
    rows = ln1_gain.shape[0]
    total = grid.total
    x, dy = tokens[0], cotangent[0]
    count, d = x.shape
    hidden = w_gate_in.shape[1]

    vectors = [ln1_gain, ln1_bias, bias_attn_out, ln2_gain, ln2_bias, bias_fc2, bias_proj, bias_depth]
    a_small = GatherSmall(
        grid, jnp.concatenate(vectors + [w_depth.reshape(-1), bias_qv, bias_fc1])
    )
    gate_out_rows = dot(jnp.eye(rows, dtype=bf16), w_gate_out, NT).astype(bf16)
    gates = jnp.concatenate([w_gate_in, gate_out_rows], 1)
    full_qkv = lax.all_gather(w_qkv, AXES, axis=0, tiled=True)
    a_two = Gather(grid, (w_attn_out, w_fc1))
    a_three = Gather(grid, (gates, w_proj))

    n_ch = lax.axis_size("ch")
    ch = lax.axis_index("ch")
    n_img, own_ch = features.shape[0], features.shape[1]
    core = grid.pos["c"]

    def along_ch(v, by):
        img = lax.axis_size("img")
        pairs = [
            (i * n_ch + j, i * n_ch + (j + by) % n_ch) for i in range(img) for j in range(n_ch)
        ]
        return lax.ppermute(v, AXES, pairs)

    def peer(v):
        return grid.send(v, "c", 1)

    def peer_half(v):
        h = v.shape[1] // 2
        return grid.send(lax.dynamic_slice(v, (0, (1 - core) * h), (v.shape[0], h)), "c", 1)

    def step(active, *values):
        states, values = lax.optimization_barrier(([a.state() for a in active], values))
        for a, state in zip(active, states):
            a.set_state(state)
        return values

    a_two.along_z()
    for _ in range(3):
        a_small.next()
    pool = jnp.asarray(pool_table(PS, FS), bf16)
    pooled_own = dot(pool, features.reshape(n_img * own_ch, -1), NT).astype(bf16)
    a_two.pack_first()
    a_small.v, pooled_own = step((a_two,), a_small.v, pooled_own)

    a_two.first()
    a_two.pack_second()
    while a_small.next():
        pass
    every, pooled_own, w_fc2 = step((a_two, a_three), a_small.v, pooled_own, w_fc2)

    full_fc2 = lax.all_gather(w_fc2, AXES, axis=0, tiled=True)
    a_two.second()
    a_two.early()
    every = every.astype(f32)
    table = every[:, : LINES * rows].reshape(total, LINES, rows)
    table = table.transpose(1, 0, 2).reshape(LINES, d)
    at = LINES * rows
    full_bias_qv = every[:, at : at + 2 * rows].reshape(-1)
    full_bias_fc1 = every[:, at + 2 * rows :].reshape(1, -1)
    bias_qkv = jnp.concatenate([full_bias_qv[:d], jnp.zeros((d,), f32), full_bias_qv[d:]])[None]
    x32 = x.astype(f32)
    normed1 = layer_norm(x32, table[LN1_GAIN], table[LN1_BIAS]).astype(bf16)
    qkv = project(normed1, full_qkv, bias_qkv)
    attended, log_total = attend(qkv)
    attended, log_total, table, full_bias_fc1, pooled_own = step(
        (a_two, a_three), attended, log_total, table, full_bias_fc1, pooled_own
    )

    a_two.cross()
    dy_far = peer_half(dy)
    attended, pooled_own, dy_far = step((a_two, a_three), attended, pooled_own, dy_far)

    a_three.along_z()
    a_three.pack_first()

    def pooled_piece(k):
        to = lax.rem(ch + k, n_ch)
        piece = lax.dynamic_slice(pooled_own, (0, to * own_ch), (count, own_ch))
        return along_ch(piece, k) if k else piece

    early = n_ch // 2 + 1
    pieces = [pooled_piece(k) for k in range(early)]
    full_attn_out, full_fc1 = a_two.whole()
    first_sum, normed2 = attn_out_norm(attended, full_attn_out, x, table)
    activation, slope = mlp_in(normed2, full_fc1, full_bias_fc1)
    activation, slope, normed2, full_attn_out, full_fc1, first_sum, pieces, pooled_own = step(
        (a_three,),
        activation,
        slope,
        normed2,
        full_attn_out,
        full_fc1,
        first_sum,
        pieces,
        pooled_own,
    )

    a_three.first()
    a_three.pack_second()
    activation_far, normed2_far = peer(activation), peer(normed2)
    pieces = pieces + [pooled_piece(k) for k in range(early, n_ch)]
    activation_far, normed2_far, slope, attended, pieces = step(
        (a_three,), activation_far, normed2_far, slope, attended, pieces
    )

    a_three.second()
    ff = activation.shape[1]
    s_one = Scatter(
        grid,
        [(activation, activation_far, dy, dy_far, 0, None, 0, ff, d // 2, 0, 0)],
        2 * ff // total,
        d // 4,
    )
    slope, attended = step((a_three, s_one), slope, attended)

    s_one.first()
    d_pre, d_bias_fc1, d_normed2 = mlp_back(dy, slope, full_fc1, full_fc2)
    d_first, d_branch, d_attended, sums_two = norm_two_back(
        d_normed2, first_sum, dy, table, full_attn_out
    )
    s_one.got, d_attended = lax.optimization_barrier((s_one.got, d_attended))
    s_one.fold_second()
    d_attended, d_first, d_branch, d_pre, full_fc2, attended, pieces = step(
        (s_one, a_three), d_attended, d_first, d_branch, d_pre, full_fc2, attended, pieces
    )

    s_one.second()
    a_three.early()
    a_three.cross()
    d_pre_far, d_branch_far = peer_half(d_pre), peer_half(d_branch)
    attended_far = peer(attended)
    s_one.fold_z()
    d_attended, d_branch, d_pre, d_pre_far, d_branch_far, attended_far = step(
        (s_one, a_three), d_attended, d_branch, d_pre, d_pre_far, d_branch_far, attended_far
    )

    s_one.along_z()
    full_gates, full_proj = a_three.whole()
    s_two = Scatter(
        grid,
        [
            (normed2, normed2_far, d_pre, d_pre_far, 0, None, 0, d, ff // 2, 0, 0),
            (attended, attended_far, d_branch, d_branch_far, 0, None, 0, d, d // 2, 0, ff // 4),
        ],
        2 * rows,
        (ff + d) // 4,
    )
    d_attended, normed1, pieces, full_gates, full_proj = step(
        (s_two,), d_attended, normed1, pieces, full_gates, full_proj
    )

    s_two.first()
    projected, spatial, row_sums, d_gate, dy_sum = adapter(ch, pieces, full_proj, table, dy)
    d_query, d_key, d_value = attend_back(qkv, d_attended, log_total)
    s_two.got, d_query, row_sums = lax.optimization_barrier((s_two.got, d_query, row_sums))
    s_two.fold_second()
    d_query, d_key, d_value, normed1, row_sums, d_gate, dy_sum, pieces = step(
        (s_one, s_two), d_query, d_key, d_value, normed1, row_sums, d_gate, dy_sum, pieces
    )

    ids_plus = sample_of.astype(f32) + 1.0
    carried = jnp.concatenate(
        [row_sums, d_gate, jnp.broadcast_to(ids_plus[:, None], (1, 128))], 1
    )
    near = neighbours(grid, carried, REACH)
    pooled = jnp.zeros((count, n_ch * own_ch), bf16)
    for k in range(n_ch):
        from_ch = lax.rem(ch - k + n_ch, n_ch)
        pooled = lax.dynamic_update_slice(pooled, pieces[k], (0, from_ch * own_ch))
    d_mixed = jnp.concatenate([d_query, d_key, d_value], -1)
    d_mixed_far, normed1_far = peer_half(d_mixed), peer(normed1)
    d_mixed, d_mixed_far, normed1_far, near, pooled = step(
        (s_two,), d_mixed, d_mixed_far, normed1_far, near, pooled
    )

    pooled_far = peer(pooled)
    gate, d_rows, pack, gate_sum = gate_step(near, full_gates, d, hidden, count)
    d_projected, d_depth, d_bias_depth, d_bias_proj = adapter_back(
        dy, projected, gate, d_rows, table
    )
    d_pooled = dot(d_projected, full_proj, NT).astype(bf16)
    pack, d_projected, pooled_far, gate, d_mixed, d_pooled = step(
        (s_two,), pack, d_projected, pooled_far, gate, d_mixed, d_pooled
    )

    pack_far, d_projected_far = peer(pack), peer_half(d_projected)
    lines = jnp.concatenate([sums_two[2:], sums_two[:2], dy_sum, d_bias_proj, d_bias_depth, d_depth], 0)
    lines = lines.reshape(LINES - 2, total, rows).transpose(1, 0, 2).reshape(total, -1)
    small = jnp.concatenate(
        [lines, d_bias_fc1.reshape(total, -1), jnp.broadcast_to(gate_sum, (total, 128))], 1
    )
    s_two.second()
    back = []
    for k in range(n_ch):
        to = lax.rem(ch + k, n_ch)
        piece = lax.dynamic_slice(d_pooled, (0, to * own_ch), (count, own_ch))
        back.append(along_ch(piece, k) if k else piece)
    wide, low = 3 * d // 4, hidden // 4
    half = d // (hidden // 2)
    s_three = Scatter(
        grid,
        [
            (normed1, normed1_far, d_mixed, d_mixed_far, 0, None, 0, d, 3 * d // 2, 0, 0),
            (pack, pack_far, pack, pack_far, 2 * half, 2 * half, 0, d, hidden // 2, 0, wide),
            (
                pack,
                pack_far,
                pack,
                pack_far,
                2 * half + 2,
                2 * half + 2,
                grid.n["z"],
                d,
                hidden // 2,
                0,
                wide + low,
            ),
            (
                pooled,
                pooled_far,
                d_projected,
                d_projected_far,
                0,
                None,
                0,
                pooled.shape[1],
                d // 2,
                0,
                wide + 2 * low,
            ),
        ],
        2 * rows,
        wide + 2 * low + pooled.shape[1] // 4,
    )
    s_two.more, s_three.away = lax.optimization_barrier((s_two.more, s_three.away))
    s_two.fold_z()
    d_query, d_key, d_value, activation, back, small = step(
        (s_one, s_two, s_three), d_query, d_key, d_value, activation, back, small
    )

    s_three.first()
    s_two.along_z()
    grad_tokens, sums_one = norm_one_back(
        (d_query, d_key, d_value), full_qkv, x, d_first, table
    )
    layer_out = layer_output(activation, full_fc2, first_sum, table, gate, spatial)
    s_three.got, layer_out, grad_tokens = lax.optimization_barrier(
        (s_three.got, layer_out, grad_tokens)
    )
    s_three.fold_second()
    layer_out, grad_tokens, sums_one, small, back = step(
        (s_one, s_two, s_three), layer_out, grad_tokens, sums_one, small, back
    )

    s_three.second()
    ones = sums_one[:2].reshape(2, total, rows).transpose(1, 0, 2).reshape(total, -1)
    d_bias_qv = sums_one[2:].reshape(total, -1)
    s_small = ScatterSmall(grid, jnp.concatenate([ones, small, d_bias_qv], 1))
    s_one.last()
    s_two.last()
    s_small.next()
    s_small.next()
    s_three.fold_z()
    s_small.v, back = step((s_one, s_two, s_three), s_small.v, back)

    s_three.along_z()
    while s_small.left:
        s_small.next()
    (g_fc2,) = s_one.results()
    g_fc1, g_attn_out = s_two.results()
    s_small.v, back, g_fc2, g_fc1 = step((s_three,), s_small.v, back, g_fc2, g_fc1)

    d_local = jnp.zeros((n_img, count, own_ch), bf16)
    for k in range(n_ch):
        from_ch = lax.rem(ch - k + n_ch, n_ch)
        d_local = lax.dynamic_update_slice(d_local, back[k][None], (from_ch, 0, 0))
    grad_features = jnp.einsum("kpc,pf->kcf", d_local, pool, preferred_element_type=f32).astype(bf16)
    s_three.last()
    summed = s_small.v[0]
    gate_mean = summed[-2 * rows - 1] / (total * d)
    g_qkv, g_gate_in, g_gate_out, g_proj = s_three.results()

    def owned(i):
        return summed[i * rows : (i + 1) * rows]

    return (
        layer_out[None],
        grad_tokens[None],
        grad_features,
        owned(LN1_GAIN),
        owned(LN1_BIAS),
        g_qkv,
        summed[-2 * rows :],
        g_attn_out,
        owned(BIAS_OUT),
        owned(LN2_GAIN),
        owned(LN2_BIAS),
        g_fc1,
        summed[at : at + 4 * rows],
        g_fc2,
        owned(BIAS_FC2),
        g_proj,
        owned(BIAS_PROJ),
        summed[DEPTH * rows : at].reshape(9, rows),
        owned(BIAS_DEPTH),
        g_gate_in,
        g_gate_out.T,
        gate_mean,
    )


def solution(mesh):
    return jax.shard_map(
        shards,
        mesh=mesh,
        in_specs=(
            P(("img", "ch"), None, None),
            P("img", "ch", None),
            P(("img", "ch")),
            P(("img", "ch"), None, None),
            P(("img", "ch")),
            P(("img", "ch")),
            P(("img", "ch"), None),
            P(("img", "ch")),
            P(("img", "ch"), None),
            P(("img", "ch")),
            P(("img", "ch")),
            P(("img", "ch")),
            P(("img", "ch"), None),
            P(("img", "ch")),
            P(("img", "ch"), None),
            P(("img", "ch")),
            P(("img", "ch"), None),
            P(("img", "ch")),
            P(None, ("img", "ch")),
            P(("img", "ch")),
            P(("img", "ch"), None),
            P(None, ("img", "ch")),
        ),
        out_specs=(
            P(("img", "ch"), None, None),
            P(("img", "ch"), None, None),
            P("img", "ch", None),
            P(("img", "ch")),
            P(("img", "ch")),
            P(("img", "ch"), None),
            P(("img", "ch")),
            P(("img", "ch"), None),
            P(("img", "ch")),
            P(("img", "ch")),
            P(("img", "ch")),
            P(("img", "ch"), None),
            P(("img", "ch")),
            P(("img", "ch"), None),
            P(("img", "ch")),
            P(("img", "ch"), None),
            P(("img", "ch")),
            P(None, ("img", "ch")),
            P(("img", "ch")),
            P(("img", "ch"), None),
            P(None, ("img", "ch")),
            P(),
        ),
        check_vma=False,
    )
```

```python
import functools
import math

import jax
import numpy as np
import jax.numpy as jnp
from jax import lax
from jax.experimental import pallas as pl
from jax.experimental.pallas import tpu as pltpu
from jax.sharding import PartitionSpec as P

HEAD = 64
PS = 24
FS = 32
REACH = 3
LN1_GAIN, LN1_BIAS, BIAS_OUT, LN2_GAIN, LN2_BIAS, BIAS_FC2, BIAS_PROJ, BIAS_DEPTH, DEPTH = range(9)
LINES = DEPTH + 9

norm_eps = 1e-05
highest = lax.Precision.HIGHEST
f32, bf16 = jnp.float32, jnp.bfloat16
AXES = ("img", "ch")
FREE = pl.CostEstimate(flops=0, bytes_accessed=0, transcendentals=0)
NN = (((1,), (0,)), ((), ()))
NT = (((1,), (1,)), ((), ()))
TN = (((0,), (0,)), ((), ()))


class Grid:
    def __init__(self):
        img, ch = lax.axis_size("img"), lax.axis_size("ch")
        depth = 4 if img % 4 == 0 else 1
        self.n = {"z": depth, "x": img // depth, "y": ch // 2, "c": 2}
        self.stride = {"c": 1, "y": 2, "x": ch, "z": ch * (img // depth)}
        self.total = img * ch
        me = lax.axis_index(AXES)
        self.me = me
        self.pos = {a: lax.rem(lax.div(me, self.stride[a]), self.n[a]) for a in self.n}

    def send(self, v, axis, by):
        n, s = self.n[axis], self.stride[axis]
        pairs = []
        for i in range(self.total):
            a = (i // s) % n
            pairs.append((i, i + ((a + by) % n - a) * s))
        return lax.ppermute(v, AXES, pairs)

    def other(self, axis, by):
        return lax.rem(self.pos[axis] + by, self.n[axis])

    def swap(self, v, bit):
        return lax.ppermute(v, AXES, [(i, i ^ bit) for i in range(self.total)])


class GatherSmall:
    def __init__(self, grid, v):
        self.grid, self.v, self.bit = grid, v[None], 1

    def next(self):
        got = self.grid.swap(self.v, self.bit)
        pair = (self.v, got)
        upper = jnp.bitwise_and(self.grid.me, self.bit) != 0
        self.v = jnp.where(upper, jnp.concatenate(pair[::-1], 0), jnp.concatenate(pair, 0))
        self.bit *= 2
        return self.bit < self.grid.total


class ScatterSmall:
    def __init__(self, grid, v):
        self.grid, self.v = grid, v
        bits = [1 << i for i in range(grid.total.bit_length() - 1)]
        stride = grid.stride["z"]
        self.left = [b for b in bits if b >= stride][::-1] + [b for b in bits if b < stride][::-1]
        self.shape = {b: 2 for b in bits}

    def next(self):
        bit = self.left.pop(0)
        del self.shape[bit]
        low = 2 ** sum(b < bit for b in self.shape)
        t = self.v.reshape(-1, 2, low, self.v.shape[1])
        upper = (jnp.bitwise_and(self.grid.me, bit) != 0).astype(jnp.int32)
        mine = lax.dynamic_index_in_dim(t, upper, 1, keepdims=False)
        away = lax.dynamic_index_in_dim(t, 1 - upper, 1, keepdims=False)
        mine, away = (u.reshape(-1, t.shape[3]) for u in (mine, away))
        self.v = mine + self.grid.swap(away, bit)


def after(value, done):
    return lax.optimization_barrier((value, done))[0]


class Gather:
    def __init__(self, grid, params):
        self.grid = grid
        self.width = width = min(p.shape[1] for p in params)
        self.q = width // 2
        self.places, blocks, at = [], [], 0
        for i, p in enumerate(params):
            r = p.shape[0]
            held = -(-r // 16) * 16
            for j in range(p.shape[1] // width):
                block = p[:, j * width : (j + 1) * width]
                blocks.append(jnp.pad(block, ((0, held - r), (0, 0))) if held > r else block)
                self.places.append((i, at, r if r % 8 == 0 else held, j * width))
                at += held
        self.shapes = [p.shape for p in params]
        self.shard = jnp.concatenate(blocks, 0)

    def along_z(self):
        g = self.grid
        self.z = [self.shard] + [g.send(self.shard, "z", k) for k in range(1, g.n["z"])]

    def pack_first(self):
        self.s0 = [
            jnp.stack([p[:, i * self.q : (i + 1) * self.q] for p in self.z]) for i in range(2)
        ]
        del self.z

    def first(self):
        self.r1 = [self.every(self.s0[i], "xy"[i]) for i in range(2)]

    def pack_second(self):
        self.s1 = [jnp.concatenate([self.s0[i]] + self.r1[i], 0) for i in range(2)]
        del self.s0, self.r1

    def second(self):
        self.r2 = [self.every(self.s1[i], "yx"[i]) for i in range(2)]

    def early(self):
        self.c1 = [self.over(s) for s in self.s1]

    def cross(self):
        self.c2 = [[self.over(b) for b in r] for r in self.r2]

    def every(self, v, axis):
        return [self.grid.send(v, axis, k) for k in range(1, self.grid.n[axis])]

    def over(self, v):
        return self.grid.send(v, "c", 1)


    def state(self):
        names = ("shard", "z", "s0", "s1", "r1", "r2", "c1", "c2")
        return {k: v for k, v in vars(self).items() if k in names}

    def set_state(self, state):
        for k, v in state.items():
            setattr(self, k, v)

    def whole(self):
        n, q, place_of = self.grid.n, self.q, self.places
        nz, nx, ny = n["z"], n["x"], n["y"]
        arrays, plan = [], []
        for core_rel, (s1, r2) in enumerate(((self.s1, self.r2), (self.c1, self.c2))):
            for part, (first, second) in enumerate((("x", "y"), ("y", "x"))):
                for k2, buf in enumerate([s1[part]] + r2[part]):
                    for k1 in range(n[first]):
                        for kz in range(nz):
                            rel = {first: k1, second: k2}
                            plan.append((len(arrays), k1 * nz + kz, core_rel, part, kz, rel))
                    arrays.append(buf)
        count = len(self.shapes)
        tall = {param: r for param, _, r, _ in place_of}

        def body(place, *refs):
            ins, outs = refs[: len(arrays)], refs[len(arrays) : len(arrays) + count]
            held, (sems, out_sems) = refs[len(arrays) + count : -2], refs[-2:]
            z, x, y, c = place[0], place[1], place[2], place[3]
            waits = [[] for _ in range(nz)]
            for i, j, core_rel, part, kz, rel in plan:
                zz = lax.rem(z - kz + nz, nz)
                xx = lax.rem(x - rel["x"] + nx, nx)
                yy = lax.rem(y - rel["y"] + ny, ny)
                cc = lax.rem(c + core_rel, 2)
                for param, row, r, col in place_of:
                    copy = pltpu.make_async_copy(
                        ins[i].at[j, pl.ds(row, r)],
                        held[param].at[zz, xx, yy, cc, :, pl.ds(col + part * q, q)],
                        sems.at[kz],
                    )
                    copy.start()
                    waits[kz].append(copy)
            after = []
            for kz in range(nz):
                for copy in waits[kz]:
                    copy.wait()
                zz = lax.rem(z - kz + nz, nz)
                for param in range(count):
                    copy = pltpu.make_async_copy(
                        held[param].at[zz], outs[param].at[zz], out_sems.at[kz]
                    )
                    copy.start()
                    after.append(copy)
            for copy in after:
                copy.wait()

        place = jnp.stack([self.grid.pos[a] for a in ("z", "x", "y", "c")]).astype(jnp.int32)
        devices = nz * nx * ny * 2
        room = sum(devices * (r + 8) * w * 2 for r, w in self.shapes)
        shapes = [(nz, nx, ny, 2, tall[i], w) for i, (_, w) in enumerate(self.shapes)]
        whole = pl.pallas_call(
            body,
            out_shape=[jax.ShapeDtypeStruct(s, bf16) for s in shapes],
            in_specs=[pl.BlockSpec(memory_space=pltpu.SMEM)]
            + [pl.BlockSpec(memory_space=pltpu.HBM)] * len(arrays),
            out_specs=[pl.BlockSpec(memory_space=pltpu.HBM)] * count,
            scratch_shapes=[pltpu.VMEM(s, bf16) for s in shapes]
            + [pltpu.SemaphoreType.DMA((nz,)), pltpu.SemaphoreType.DMA((nz,))],
            compiler_params=pltpu.CompilerParams(vmem_limit_bytes=room + (4 << 20)),
            cost_estimate=FREE,
            name="assemble",
        )(place, *arrays)
        return [
            w[:, :, :, :, :r].reshape(devices * r, width) for w, (r, width) in zip(whole, self.shapes)
        ]


def tail_of(r, q, keep):
    extra = r - keep
    return extra, keep // extra, q * extra // keep


def place_share(ref, value, row, col):
    r, q, keep = value.shape[1] // 2, value.shape[2], ref.shape[2] // 2
    if row or r <= keep:
        ref[0, :, row : row + 2 * r, col : col + q] = value
        return
    extra, count, w = tail_of(r, q, keep)
    for c in range(2):
        ref[0, :, c * keep : (c + 1) * keep, col : col + q] = value[:, c * r : c * r + keep]
        for j in range(count):
            at = c * keep + j * extra
            ref[0, :, at : at + extra, col + q : col + q + w] = value[
                :, c * r + keep : (c + 1) * r, j * w : (j + 1) * w
            ]


def weight_grad_body(grid_n, terms, scratch, pos_ref, *refs):
    nx, ny = grid_n
    outs = refs[4 * len(terms) :]
    keep_a, keep_b = outs[0], outs[1]
    away_a, away_b = outs[2 : 1 + ny], outs[1 + ny :]
    for i, (r2, q, row, col) in enumerate(terms):
        l0, l1, r0, r1 = refs[4 * i : 4 * i + 4]
        o = dot(l0[...], r0[...], TN) + dot(l1[...], r1[...], TN)
        o = o.reshape(nx, ny, r2, 2 * q)

        def split_y(y, o=o, row=row, col=col, q=q):
            place_share(keep_a, o[:, y, :, :q].astype(bf16), row, col)
            for k in range(1, ny):
                place_share(away_a[k - 1], o[:, (y + k) % ny, :, :q].astype(bf16), row, col)

        def split_x(x, o=o, row=row, col=col, q=q):
            place_share(keep_b, o[x, :, :, q:].astype(bf16), row, col)
            for k in range(1, nx):
                place_share(away_b[k - 1], o[(x + k) % nx, :, :, q:].astype(bf16), row, col)

        for y in range(ny):
            pl.when(pos_ref[2] == y)(functools.partial(split_y, y))
        for x in range(nx):
            pl.when(pos_ref[1] == x)(functools.partial(split_x, x))


class Scatter:
    def __init__(self, grid, terms, height, width):
        self.grid = grid
        n = grid.n
        nz, nx, ny = n["z"], n["x"], n["y"]
        self.place = jnp.stack([grid.pos[a] for a in ("z", "x", "y", "c")]).astype(jnp.int32)
        self.height, self.width = height, width
        specs, arrays, shapes = [], [], []
        self.parts = []
        for left, left_far, right, right_far, at, at_far, left_at, rows, half, row, col in terms:
            t, band = left.shape[0], rows // nz
            r2, q = band // (nx * ny), half // 2
            lspec = pl.BlockSpec((t, band), lambda i, p, left_at=left_at: (0, left_at + i))
            specs += [lspec, lspec]
            specs += [pl.BlockSpec((t, half), lambda i, p, at=at: (0, at + p[3]))]
            if at_far is None:
                specs += [pl.BlockSpec((t, half), lambda i, p: (0, 0))]
            else:
                specs += [pl.BlockSpec((t, half), lambda i, p, at=at_far: (0, at + p[3]))]
            arrays += [left, left_far, right, right_far]
            shapes.append((r2, q, row, col))
            self.parts.append((r2 // 2, q, row, col))
        a = jax.ShapeDtypeStruct((nz, nx, height, width), bf16)
        b = jax.ShapeDtypeStruct((nz, ny, height, width), bf16)
        sa = pl.BlockSpec((1, nx, height, width), lambda i, p: (i, 0, 0, 0))
        sb = pl.BlockSpec((1, ny, height, width), lambda i, p: (i, 0, 0, 0))
        sums = pl.pallas_call(
            functools.partial(weight_grad_body, (nx, ny), shapes, None),
            grid_spec=pltpu.PrefetchScalarGridSpec(
                num_scalar_prefetch=1,
                grid=(nz,),
                in_specs=specs,
                out_specs=[sa, sb] + [sa] * (ny - 1) + [sb] * (nx - 1),
            ),
            out_shape=[a, b] + [a] * (ny - 1) + [b] * (nx - 1),
            compiler_params=pltpu.CompilerParams(vmem_limit_bytes=56 << 20),
            cost_estimate=FREE,
            name="weight_grad",
        )(self.place, *arrays)
        self.keep = list(sums[:2])
        self.away = [list(sums[2 : 1 + ny]), list(sums[1 + ny :])]

    def state(self):
        names = ("keep", "away", "got", "more", "sent", "kept", "own", "back")
        return {k: v for k, v in vars(self).items() if k in names}

    def set_state(self, state):
        for k, v in state.items():
            setattr(self, k, v)

    def first(self):
        self.got = [
            [self.grid.send(v, "yx"[i], k) for k, v in enumerate(self.away[i], 1)] for i in range(2)
        ]
        del self.away

    def fold_second(self):
        g, n = self.grid, self.grid.n
        nz, counts = n["z"], (n["x"], n["y"])
        block = (nz, 1, self.height, self.width)
        specs, arrays, plan = [], [], []
        for i in range(2):
            for k in range(1, counts[i]):

                def place(_, p, i=i, k=k):
                    return (0, lax.rem(p[1 + i] + k, counts[i]), 0, 0)

                terms = [self.keep[i]] + self.got[i]
                plan.append(len(terms))
                arrays += terms
                specs += [pl.BlockSpec(block, place)] * len(terms)

        def body(pos, *refs):
            at = 0
            for j, count in enumerate(plan):
                total = refs[at][:, 0].astype(f32)
                for ref in refs[at + 1 : at + count]:
                    total = total + ref[:, 0].astype(f32)
                refs[len(arrays) + j][...] = total.astype(bf16)
                at += count

        shape = jax.ShapeDtypeStruct((nz, self.height, self.width), bf16)
        sent = pl.pallas_call(
            body,
            grid_spec=pltpu.PrefetchScalarGridSpec(
                num_scalar_prefetch=1,
                grid=(1,),
                in_specs=specs,
                out_specs=[pl.BlockSpec(shape.shape, lambda i, p: (0, 0, 0))] * len(plan),
            ),
            out_shape=[shape] * len(plan),
            compiler_params=pltpu.CompilerParams(vmem_limit_bytes=56 << 20),
            cost_estimate=FREE,
            name="fold_second",
        )(self.place, *arrays)
        self.sent = list(sent)

    def second(self):
        g, sent = self.grid, self.sent
        counts = (g.n["x"], g.n["y"])
        at = counts[0] - 1
        del self.sent
        self.more = [
            [g.send(sent[k - 1], "x", k) for k in range(1, counts[0])],
            [g.send(sent[at + k - 1], "y", k) for k in range(1, counts[1])],
        ]

    def fold_z(self):
        g, n = self.grid, self.grid.n
        nz, counts = n["z"], (n["x"], n["y"])
        h, w = self.height, self.width
        specs, arrays, plan = [], [], []
        for i in range(2):
            terms = [self.keep[i]] + self.got[i]
            specs += [
                pl.BlockSpec(
                    (1, 1, h, w), lambda s, p, i=i: (lax.rem(p[0] + s, nz), p[1 + i], 0, 0)
                )
            ] * len(terms)
            specs += [
                pl.BlockSpec((1, h, w), lambda s, p: (lax.rem(p[0] + s, nz), 0, 0))
            ] * len(self.more[i])
            arrays += terms + self.more[i]
            plan.append((len(terms), len(self.more[i])))

        def body(pos, *refs):
            at = 0
            for i, (wide, narrow) in enumerate(plan):
                total = refs[at][0, 0].astype(f32)
                for ref in refs[at + 1 : at + wide]:
                    total = total + ref[0, 0].astype(f32)
                for ref in refs[at + wide : at + wide + narrow]:
                    total = total + ref[0].astype(f32)
                at += wide + narrow
                for k in range(nz):

                    def put(k=k, i=i, total=total):
                        out = refs[len(arrays) + k]
                        out[:, i * w : (i + 1) * w] = total.astype(out.dtype)

                    pl.when(pl.program_id(0) == k)(put)

        sent = pl.pallas_call(
            body,
            grid_spec=pltpu.PrefetchScalarGridSpec(
                num_scalar_prefetch=1,
                grid=(nz,),
                in_specs=specs,
                out_specs=[pl.BlockSpec((h, 2 * w), lambda s, p: (0, 0))] * nz,
            ),
            out_shape=[jax.ShapeDtypeStruct((h, 2 * w), bf16 if k else f32) for k in range(nz)],
            compiler_params=pltpu.CompilerParams(vmem_limit_bytes=56 << 20),
            cost_estimate=FREE,
            name="fold_z",
        )(self.place, *arrays)
        self.sent = list(sent)
        del self.keep, self.got, self.more

    def along_z(self):
        sent = self.sent
        self.kept = [sent[0]] + [self.grid.send(v, "z", k) for k, v in enumerate(sent[1:], 1)]
        del self.sent

    def last(self):
        w = self.width
        shape = jax.ShapeDtypeStruct((self.height // 2, 2 * w), f32)
        rows = sorted({(row, min(r, self.height // 2)) for r, _, row, _ in self.parts})

        def body(pos, *refs):
            own, away = refs[-2], refs[-1]
            total = refs[0][...]
            for ref in refs[1:-2]:
                total = total + ref[...].astype(f32)

            def put(c):
                for row, r in rows:
                    to = slice(row // 2, row // 2 + r)
                    own[to] = total[row + c * r : row + c * r + r]
                    away[to] = total[row + (1 - c) * r : row + (1 - c) * r + r]

            for c in range(2):
                pl.when(pos[3] == c)(functools.partial(put, c))

        self.own, away = pl.pallas_call(
            body,
            in_specs=[pl.BlockSpec(memory_space=pltpu.SMEM)]
            + [pl.BlockSpec(memory_space=pltpu.VMEM)] * len(self.kept),
            out_specs=[pl.BlockSpec(memory_space=pltpu.VMEM)] * 2,
            out_shape=[shape, shape],
            compiler_params=pltpu.CompilerParams(vmem_limit_bytes=56 << 20),
            cost_estimate=FREE,
            name="fold_last",
        )(self.place, *self.kept)
        self.back = self.grid.send(away, "c", 1)
        del self.kept

    def results(self):
        w = self.width

        def body(pos, own, back, *outs):
            def put(c):
                for out, (r, q, row, col) in zip(outs, self.parts):
                    keep = r if row else min(r, self.height // 2)
                    rs = slice(row // 2, row // 2 + keep)
                    for half, ref in ((c, own), (1 - c, back)):
                        for part in range(2):
                            at, from_col = 2 * half * q + part * q, part * w + col
                            out[:keep, at : at + q] = ref[rs, from_col : from_col + q]
                            if keep == r:
                                continue
                            extra, count, wide = tail_of(r, q, keep)
                            for j in range(count):
                                to = at + j * wide
                                out[keep:, to : to + wide] = ref[
                                    j * extra : (j + 1) * extra, from_col + q : from_col + q + wide
                                ]

            for c in range(2):
                pl.when(pos[3] == c)(functools.partial(put, c))

        return pl.pallas_call(
            body,
            in_specs=[pl.BlockSpec(memory_space=pltpu.SMEM)]
            + [pl.BlockSpec(memory_space=pltpu.VMEM)] * 2,
            out_specs=[pl.BlockSpec(memory_space=pltpu.VMEM)] * len(self.parts),
            out_shape=[jax.ShapeDtypeStruct((r, 4 * q), f32) for r, q, _, _ in self.parts],
            compiler_params=pltpu.CompilerParams(vmem_limit_bytes=56 << 20),
            cost_estimate=FREE,
            name="fold_out",
        )(self.place, self.own, self.back)


def neighbours(grid, v):
    def move(u, by):
        pairs = [(i, i + by) for i in range(grid.total) if 0 <= i + by < grid.total]
        return lax.ppermute(u, AXES, pairs)

    left, right = move(v, 1), move(v, -1)
    lefts = move(jnp.concatenate([v, left], 0), 2)
    rights = move(jnp.concatenate([v, right], 0), -2)
    return v, left, right, lefts, rights


def layer_norm(inputs, scale_gain, offset_bias):
    centre = jnp.mean(inputs, axis=-1, keepdims=True)
    centred = inputs - centre
    spread = jnp.mean(centred * centred, axis=-1, keepdims=True)
    return centred * lax.rsqrt(spread + norm_eps) * scale_gain + offset_bias


def dot(a, b, dims=NN):
    return lax.dot_general(a, b, dims, preferred_element_type=f32)

def attend_body(q_ref, k_ref, v_ref, o_ref, lse_ref):
    t = q_ref.shape[0]
    first = lax.broadcasted_iota(jnp.int32, (t, 2 * HEAD), 1) < HEAD
    q, k, v = q_ref[...], k_ref[...], v_ref[...]
    out, totals = [], []
    for side in range(2):
        keep = first if side == 0 else jnp.logical_not(first)
        s = dot(q, jnp.where(keep, k, jnp.zeros_like(k)), NT)
        top = jnp.max(s, axis=-1, keepdims=True)
        p = jnp.exp((s - top) * HEAD ** -0.5)
        total = jnp.sum(p, axis=-1, keepdims=True)
        o = dot((p * (1.0 / total)).astype(bf16), jnp.where(keep, v, jnp.zeros_like(v)))
        out.append(o)
        totals.append(top * HEAD ** -0.5 + jnp.log(total))
    o_ref[...] = (out[0] + out[1]).astype(bf16)
    lse_ref[...] = jnp.where(first, totals[0], totals[1])

def attend(qkv):
    t, width = qkv.shape
    n = width // 3 // (2 * HEAD)
    spec = lambda off: pl.BlockSpec((t, 2 * HEAD), lambda i, off=off: (0, off * n + i))
    return pl.pallas_call(
        attend_body, grid=(n,),
        in_specs=[spec(0), spec(1), spec(2)],
        out_specs=[spec(0), spec(0)],
        out_shape=[jax.ShapeDtypeStruct((t, width // 3), bf16), jax.ShapeDtypeStruct((t, width // 3), f32)],
        compiler_params=pltpu.CompilerParams(vmem_limit_bytes=48 << 20),
        cost_estimate=FREE,
        name="attend",
    )(qkv, qkv, qkv)

def attend_back_body(q_ref, k_ref, v_ref, do_ref, lse_ref, dq_ref, dk_ref, dv_ref):
    t = q_ref.shape[0]
    first = lax.broadcasted_iota(jnp.int32, (t, 2 * HEAD), 1) < HEAD
    q, k, v, do = q_ref[...], k_ref[...], v_ref[...], do_ref[...]
    zero = jnp.zeros_like(k)
    dq = dk = dv = None
    for side in range(2):
        keep = first if side == 0 else jnp.logical_not(first)
        km, vm = jnp.where(keep, k, zero), jnp.where(keep, v, zero)
        qm, dom = jnp.where(keep, q, zero), jnp.where(keep, do, zero)
        lse = lse_ref[:, side * HEAD:side * HEAD + 1]
        p = jnp.exp(dot(q, km, NT) * HEAD ** -0.5 - lse)
        dp = dot(do, vm, NT)
        inner = jnp.sum(p * dp, axis=-1, keepdims=True)
        ds = (p * ((dp - inner) * HEAD ** -0.5)).astype(bf16)
        dq_ = dot(ds, km)
        dv_ = dot(dom, p.astype(bf16), TN)
        dk_ = dot(qm, ds, TN)
        dq = dq_ if dq is None else dq + dq_
        dv = dv_ if dv is None else dv + dv_
        dk = dk_ if dk is None else dk + dk_
    dq_ref[...] = dq.astype(bf16)
    dk_ref[...] = dk.T.astype(bf16)
    dv_ref[...] = dv.T.astype(bf16)

def attend_back(qkv, d_attended, lse):
    t, width = qkv.shape
    n = width // 3 // (2 * HEAD)
    spec = lambda off: pl.BlockSpec((t, 2 * HEAD), lambda i, off=off: (0, off * n + i))
    shape = jax.ShapeDtypeStruct((t, width // 3), bf16)
    return pl.pallas_call(
        attend_back_body, grid=(n,),
        in_specs=[spec(0), spec(1), spec(2), spec(0), spec(0)],
        out_specs=[spec(0)] * 3,
        out_shape=[shape] * 3,
        compiler_params=pltpu.CompilerParams(vmem_limit_bytes=48 << 20),
        cost_estimate=FREE,
        name="attend_back",
    )(qkv, qkv, qkv, d_attended, lse)

def gelu_parts(v):
    e = jnp.exp(-0.5 * v * v)
    t = 1.0 / (1.0 + (0.3275911 * 0.5 ** 0.5) * jnp.abs(v))
    poly = t * (0.127414796 + t * (-0.142248368 + t * (0.7107068705 + t * (-0.7265760135 + t * 0.5307027145))))
    tail = poly * e
    phi = jnp.where(v < 0, tail, 1.0 - tail)
    return v * phi, phi + v * (e * (2.0 * math.pi) ** -0.5)

def flat(ref):
    w = ref[...]
    return w.reshape(-1, w.shape[-1])

def joined_spec(joined, block):
    n, _, rows, d = joined.shape
    per = d // block
    return pl.BlockSpec((n, 1, rows, block), lambda i: (0, 1 + i // per, 0, i % per))

def mlp_in_body(n_ref, w_ref, b_ref, act_ref, slope_ref):
    v = dot(n_ref[...], flat(w_ref)) + b_ref[...]
    act, slope = gelu_parts(v)
    act_ref[...] = act.astype(bf16)
    slope_ref[...] = slope.astype(bf16)

def mlp_in(normed, w, bias, block=512):
    t, d = normed.shape
    ff = bias.shape[-1]
    out = pl.BlockSpec((t, block), lambda i: (0, i))
    shape = jax.ShapeDtypeStruct((t, ff), bf16)
    return pl.pallas_call(
        mlp_in_body, grid=(ff // block,),
        in_specs=[pl.BlockSpec((t, d), lambda i: (0, 0)), joined_spec(w, block), pl.BlockSpec((1, block), lambda i: (0, i))],
        out_specs=[out, out], out_shape=[shape, shape],
        compiler_params=pltpu.CompilerParams(vmem_limit_bytes=48 << 20),
        cost_estimate=FREE,
        name="mlp_in",
    )(normed, w, bias.reshape(1, -1))

def mlp_back_body(dy_ref, slope_ref, w1_ref, w2_ref, dpre_ref, db_ref, dn_ref):
    g = dot(dy_ref[...], w2_ref[...], NT) * slope_ref[...].astype(f32)
    low = g.astype(bf16)
    dpre_ref[...] = low
    db_ref[...] = jnp.sum(low.astype(f32), axis=0, keepdims=True)
    dn = dot(low, flat(w1_ref), NT)
    @pl.when(pl.program_id(0) == 0)
    def _(): dn_ref[...] = dn
    @pl.when(pl.program_id(0) > 0)
    def _(): dn_ref[...] += dn

def mlp_back(dy, slope, w1, w2, block=512):
    t, d = dy.shape
    ff = w2.shape[0]
    whole = pl.BlockSpec((t, d), lambda i: (0, 0))
    part = pl.BlockSpec((t, block), lambda i: (0, i))
    return pl.pallas_call(
        mlp_back_body, grid=(ff // block,),
        in_specs=[whole, part, joined_spec(w1, block), pl.BlockSpec((block, d), lambda i: (i, 0))],
        out_specs=[part, pl.BlockSpec((1, block), lambda i: (0, i)), whole],
        out_shape=[jax.ShapeDtypeStruct((t, ff), bf16), jax.ShapeDtypeStruct((1, ff), f32), jax.ShapeDtypeStruct((t, d), f32)],
        compiler_params=pltpu.CompilerParams(vmem_limit_bytes=48 << 20),
        cost_estimate=FREE,
        name="mlp_back",
    )(dy, slope, w1, w2)

def side_steps(x, side):
    n = x.shape[0]
    b = lax.rem(lax.broadcasted_iota(jnp.int32, x.shape, 0), side)
    before = jnp.where(b == 0, 0.0, pltpu.roll(x, 1, 0))
    after = jnp.where(b == side - 1, 0.0, pltpu.roll(x, n - 1, 0))
    return before, after

def up(x, by):
    return jnp.concatenate([jnp.zeros((by, x.shape[1]), x.dtype), x[:-by]], 0)

def down(x, by):
    return jnp.concatenate([x[by:], jnp.zeros((by, x.shape[1]), x.dtype)], 0)

def adapter_body(n_pieces, side, pos_ref, *refs):
    pieces, (w_ref, table_ref, dy_ref, proj_ref, spat_ref, rows_ref, dg_ref, dys_ref) = refs[:n_pieces], refs[n_pieces:]
    x = table_ref[BIAS_PROJ : BIAS_PROJ + 1]
    for k in range(n_pieces):
        x = x + dot(pieces[k][...], w_ref[lax.rem(pos_ref[0] - k + n_pieces, n_pieces)])
    proj_ref[...] = x
    before, after = side_steps(x, side)
    w = table_ref[DEPTH : DEPTH + 9]
    y = [before * w[3 * s:3 * s + 1] + x * w[3 * s + 1:3 * s + 2] + after * w[3 * s + 2:3 * s + 3] for s in range(3)]
    spatial = up(y[0], side) + y[1] + down(y[2], side) + table_ref[BIAS_DEPTH : BIAS_DEPTH + 1]
    spat_ref[...] = spatial
    rows_ref[...] = jnp.sum(spatial, axis=0, keepdims=True)
    dy = dy_ref[...].astype(f32)
    dg_ref[...] = jnp.sum(dy * spatial, axis=0, keepdims=True)
    dys_ref[...] = jnp.sum(dy, axis=0, keepdims=True)

def adapter(pos, pieces, w_proj, table, dy, side=PS, block=256):
    t, d = dy.shape
    n, width = len(pieces), pieces[0].shape[1]
    whole = pl.BlockSpec((t, width), lambda i: (0, 0))
    part = pl.BlockSpec((t, block), lambda i: (0, i))
    row = pl.BlockSpec((1, block), lambda i: (0, i))
    big, line = jax.ShapeDtypeStruct((t, d), f32), jax.ShapeDtypeStruct((1, d), f32)
    return pl.pallas_call(
        functools.partial(adapter_body, n, side), grid=(d // block,),
        in_specs=[pl.BlockSpec(memory_space=pltpu.SMEM)] + [whole] * n + [pl.BlockSpec((n, width, block), lambda i: (0, 0, i)), pl.BlockSpec((table.shape[0], block), lambda i: (0, i)), part],
        out_specs=[part, part, row, row, row], out_shape=[big, big, line, line, line],
        compiler_params=pltpu.CompilerParams(vmem_limit_bytes=48 << 20),
        cost_estimate=FREE,
        name="adapter",
    )(pos.reshape(1).astype(jnp.int32), *pieces, w_proj.reshape(n, width, d), table, dy)

def adapter_back_body(side, dy_ref, proj_ref, gate_ref, dr_ref, table_ref, dp_ref, dwd_ref, dbd_ref, dbp_ref):
    ds = dy_ref[...].astype(f32) * gate_ref[...] + dr_ref[...]
    dbd_ref[...] = jnp.sum(ds, axis=0, keepdims=True)
    before, after = side_steps(ds, side)
    w = table_ref[DEPTH : DEPTH + 9]
    y = [after * w[3 * s:3 * s + 1] + ds * w[3 * s + 1:3 * s + 2] + before * w[3 * s + 2:3 * s + 3] for s in range(3)]
    low = (down(y[0], side) + y[1] + up(y[2], side)).astype(bf16)
    dp_ref[...] = low
    dbp_ref[...] = jnp.sum(low.astype(f32), axis=0, keepdims=True)
    x = proj_ref[...]
    x_before, x_after = side_steps(x, side)
    for t, c in enumerate((x_before, x, x_after)):
        dwd_ref[t:t + 1] = jnp.sum(ds[side:] * c[:-side], axis=0, keepdims=True)
        dwd_ref[3 + t:4 + t] = jnp.sum(ds * c, axis=0, keepdims=True)
        dwd_ref[6 + t:7 + t] = jnp.sum(ds[:-side] * c[side:], axis=0, keepdims=True)

def adapter_back(dy, projected, gate, d_rows, table, side=PS, block=256):
    t, d = dy.shape
    part = pl.BlockSpec((t, block), lambda i: (0, i))
    row = pl.BlockSpec((1, block), lambda i: (0, i))
    nine = pl.BlockSpec((9, block), lambda i: (0, i))
    line = jax.ShapeDtypeStruct((1, d), f32)
    return pl.pallas_call(
        functools.partial(adapter_back_body, side), grid=(d // block,),
        in_specs=[part, part, row, row, pl.BlockSpec((table.shape[0], block), lambda i: (0, i))], out_specs=[part, nine, row, row],
        out_shape=[jax.ShapeDtypeStruct((t, d), bf16), jax.ShapeDtypeStruct((9, d), f32), line, line],
        compiler_params=pltpu.CompilerParams(vmem_limit_bytes=48 << 20),
        cost_estimate=FREE,
        name="adapter_back",
    )(dy, projected, gate, d_rows, table)


def rows_call(body, name, t, steps, ins, outs, sums):
    b = t // steps

    def spec(shape, by_rows):
        if by_rows:
            return pl.BlockSpec((b, shape[1]), lambda i: (i, 0))
        if len(shape) == 4:
            return pl.BlockSpec((shape[0], 1) + shape[2:], lambda i: (0, 0, 0, 0))
        return pl.BlockSpec(shape, lambda i: (0, 0))

    out_specs = [pl.BlockSpec((b, w), lambda i: (i, 0)) for w, _ in outs]
    shapes = [jax.ShapeDtypeStruct((t, w), dt) for w, dt in outs]
    if sums:
        out_specs.append(pl.BlockSpec(sums, lambda i: (0, 0)))
        shapes.append(jax.ShapeDtypeStruct(sums, f32))
    return pl.pallas_call(
        body,
        grid=(steps,),
        in_specs=[spec(a.shape, by_rows) for a, by_rows in ins],
        out_specs=out_specs,
        out_shape=shapes,
        compiler_params=pltpu.CompilerParams(vmem_limit_bytes=48 << 20),
        cost_estimate=FREE,
        name=name,
    )(*[a for a, _ in ins])


def add_sums(ref, values):
    total = jnp.concatenate([jnp.sum(v, axis=0, keepdims=True) for v in values], 0)

    @pl.when(pl.program_id(0) == 0)
    def _():
        ref[...] = total

    @pl.when(pl.program_id(0) > 0)
    def _():
        ref[...] += total


def norm_parts(x):
    centred = x - jnp.mean(x, axis=-1, keepdims=True)
    rstd = lax.rsqrt(jnp.mean(centred * centred, axis=-1, keepdims=True) + norm_eps)
    return centred * rstd, rstd


def norm_back(d_normed, x, gain):
    xhat, rstd = norm_parts(x)
    u = d_normed * gain
    shift = jnp.mean(u, axis=-1, keepdims=True)
    slope = jnp.mean(u * xhat, axis=-1, keepdims=True)
    return (u - shift - xhat * slope) * rstd, d_normed * xhat


def attn_out_norm(attended, w, x, table):
    def body(a_ref, w_ref, x_ref, t_ref, first_ref, n_ref):
        first = x_ref[...].astype(f32) + dot(a_ref[...], flat(w_ref)) + t_ref[BIAS_OUT : BIAS_OUT + 1]
        first_ref[...] = first
        xhat, _ = norm_parts(first)
        n_ref[...] = (
            xhat * t_ref[LN2_GAIN : LN2_GAIN + 1] + t_ref[LN2_BIAS : LN2_BIAS + 1]
        ).astype(bf16)

    t, d = x.shape
    ins = [(attended, True), (w, False), (x, True), (table, False)]
    return rows_call(body, "attn_out", t, 4, ins, [(d, f32), (d, bf16)], None)


def norm_two_back(d_normed2, first_sum, dy, table, w):
    def body(dn_ref, x_ref, dy_ref, t_ref, w_ref, first_ref, branch_ref, att_ref, sum_ref):
        dn = dn_ref[...]
        dx, scaled = norm_back(dn, x_ref[...], t_ref[LN2_GAIN : LN2_GAIN + 1])
        first = dy_ref[...].astype(f32) + dx
        low = first.astype(bf16)
        first_ref[...] = first
        branch_ref[...] = low
        att_ref[...] = dot(low, flat(w_ref), NT).astype(bf16)
        add_sums(sum_ref, (scaled, dn, low.astype(f32)))

    t, d = dy.shape
    ins = [(d_normed2, True), (first_sum, True), (dy, True), (table, False), (w, False)]
    return rows_call(body, "norm_two", t, 4, ins, [(d, f32), (d, bf16), (d, bf16)], (3, d))


def norm_one_back(parts, w, x, d_first, table):
    def body(q_ref, k_ref, v_ref, w_ref, x_ref, first_ref, t_ref, out_ref, sum_ref):
        d = x_ref.shape[1]
        q, k, v = q_ref[...], k_ref[...], v_ref[...]
        dn = dot(q, w_ref[:, :d], NT) + dot(k, w_ref[:, d : 2 * d], NT) + dot(v, w_ref[:, 2 * d :], NT)
        dx, scaled = norm_back(dn, x_ref[...].astype(f32), t_ref[LN1_GAIN : LN1_GAIN + 1])
        out_ref[...] = (first_ref[...] + dx).astype(bf16)
        add_sums(sum_ref, (scaled, dn, q.astype(f32), v.astype(f32)))

    t, d = x.shape
    ins = [(p, True) for p in parts] + [(w, False), (x, True), (d_first, True), (table, False)]
    return rows_call(body, "norm_one", t, 4, ins, [(d, bf16)], (4, d))


def columns_call(body, name, block, ins, width, dtype):
    t = ins[0][0].shape[0]

    def spec(shape, by_columns):
        if by_columns:
            return pl.BlockSpec((shape[0], block), lambda i: (0, i))
        return pl.BlockSpec(shape, lambda i: (0, 0))

    return pl.pallas_call(
        body,
        grid=(width // block,),
        in_specs=[spec(a.shape, by) for a, by in ins],
        out_specs=pl.BlockSpec((t, block), lambda i: (0, i)),
        out_shape=jax.ShapeDtypeStruct((t, width), dtype),
        compiler_params=pltpu.CompilerParams(vmem_limit_bytes=48 << 20),
        cost_estimate=FREE,
        name=name,
    )(*[a for a, _ in ins])


def project(normed, w, bias):
    def body(n_ref, w_ref, b_ref, out_ref):
        out_ref[...] = (dot(n_ref[...], w_ref[...]) + b_ref[...]).astype(bf16)

    ins = [(normed, False), (w, True), (bias, True)]
    return columns_call(body, "project", 512, ins, w.shape[1], bf16)


def layer_output(activation, w, first_sum, table, gate, spatial):
    def body(a_ref, w_ref, x_ref, t_ref, g_ref, s_ref, out_ref):
        total = x_ref[...] + dot(a_ref[...], w_ref[...]) + t_ref[BIAS_FC2 : BIAS_FC2 + 1]
        out_ref[...] = (total + g_ref[...] * s_ref[...]).astype(bf16)

    ins = [(activation, False), (w, True), (first_sum, True), (table, True), (gate, True), (spatial, True)]
    return columns_call(body, "layer_output", 256, ins, w.shape[1], bf16)


def dot3(x, w, dims=NN):
    a = x.astype(bf16)
    rest = x - a.astype(f32)
    b = rest.astype(bf16)
    c = (rest - b.astype(f32)).astype(bf16)
    return dot(a, w, dims) + dot(b, w, dims) + dot(c, w, dims)


def gate_body(n_near, tokens, d, *refs):
    near_refs, refs = refs[:n_near], refs[n_near:]
    win_ref, wout_ref, gate_ref, drows_ref, pack_ref, sum_ref = refs
    near = [ref[i : i + 1] for ref in near_refs for i in range(ref.shape[0])]
    n_near = len(near)
    own = near[0][:, 2 * d :]
    match = [(near[i][:, 2 * d :] == own).astype(f32) for i in range(n_near)]
    count = functools.reduce(lambda a, b: a + b, match)[:, :1] * tokens
    rows = d_gates = None
    for i in range(n_near):
        weight = match[i][:, :1]
        row, d_gate = weight * near[i][:, :d], weight * near[i][:, d : 2 * d]
        rows = row if i == 0 else rows + row
        d_gates = d_gate if i == 0 else d_gates + d_gate
    second = lax.broadcasted_iota(jnp.int32, (8, d), 0) == 1
    mean = jnp.broadcast_to(rows / count, (8, d))
    d_gate = jnp.where(second, jnp.broadcast_to(d_gates, (8, d)), jnp.broadcast_to(near[0][:, d : 2 * d], (8, d)))
    win, wout = win_ref[...], wout_ref[...]
    act, slope = gelu_parts(dot3(mean, win))
    gate = jnp.tanh(dot3(act, wout, NT))
    d_pre = d_gate * (1.0 - gate * gate)
    d_hidden = dot3(d_pre, wout) * slope
    d_mean = dot3(d_hidden, win, NT)
    gate_ref[...] = gate[:1]
    drows_ref[...] = d_mean[1:2] / count
    sum_ref[...] = jnp.zeros((1, 128), f32) + jnp.sum(gate[:1])
    at = 0
    for v, order in ((mean, (0, 0, 1)), (d_pre, (0, 0, 1)), (d_hidden, (0, 1, 0)), (act, (0, 1, 0))):
        line = jnp.broadcast_to(v[:1], v.shape)
        high = line.astype(bf16)
        low = (line - high.astype(f32)).astype(bf16)
        place = lax.broadcasted_iota(jnp.int32, v.shape, 0)
        kind = jnp.where(place == 1, order[1], jnp.where(place == 2, order[2], 0))
        pick = jnp.where(kind == 1, low.astype(f32), high.astype(f32))
        pack_ref[:, at : at + v.shape[1]] = jnp.where(place < 3, pick, 0.0).astype(bf16)
        at += v.shape[1]


def gate_step(near, gates, d, hidden, tokens):
    n = len(near)

    def line(k):
        return jax.ShapeDtypeStruct((1, k), f32)

    def at(k):
        return pl.BlockSpec((1, k), lambda j: (0, 0))

    k = 2 * d + 2 * hidden
    return pl.pallas_call(
        functools.partial(gate_body, n, tokens, d),
        grid=(1,),
        in_specs=[pl.BlockSpec(v.shape, lambda j: (0, 0)) for v in near]
        + [pl.BlockSpec((d, hidden), lambda j, b=b: (0, b)) for b in range(2)],
        out_specs=[at(d), at(d), pl.BlockSpec((8, k), lambda j: (0, 0)), at(128)],
        out_shape=[line(d), line(d), jax.ShapeDtypeStruct((8, k), bf16), line(128)],
        compiler_params=pltpu.CompilerParams(vmem_limit_bytes=32 << 20),
        cost_estimate=FREE,
        name="gate",
    )(*near, gates, gates)


def pool_table(coarse_side, fine_side):
    coarse, fine = np.arange(coarse_side)[:, None], np.arange(fine_side)[None]
    start = coarse * fine_side // coarse_side
    end = ((coarse + 1) * fine_side + coarse_side - 1) // coarse_side
    single = np.where((fine >= start) & (fine < end), 1.0, 0.0) / (end - start)
    return np.kron(single, single)


def token_sum(values):
    return jnp.sum(values.astype(f32), axis=0)


def shards(
    tokens,
    features,
    sample_of,
    cotangent,
    ln1_gain,
    ln1_bias,
    w_qkv,
    bias_qv,
    w_attn_out,
    bias_attn_out,
    ln2_gain,
    ln2_bias,
    w_fc1,
    bias_fc1,
    w_fc2,
    bias_fc2,
    w_proj,
    bias_proj,
    w_depth,
    bias_depth,
    w_gate_in,
    w_gate_out,
):
    grid = Grid()
    rows = ln1_gain.shape[0]
    total = grid.total
    x, dy = tokens[0], cotangent[0]
    count, d = x.shape
    hidden = w_gate_in.shape[1]

    vectors = [ln1_gain, ln1_bias, bias_attn_out, ln2_gain, ln2_bias, bias_fc2, bias_proj, bias_depth]
    a_small = GatherSmall(
        grid, jnp.concatenate(vectors + [w_depth.reshape(-1), bias_qv, bias_fc1])
    )
    gate_out_rows = dot(jnp.eye(rows, dtype=bf16), w_gate_out, NT).astype(bf16)
    gates = jnp.concatenate([w_gate_in, gate_out_rows], 1)
    gate_out_rows = dot(jnp.eye(rows, dtype=bf16), w_gate_out, NT).astype(bf16)
    gates = jnp.concatenate([w_gate_in, gate_out_rows], 1)
    full_qkv = lax.all_gather(w_qkv, AXES, axis=0, tiled=True)
    joined = lax.all_gather(
        jnp.concatenate([w_attn_out] + [w_fc1[:, i : i + d] for i in range(0, w_fc1.shape[1], d)], 0),
        AXES,
    )
    joined = joined.reshape(total, -1, rows, d)
    if rows % 16:
        joined = joined.transpose(1, 0, 2, 3).reshape(1, -1, d, d)
    mixed_shard = jnp.concatenate([gates, w_proj], 0)
    a_qkv, a_fc2 = Gather(grid, (w_qkv,)), Gather(grid, (w_fc2,))

    n_ch = lax.axis_size("ch")
    ch = lax.axis_index("ch")
    n_img, own_ch = features.shape[0], features.shape[1]
    core = grid.pos["c"]

    def along_ch(v, by):
        img = lax.axis_size("img")
        pairs = [
            (i * n_ch + j, i * n_ch + (j + by) % n_ch) for i in range(img) for j in range(n_ch)
        ]
        return lax.ppermute(v, AXES, pairs)

    def peer(v):
        return grid.send(v, "c", 1)

    def peer_half(v):
        h = v.shape[1] // 2
        return grid.send(lax.dynamic_slice(v, (0, (1 - core) * h), (v.shape[0], h)), "c", 1)

    def step(active, *values):
        states, values = lax.optimization_barrier(([a.state() for a in active], values))
        for a, state in zip(active, states):
            a.set_state(state)
        return values

    a_qkv.along_z()
    for _ in range(3):
        a_small.next()
    pool = jnp.asarray(pool_table(PS, FS), bf16)
    pooled_own = dot(pool, features.reshape(n_img * own_ch, -1), NT).astype(bf16)
    a_qkv.pack_first()
    a_small.v, pooled_own = step((a_qkv,), a_small.v, pooled_own)

    a_qkv.first()
    a_qkv.pack_second()
    while a_small.next():
        pass
    every, pooled_own = step((a_qkv, a_fc2), a_small.v, pooled_own)

    a_qkv.second()
    a_fc2.along_z()
    a_fc2.pack_first()
    every = every.astype(f32)
    table = every[:, : LINES * rows].reshape(total, LINES, rows)
    table = table.transpose(1, 0, 2).reshape(LINES, d)
    at = LINES * rows
    full_bias_qv = every[:, at : at + 2 * rows].reshape(-1)
    full_bias_fc1 = every[:, at + 2 * rows :].reshape(1, -1)
    bias_qkv = jnp.concatenate([full_bias_qv[:d], jnp.zeros((d,), f32), full_bias_qv[d:]])[None]
    x32 = x.astype(f32)
    normed1 = layer_norm(x32, table[LN1_GAIN], table[LN1_BIAS]).astype(bf16)
    cuts = []
    for k in range(n_ch):
        to = lax.rem(ch + k, n_ch)
        cuts.append(lax.dynamic_slice(pooled_own, (0, to * own_ch), (count, own_ch)))
    normed1, table, full_bias_fc1, bias_qkv, cuts = step(
        (a_qkv, a_fc2), normed1, table, full_bias_fc1, bias_qkv, cuts
    )

    a_qkv.early()
    a_qkv.cross()
    dy_far = peer_half(dy)
    normed1, cuts, dy_far = step((a_qkv, a_fc2), normed1, cuts, dy_far)

    def pooled_piece(k):
        return along_ch(cuts[k], k) if k else cuts[k]

    a_fc2.first()
    early = n_ch // 2 + 1
    pieces = [pooled_piece(k) for k in range(early)]
    (full_qkv,) = a_qkv.whole()
    qkv = project(normed1, full_qkv, bias_qkv)
    attended, log_total = attend(qkv)
    a_fc2.s0, a_fc2.r1, attended = lax.optimization_barrier((a_fc2.s0, a_fc2.r1, attended))
    a_fc2.pack_second()
    attended, log_total, pieces, cuts, full_qkv, mixed_shard = step(
        (a_fc2,), attended, log_total, pieces, cuts, full_qkv, mixed_shard
    )

    mixed_w = lax.all_gather(mixed_shard, AXES)
    a_fc2.second()
    attended_far = peer(attended)
    first_sum, normed2 = attn_out_norm(attended, joined, x, table)
    activation, slope = mlp_in(normed2, joined, full_bias_fc1)
    activation, slope, normed2, first_sum, cuts, attended_far = step(
        (a_fc2,), activation, slope, normed2, first_sum, cuts, attended_far
    )

    activation_far, normed2_far = peer(activation), peer(normed2)
    pieces = pieces + [pooled_piece(k) for k in range(early, n_ch)]
    a_fc2.early()
    a_fc2.cross()
    pooled = jnp.zeros((count, n_ch * own_ch), bf16)
    for k in range(n_ch):
        from_ch = lax.rem(ch - k + n_ch, n_ch)
        pooled = lax.dynamic_update_slice(pooled, pieces[k], (0, from_ch * own_ch))
    activation_far, normed2_far, slope, attended, pieces, pooled = step(
        (a_fc2,), activation_far, normed2_far, slope, attended, pieces, pooled
    )

    (full_fc2,) = a_fc2.whole()
    ff = activation.shape[1]
    s_one = Scatter(
        grid,
        [(activation, activation_far, dy, dy_far, 0, None, 0, ff, d // 2, 0, 0)],
        2 * ff // total,
        d // 4,
    )
    slope, attended, pieces, full_fc2 = step((s_one,), slope, attended, pieces, full_fc2)

    s_one.first()
    d_pre, d_bias_fc1, d_normed2 = mlp_back(dy, slope, joined, full_fc2)
    d_first, d_branch, d_attended, sums_two = norm_two_back(
        d_normed2, first_sum, dy, table, joined
    )
    s_one.got, d_attended = lax.optimization_barrier((s_one.got, d_attended))
    s_one.fold_second()
    d_attended, d_first, d_branch, d_pre, full_fc2, attended, pieces = step(
        (s_one,), d_attended, d_first, d_branch, d_pre, full_fc2, attended, pieces
    )

    s_one.second()
    d_pre_far, d_branch_far = peer_half(d_pre), peer_half(d_branch)
    full_gates = mixed_w[:, :rows].reshape(d, 2 * hidden)
    full_proj = mixed_w[:, rows:].reshape(-1, d)
    projected, spatial, row_sums, d_gate, dy_sum = adapter(ch, pieces, full_proj, table, dy)
    ids_plus = sample_of.astype(f32) + 1.0
    carried = jnp.concatenate(
        [row_sums, d_gate, jnp.broadcast_to(ids_plus[:, None], (1, 128))], 1
    )
    s_one.more, carried = lax.optimization_barrier((s_one.more, carried))
    s_one.fold_z()
    d_attended, d_branch, d_pre, d_pre_far, d_branch_far, carried, full_gates, full_proj = step(
        (s_one,), d_attended, d_branch, d_pre, d_pre_far, d_branch_far, carried, full_gates, full_proj
    )

    near = neighbours(grid, carried)
    s_two = Scatter(
        grid,
        [
            (normed2, normed2_far, d_pre, d_pre_far, 0, None, 0, d, ff // 2, 0, 0),
            (attended, attended_far, d_branch, d_branch_far, 0, None, 0, d, d // 2, 0, ff // 4),
        ],
        2 * rows,
        (ff + d) // 4,
    )
    d_attended, normed1, near = step((s_one, s_two), d_attended, normed1, near)

    s_two.first()
    s_one.along_z()
    d_query, d_key, d_value = attend_back(qkv, d_attended, log_total)
    gate, d_rows, pack, gate_sum = gate_step(near, full_gates, d, hidden, count)
    d_projected, d_depth, d_bias_depth, d_bias_proj = adapter_back(
        dy, projected, gate, d_rows, table
    )
    s_two.got, d_query, d_projected = lax.optimization_barrier((s_two.got, d_query, d_projected))
    s_two.fold_second()
    d_query, d_key, d_value, normed1, pack, d_projected, gate, pooled = step(
        (s_one, s_two), d_query, d_key, d_value, normed1, pack, d_projected, gate, pooled
    )

    d_mixed = jnp.concatenate([d_query, d_key, d_value], -1)
    d_mixed_far, normed1_far, pooled_far = peer_half(d_mixed), peer(normed1), peer(pooled)
    pack_far, d_projected_far = peer(pack), peer_half(d_projected)
    d_pooled = dot(d_projected, full_proj, NT).astype(bf16)
    d_mixed, d_mixed_far, normed1_far, pooled_far, pack_far, d_projected_far, d_pooled = step(
        (s_two,),
        d_mixed,
        d_mixed_far,
        normed1_far,
        pooled_far,
        pack_far,
        d_projected_far,
        d_pooled,
    )

    s_two.second()
    lines = jnp.concatenate([sums_two[2:], sums_two[:2], dy_sum, d_bias_proj, d_bias_depth, d_depth], 0)
    lines = lines.reshape(LINES - 2, total, rows).transpose(1, 0, 2).reshape(total, -1)
    small = jnp.concatenate(
        [lines, d_bias_fc1.reshape(total, -1), jnp.broadcast_to(gate_sum, (total, 128))], 1
    )
    back = []
    for k in range(n_ch):
        to = lax.rem(ch + k, n_ch)
        piece = lax.dynamic_slice(d_pooled, (0, to * own_ch), (count, own_ch))
        back.append(along_ch(piece, k) if k else piece)
    wide, low = 3 * d // 4, hidden // 4
    half = d // (hidden // 2)
    s_three = Scatter(
        grid,
        [
            (normed1, normed1_far, d_mixed, d_mixed_far, 0, None, 0, d, 3 * d // 2, 0, 0),
            (pack, pack_far, pack, pack_far, 2 * half, 2 * half, 0, d, hidden // 2, 0, wide),
            (
                pack,
                pack_far,
                pack,
                pack_far,
                2 * half + 2,
                2 * half + 2,
                grid.n["z"],
                d,
                hidden // 2,
                0,
                wide + low,
            ),
            (
                pooled,
                pooled_far,
                d_projected,
                d_projected_far,
                0,
                None,
                0,
                pooled.shape[1],
                d // 2,
                0,
                wide + 2 * low,
            ),
        ],
        2 * rows,
        wide + 2 * low + pooled.shape[1] // 4,
    )
    s_two.more, s_three.away = lax.optimization_barrier((s_two.more, s_three.away))
    s_two.fold_z()
    d_query, d_key, d_value, activation, back, small = step(
        (s_one, s_two, s_three), d_query, d_key, d_value, activation, back, small
    )

    s_three.first()
    s_two.along_z()
    grad_tokens, sums_one = norm_one_back(
        (d_query, d_key, d_value), full_qkv, x, d_first, table
    )
    layer_out = layer_output(activation, full_fc2, first_sum, table, gate, spatial)
    s_three.got, layer_out, grad_tokens = lax.optimization_barrier(
        (s_three.got, layer_out, grad_tokens)
    )
    s_three.fold_second()
    layer_out, grad_tokens, sums_one, small, back = step(
        (s_one, s_two, s_three), layer_out, grad_tokens, sums_one, small, back
    )

    s_three.second()
    ones = sums_one[:2].reshape(2, total, rows).transpose(1, 0, 2).reshape(total, -1)
    d_bias_qv = sums_one[2:].reshape(total, -1)
    s_small = ScatterSmall(grid, jnp.concatenate([ones, small, d_bias_qv], 1))
    s_one.last()
    s_two.last()
    s_small.next()
    s_small.next()
    s_three.fold_z()
    s_small.v, back = step((s_one, s_two, s_three), s_small.v, back)

    s_three.along_z()
    while s_small.left:
        s_small.next()
    (g_fc2,) = s_one.results()
    g_fc1, g_attn_out = s_two.results()
    s_small.v, back, g_fc2, g_fc1 = step((s_three,), s_small.v, back, g_fc2, g_fc1)

    d_local = jnp.zeros((n_img, count, own_ch), bf16)
    for k in range(n_ch):
        from_ch = lax.rem(ch - k + n_ch, n_ch)
        d_local = lax.dynamic_update_slice(d_local, back[k][None], (from_ch, 0, 0))
    grad_features = jnp.einsum("kpc,pf->kcf", d_local, pool, preferred_element_type=f32).astype(bf16)
    s_three.last()
    summed = s_small.v[0]
    gate_mean = summed[-2 * rows - 1] / (total * d)
    g_qkv, g_gate_in, g_gate_out, g_proj = s_three.results()

    def owned(i):
        return summed[i * rows : (i + 1) * rows]

    return (
        layer_out[None],
        grad_tokens[None],
        grad_features,
        owned(LN1_GAIN),
        owned(LN1_BIAS),
        g_qkv,
        summed[-2 * rows :],
        g_attn_out,
        owned(BIAS_OUT),
        owned(LN2_GAIN),
        owned(LN2_BIAS),
        g_fc1,
        summed[at : at + 4 * rows],
        g_fc2,
        owned(BIAS_FC2),
        g_proj,
        owned(BIAS_PROJ),
        summed[DEPTH * rows : at].reshape(9, rows),
        owned(BIAS_DEPTH),
        g_gate_in,
        g_gate_out.T,
        gate_mean,
    )


def solution(mesh):
    return jax.shard_map(
        shards,
        mesh=mesh,
        in_specs=(
            P(("img", "ch"), None, None),
            P("img", "ch", None),
            P(("img", "ch")),
            P(("img", "ch"), None, None),
            P(("img", "ch")),
            P(("img", "ch")),
            P(("img", "ch"), None),
            P(("img", "ch")),
            P(("img", "ch"), None),
            P(("img", "ch")),
            P(("img", "ch")),
            P(("img", "ch")),
            P(("img", "ch"), None),
            P(("img", "ch")),
            P(("img", "ch"), None),
            P(("img", "ch")),
            P(("img", "ch"), None),
            P(("img", "ch")),
            P(None, ("img", "ch")),
            P(("img", "ch")),
            P(("img", "ch"), None),
            P(None, ("img", "ch")),
        ),
        out_specs=(
            P(("img", "ch"), None, None),
            P(("img", "ch"), None, None),
            P("img", "ch", None),
            P(("img", "ch")),
            P(("img", "ch")),
            P(("img", "ch"), None),
            P(("img", "ch")),
            P(("img", "ch"), None),
            P(("img", "ch")),
            P(("img", "ch")),
            P(("img", "ch")),
            P(("img", "ch"), None),
            P(("img", "ch")),
            P(("img", "ch"), None),
            P(("img", "ch")),
            P(("img", "ch"), None),
            P(("img", "ch")),
            P(None, ("img", "ch")),
            P(("img", "ch")),
            P(("img", "ch"), None),
            P(None, ("img", "ch")),
            P(),
        ),
        check_vma=False,
    )
```

```python
import functools
import math

import jax
import numpy as np
import jax.numpy as jnp
from jax import lax
from jax.experimental import pallas as pl
from jax.experimental.pallas import tpu as pltpu
from jax.sharding import PartitionSpec as P

HEAD = 64
PS = 24
FS = 32
REACH = 3
LN1_GAIN, LN1_BIAS, BIAS_OUT, LN2_GAIN, LN2_BIAS, BIAS_FC2, BIAS_PROJ, BIAS_DEPTH, DEPTH = range(9)
LINES = DEPTH + 9

norm_eps = 1e-05
highest = lax.Precision.HIGHEST
f32, bf16 = jnp.float32, jnp.bfloat16
AXES = ("img", "ch")
FREE = pl.CostEstimate(flops=0, bytes_accessed=0, transcendentals=0)
NN = (((1,), (0,)), ((), ()))
NT = (((1,), (1,)), ((), ()))
TN = (((0,), (0,)), ((), ()))


class Grid:
    def __init__(self):
        img, ch = lax.axis_size("img"), lax.axis_size("ch")
        depth = 4 if img % 4 == 0 else 1
        self.n = {"z": depth, "x": img // depth, "y": ch // 2, "c": 2}
        self.stride = {"c": 1, "y": 2, "x": ch, "z": ch * (img // depth)}
        self.total = img * ch
        me = lax.axis_index(AXES)
        self.me = me
        self.pos = {a: lax.rem(lax.div(me, self.stride[a]), self.n[a]) for a in self.n}

    def send(self, v, axis, by):
        n, s = self.n[axis], self.stride[axis]
        pairs = []
        for i in range(self.total):
            a = (i // s) % n
            pairs.append((i, i + ((a + by) % n - a) * s))
        return lax.ppermute(v, AXES, pairs)

    def other(self, axis, by):
        return lax.rem(self.pos[axis] + by, self.n[axis])

    def swap(self, v, bit):
        return lax.ppermute(v, AXES, [(i, i ^ bit) for i in range(self.total)])


class GatherSmall:
    def __init__(self, grid, v):
        self.grid, self.v, self.bit = grid, v[None], 1

    def next(self):
        got = self.grid.swap(self.v, self.bit)
        pair = (self.v, got)
        upper = jnp.bitwise_and(self.grid.me, self.bit) != 0
        self.v = jnp.where(upper, jnp.concatenate(pair[::-1], 0), jnp.concatenate(pair, 0))
        self.bit *= 2
        return self.bit < self.grid.total


class ScatterSmall:
    def __init__(self, grid, v):
        self.grid, self.v = grid, v
        bits = [1 << i for i in range(grid.total.bit_length() - 1)]
        stride = grid.stride["z"]
        self.left = [b for b in bits if b >= stride][::-1] + [b for b in bits if b < stride][::-1]
        self.shape = {b: 2 for b in bits}

    def next(self):
        bit = self.left.pop(0)
        del self.shape[bit]
        low = 2 ** sum(b < bit for b in self.shape)
        t = self.v.reshape(-1, 2, low, self.v.shape[1])
        upper = (jnp.bitwise_and(self.grid.me, bit) != 0).astype(jnp.int32)
        mine = lax.dynamic_index_in_dim(t, upper, 1, keepdims=False)
        away = lax.dynamic_index_in_dim(t, 1 - upper, 1, keepdims=False)
        mine, away = (u.reshape(-1, t.shape[3]) for u in (mine, away))
        self.v = mine + self.grid.swap(away, bit)


def after(value, done):
    return lax.optimization_barrier((value, done))[0]


class Gather:
    def __init__(self, grid, params):
        self.grid = grid
        self.width = width = min(p.shape[1] for p in params)
        self.q = width // 2
        self.places, blocks, at = [], [], 0
        for i, p in enumerate(params):
            r = p.shape[0]
            held = -(-r // 16) * 16
            for j in range(p.shape[1] // width):
                block = p[:, j * width : (j + 1) * width]
                blocks.append(jnp.pad(block, ((0, held - r), (0, 0))) if held > r else block)
                self.places.append((i, at, r if r % 8 == 0 else held, j * width))
                at += held
        self.shapes = [p.shape for p in params]
        self.shard = jnp.concatenate(blocks, 0)

    def along_z(self):
        g = self.grid
        self.z = [self.shard] + [g.send(self.shard, "z", k) for k in range(1, g.n["z"])]

    def pack_first(self):
        self.s0 = [
            jnp.stack([p[:, i * self.q : (i + 1) * self.q] for p in self.z]) for i in range(2)
        ]
        del self.z

    def first(self):
        self.r1 = [self.every(self.s0[i], "xy"[i]) for i in range(2)]

    def pack_second(self):
        self.s1 = [jnp.concatenate([self.s0[i]] + self.r1[i], 0) for i in range(2)]
        del self.s0, self.r1

    def second(self):
        self.r2 = [self.every(self.s1[i], "yx"[i]) for i in range(2)]

    def early(self):
        self.c1 = [self.over(s) for s in self.s1]

    def cross(self):
        self.c2 = [[self.over(b) for b in r] for r in self.r2]

    def every(self, v, axis):
        return [self.grid.send(v, axis, k) for k in range(1, self.grid.n[axis])]

    def over(self, v):
        return self.grid.send(v, "c", 1)


    def state(self):
        names = ("shard", "z", "s0", "s1", "r1", "r2", "c1", "c2")
        return {k: v for k, v in vars(self).items() if k in names}

    def set_state(self, state):
        for k, v in state.items():
            setattr(self, k, v)

    def whole(self):
        n, q, place_of = self.grid.n, self.q, self.places
        nz, nx, ny = n["z"], n["x"], n["y"]
        arrays, plan = [], []
        for core_rel, (s1, r2) in enumerate(((self.s1, self.r2), (self.c1, self.c2))):
            for part, (first, second) in enumerate((("x", "y"), ("y", "x"))):
                for k2, buf in enumerate([s1[part]] + r2[part]):
                    for k1 in range(n[first]):
                        for kz in range(nz):
                            rel = {first: k1, second: k2}
                            plan.append((len(arrays), k1 * nz + kz, core_rel, part, kz, rel))
                    arrays.append(buf)
        count = len(self.shapes)
        tall = {param: r for param, _, r, _ in place_of}

        def body(place, *refs):
            ins, outs = refs[: len(arrays)], refs[len(arrays) : len(arrays) + count]
            held, (sems, out_sems) = refs[len(arrays) + count : -2], refs[-2:]
            z, x, y, c = place[0], place[1], place[2], place[3]
            waits = [[] for _ in range(nz)]
            for i, j, core_rel, part, kz, rel in plan:
                zz = lax.rem(z - kz + nz, nz)
                xx = lax.rem(x - rel["x"] + nx, nx)
                yy = lax.rem(y - rel["y"] + ny, ny)
                cc = lax.rem(c + core_rel, 2)
                for param, row, r, col in place_of:
                    copy = pltpu.make_async_copy(
                        ins[i].at[j, pl.ds(row, r)],
                        held[param].at[zz, xx, yy, cc, :, pl.ds(col + part * q, q)],
                        sems.at[kz],
                    )
                    copy.start()
                    waits[kz].append(copy)
            after = []
            for kz in range(nz):
                for copy in waits[kz]:
                    copy.wait()
                zz = lax.rem(z - kz + nz, nz)
                for param in range(count):
                    copy = pltpu.make_async_copy(
                        held[param].at[zz], outs[param].at[zz], out_sems.at[kz]
                    )
                    copy.start()
                    after.append(copy)
            for copy in after:
                copy.wait()

        place = jnp.stack([self.grid.pos[a] for a in ("z", "x", "y", "c")]).astype(jnp.int32)
        devices = nz * nx * ny * 2
        room = sum(devices * (r + 8) * w * 2 for r, w in self.shapes)
        shapes = [(nz, nx, ny, 2, tall[i], w) for i, (_, w) in enumerate(self.shapes)]
        whole = pl.pallas_call(
            body,
            out_shape=[jax.ShapeDtypeStruct(s, bf16) for s in shapes],
            in_specs=[pl.BlockSpec(memory_space=pltpu.SMEM)]
            + [pl.BlockSpec(memory_space=pltpu.HBM)] * len(arrays),
            out_specs=[pl.BlockSpec(memory_space=pltpu.HBM)] * count,
            scratch_shapes=[pltpu.VMEM(s, bf16) for s in shapes]
            + [pltpu.SemaphoreType.DMA((nz,)), pltpu.SemaphoreType.DMA((nz,))],
            compiler_params=pltpu.CompilerParams(vmem_limit_bytes=room + (4 << 20)),
            cost_estimate=FREE,
            name="assemble",
        )(place, *arrays)
        return [
            w[:, :, :, :, :r].reshape(devices * r, width) for w, (r, width) in zip(whole, self.shapes)
        ]


def tail_of(r, q, keep):
    extra = r - keep
    return extra, keep // extra, q * extra // keep


def place_share(ref, value, row, col):
    r, q, keep = value.shape[1] // 2, value.shape[2], ref.shape[2] // 2
    if row or r <= keep:
        ref[0, :, row : row + 2 * r, col : col + q] = value
        return
    extra, count, w = tail_of(r, q, keep)
    for c in range(2):
        ref[0, :, c * keep : (c + 1) * keep, col : col + q] = value[:, c * r : c * r + keep]
        for j in range(count):
            at = c * keep + j * extra
            ref[0, :, at : at + extra, col + q : col + q + w] = value[
                :, c * r + keep : (c + 1) * r, j * w : (j + 1) * w
            ]


def weight_grad_body(grid_n, terms, scratch, pos_ref, *refs):
    nx, ny = grid_n
    outs = refs[4 * len(terms) :]
    keep_a, keep_b = outs[0], outs[1]
    away_a, away_b = outs[2 : 1 + ny], outs[1 + ny :]
    for i, (r2, q, row, col) in enumerate(terms):
        l0, l1, r0, r1 = refs[4 * i : 4 * i + 4]
        o = dot(l0[...], r0[...], TN) + dot(l1[...], r1[...], TN)
        o = o.reshape(nx, ny, r2, 2 * q)

        def split_y(y, o=o, row=row, col=col, q=q):
            place_share(keep_a, o[:, y, :, :q].astype(bf16), row, col)
            for k in range(1, ny):
                place_share(away_a[k - 1], o[:, (y + k) % ny, :, :q].astype(bf16), row, col)

        def split_x(x, o=o, row=row, col=col, q=q):
            place_share(keep_b, o[x, :, :, q:].astype(bf16), row, col)
            for k in range(1, nx):
                place_share(away_b[k - 1], o[(x + k) % nx, :, :, q:].astype(bf16), row, col)

        for y in range(ny):
            pl.when(pos_ref[2] == y)(functools.partial(split_y, y))
        for x in range(nx):
            pl.when(pos_ref[1] == x)(functools.partial(split_x, x))


class Scatter:
    def __init__(self, grid, terms, height, width):
        self.grid = grid
        n = grid.n
        nz, nx, ny = n["z"], n["x"], n["y"]
        self.place = jnp.stack([grid.pos[a] for a in ("z", "x", "y", "c")]).astype(jnp.int32)
        self.height, self.width = height, width
        specs, arrays, shapes = [], [], []
        self.parts = []
        for left, left_far, right, right_far, at, at_far, left_at, rows, half, row, col in terms:
            t, band = left.shape[0], rows // nz
            r2, q = band // (nx * ny), half // 2
            lspec = pl.BlockSpec((t, band), lambda i, p, left_at=left_at: (0, left_at + i))
            specs += [lspec, lspec]
            specs += [pl.BlockSpec((t, half), lambda i, p, at=at: (0, at + p[3]))]
            if at_far is None:
                specs += [pl.BlockSpec((t, half), lambda i, p: (0, 0))]
            else:
                specs += [pl.BlockSpec((t, half), lambda i, p, at=at_far: (0, at + p[3]))]
            arrays += [left, left_far, right, right_far]
            shapes.append((r2, q, row, col))
            self.parts.append((r2 // 2, q, row, col))
        a = jax.ShapeDtypeStruct((nz, nx, height, width), bf16)
        b = jax.ShapeDtypeStruct((nz, ny, height, width), bf16)
        sa = pl.BlockSpec((1, nx, height, width), lambda i, p: (i, 0, 0, 0))
        sb = pl.BlockSpec((1, ny, height, width), lambda i, p: (i, 0, 0, 0))
        sums = pl.pallas_call(
            functools.partial(weight_grad_body, (nx, ny), shapes, None),
            grid_spec=pltpu.PrefetchScalarGridSpec(
                num_scalar_prefetch=1,
                grid=(nz,),
                in_specs=specs,
                out_specs=[sa, sb] + [sa] * (ny - 1) + [sb] * (nx - 1),
            ),
            out_shape=[a, b] + [a] * (ny - 1) + [b] * (nx - 1),
            compiler_params=pltpu.CompilerParams(vmem_limit_bytes=56 << 20),
            cost_estimate=FREE,
            name="weight_grad",
        )(self.place, *arrays)
        self.keep = list(sums[:2])
        self.away = [list(sums[2 : 1 + ny]), list(sums[1 + ny :])]

    def state(self):
        names = ("keep", "away", "got", "more", "sent", "kept", "own", "back")
        return {k: v for k, v in vars(self).items() if k in names}

    def set_state(self, state):
        for k, v in state.items():
            setattr(self, k, v)

    def first(self):
        self.got = [
            [self.grid.send(v, "yx"[i], k) for k, v in enumerate(self.away[i], 1)] for i in range(2)
        ]
        del self.away

    def fold_second(self):
        g, n = self.grid, self.grid.n
        nz, counts = n["z"], (n["x"], n["y"])
        block = (nz, 1, self.height, self.width)
        specs, arrays, plan = [], [], []
        for i in range(2):
            for k in range(1, counts[i]):

                def place(_, p, i=i, k=k):
                    return (0, lax.rem(p[1 + i] + k, counts[i]), 0, 0)

                terms = [self.keep[i]] + self.got[i]
                plan.append(len(terms))
                arrays += terms
                specs += [pl.BlockSpec(block, place)] * len(terms)

        def body(pos, *refs):
            at = 0
            for j, count in enumerate(plan):
                total = refs[at][:, 0].astype(f32)
                for ref in refs[at + 1 : at + count]:
                    total = total + ref[:, 0].astype(f32)
                refs[len(arrays) + j][...] = total.astype(bf16)
                at += count

        shape = jax.ShapeDtypeStruct((nz, self.height, self.width), bf16)
        sent = pl.pallas_call(
            body,
            grid_spec=pltpu.PrefetchScalarGridSpec(
                num_scalar_prefetch=1,
                grid=(1,),
                in_specs=specs,
                out_specs=[pl.BlockSpec(shape.shape, lambda i, p: (0, 0, 0))] * len(plan),
            ),
            out_shape=[shape] * len(plan),
            compiler_params=pltpu.CompilerParams(vmem_limit_bytes=56 << 20),
            cost_estimate=FREE,
            name="fold_second",
        )(self.place, *arrays)
        self.sent = list(sent)

    def second(self):
        g, sent = self.grid, self.sent
        counts = (g.n["x"], g.n["y"])
        at = counts[0] - 1
        del self.sent
        self.more = [
            [g.send(sent[k - 1], "x", k) for k in range(1, counts[0])],
            [g.send(sent[at + k - 1], "y", k) for k in range(1, counts[1])],
        ]

    def fold_z(self):
        g, n = self.grid, self.grid.n
        nz, counts = n["z"], (n["x"], n["y"])
        h, w = self.height, self.width
        specs, arrays, plan = [], [], []
        for i in range(2):
            terms = [self.keep[i]] + self.got[i]
            specs += [
                pl.BlockSpec(
                    (1, 1, h, w), lambda s, p, i=i: (lax.rem(p[0] + s, nz), p[1 + i], 0, 0)
                )
            ] * len(terms)
            specs += [
                pl.BlockSpec((1, h, w), lambda s, p: (lax.rem(p[0] + s, nz), 0, 0))
            ] * len(self.more[i])
            arrays += terms + self.more[i]
            plan.append((len(terms), len(self.more[i])))

        def body(pos, *refs):
            at = 0
            for i, (wide, narrow) in enumerate(plan):
                total = refs[at][0, 0].astype(f32)
                for ref in refs[at + 1 : at + wide]:
                    total = total + ref[0, 0].astype(f32)
                for ref in refs[at + wide : at + wide + narrow]:
                    total = total + ref[0].astype(f32)
                at += wide + narrow
                for k in range(nz):

                    def put(k=k, i=i, total=total):
                        out = refs[len(arrays) + k]
                        out[:, i * w : (i + 1) * w] = total.astype(out.dtype)

                    pl.when(pl.program_id(0) == k)(put)

        sent = pl.pallas_call(
            body,
            grid_spec=pltpu.PrefetchScalarGridSpec(
                num_scalar_prefetch=1,
                grid=(nz,),
                in_specs=specs,
                out_specs=[pl.BlockSpec((h, 2 * w), lambda s, p: (0, 0))] * nz,
            ),
            out_shape=[jax.ShapeDtypeStruct((h, 2 * w), bf16 if k else f32) for k in range(nz)],
            compiler_params=pltpu.CompilerParams(vmem_limit_bytes=56 << 20),
            cost_estimate=FREE,
            name="fold_z",
        )(self.place, *arrays)
        self.sent = list(sent)
        del self.keep, self.got, self.more

    def along_z(self):
        sent = self.sent
        self.kept = [sent[0]] + [self.grid.send(v, "z", k) for k, v in enumerate(sent[1:], 1)]
        del self.sent

    def last(self):
        w = self.width
        shape = jax.ShapeDtypeStruct((self.height // 2, 2 * w), f32)
        rows = sorted({(row, min(r, self.height // 2)) for r, _, row, _ in self.parts})

        def body(pos, *refs):
            own, away = refs[-2], refs[-1]
            total = refs[0][...]
            for ref in refs[1:-2]:
                total = total + ref[...].astype(f32)

            def put(c):
                for row, r in rows:
                    to = slice(row // 2, row // 2 + r)
                    own[to] = total[row + c * r : row + c * r + r]
                    away[to] = total[row + (1 - c) * r : row + (1 - c) * r + r]

            for c in range(2):
                pl.when(pos[3] == c)(functools.partial(put, c))

        self.own, away = pl.pallas_call(
            body,
            in_specs=[pl.BlockSpec(memory_space=pltpu.SMEM)]
            + [pl.BlockSpec(memory_space=pltpu.VMEM)] * len(self.kept),
            out_specs=[pl.BlockSpec(memory_space=pltpu.VMEM)] * 2,
            out_shape=[shape, shape],
            compiler_params=pltpu.CompilerParams(vmem_limit_bytes=56 << 20),
            cost_estimate=FREE,
            name="fold_last",
        )(self.place, *self.kept)
        self.back = self.grid.send(away, "c", 1)
        del self.kept

    def results(self):
        w = self.width

        def body(pos, own, back, *outs):
            def put(c):
                for out, (r, q, row, col) in zip(outs, self.parts):
                    keep = r if row else min(r, self.height // 2)
                    rs = slice(row // 2, row // 2 + keep)
                    for half, ref in ((c, own), (1 - c, back)):
                        for part in range(2):
                            at, from_col = 2 * half * q + part * q, part * w + col
                            out[:keep, at : at + q] = ref[rs, from_col : from_col + q]
                            if keep == r:
                                continue
                            extra, count, wide = tail_of(r, q, keep)
                            for j in range(count):
                                to = at + j * wide
                                out[keep:, to : to + wide] = ref[
                                    j * extra : (j + 1) * extra, from_col + q : from_col + q + wide
                                ]

            for c in range(2):
                pl.when(pos[3] == c)(functools.partial(put, c))

        return pl.pallas_call(
            body,
            in_specs=[pl.BlockSpec(memory_space=pltpu.SMEM)]
            + [pl.BlockSpec(memory_space=pltpu.VMEM)] * 2,
            out_specs=[pl.BlockSpec(memory_space=pltpu.VMEM)] * len(self.parts),
            out_shape=[jax.ShapeDtypeStruct((r, 4 * q), f32) for r, q, _, _ in self.parts],
            compiler_params=pltpu.CompilerParams(vmem_limit_bytes=56 << 20),
            cost_estimate=FREE,
            name="fold_out",
        )(self.place, self.own, self.back)


def neighbours(grid, v):
    def move(u, by):
        pairs = [(i, i + by) for i in range(grid.total) if 0 <= i + by < grid.total]
        return lax.ppermute(u, AXES, pairs)

    left, right = move(v, 1), move(v, -1)
    lefts = move(jnp.concatenate([v, left], 0), 2)
    rights = move(jnp.concatenate([v, right], 0), -2)
    return v, left, right, lefts, rights


def layer_norm(inputs, scale_gain, offset_bias):
    centre = jnp.mean(inputs, axis=-1, keepdims=True)
    centred = inputs - centre
    spread = jnp.mean(centred * centred, axis=-1, keepdims=True)
    return centred * lax.rsqrt(spread + norm_eps) * scale_gain + offset_bias


def dot(a, b, dims=NN):
    return lax.dot_general(a, b, dims, preferred_element_type=f32)

def attend_body(q_ref, k_ref, v_ref, o_ref, lse_ref):
    t = q_ref.shape[0]
    first = lax.broadcasted_iota(jnp.int32, (t, 2 * HEAD), 1) < HEAD
    q, k, v = q_ref[...], k_ref[...], v_ref[...]
    out, totals = [], []
    for side in range(2):
        keep = first if side == 0 else jnp.logical_not(first)
        s = dot(q, jnp.where(keep, k, jnp.zeros_like(k)), NT)
        top = jnp.max(s, axis=-1, keepdims=True)
        p = jnp.exp((s - top) * HEAD ** -0.5)
        total = jnp.sum(p, axis=-1, keepdims=True)
        o = dot((p * (1.0 / total)).astype(bf16), jnp.where(keep, v, jnp.zeros_like(v)))
        out.append(o)
        totals.append(top * HEAD ** -0.5 + jnp.log(total))
    o_ref[...] = (out[0] + out[1]).astype(bf16)
    lse_ref[...] = jnp.where(first, totals[0], totals[1])

def attend(qkv):
    t, width = qkv.shape
    n = width // 3 // (2 * HEAD)
    spec = lambda off: pl.BlockSpec((t, 2 * HEAD), lambda i, off=off: (0, off * n + i))
    return pl.pallas_call(
        attend_body, grid=(n,),
        in_specs=[spec(0), spec(1), spec(2)],
        out_specs=[spec(0), spec(0)],
        out_shape=[jax.ShapeDtypeStruct((t, width // 3), bf16), jax.ShapeDtypeStruct((t, width // 3), f32)],
        compiler_params=pltpu.CompilerParams(vmem_limit_bytes=48 << 20),
        cost_estimate=FREE,
        name="attend",
    )(qkv, qkv, qkv)

def attend_back_body(q_ref, k_ref, v_ref, do_ref, lse_ref, dq_ref, dk_ref, dv_ref):
    t = q_ref.shape[0]
    first = lax.broadcasted_iota(jnp.int32, (t, 2 * HEAD), 1) < HEAD
    q, k, v, do = q_ref[...], k_ref[...], v_ref[...], do_ref[...]
    zero = jnp.zeros_like(k)
    dq = dk = dv = None
    for side in range(2):
        keep = first if side == 0 else jnp.logical_not(first)
        km, vm = jnp.where(keep, k, zero), jnp.where(keep, v, zero)
        qm, dom = jnp.where(keep, q, zero), jnp.where(keep, do, zero)
        lse = lse_ref[:, side * HEAD:side * HEAD + 1]
        p = jnp.exp(dot(q, km, NT) * HEAD ** -0.5 - lse)
        dp = dot(do, vm, NT)
        inner = jnp.sum(p * dp, axis=-1, keepdims=True)
        ds = (p * ((dp - inner) * HEAD ** -0.5)).astype(bf16)
        dq_ = dot(ds, km)
        dv_ = dot(dom, p.astype(bf16), TN)
        dk_ = dot(qm, ds, TN)
        dq = dq_ if dq is None else dq + dq_
        dv = dv_ if dv is None else dv + dv_
        dk = dk_ if dk is None else dk + dk_
    dq_ref[...] = dq.astype(bf16)
    dk_ref[...] = dk.T.astype(bf16)
    dv_ref[...] = dv.T.astype(bf16)

def attend_back(qkv, d_attended, lse):
    t, width = qkv.shape
    n = width // 3 // (2 * HEAD)
    spec = lambda off: pl.BlockSpec((t, 2 * HEAD), lambda i, off=off: (0, off * n + i))
    shape = jax.ShapeDtypeStruct((t, width // 3), bf16)
    return pl.pallas_call(
        attend_back_body, grid=(n,),
        in_specs=[spec(0), spec(1), spec(2), spec(0), spec(0)],
        out_specs=[spec(0)] * 3,
        out_shape=[shape] * 3,
        compiler_params=pltpu.CompilerParams(vmem_limit_bytes=48 << 20),
        cost_estimate=FREE,
        name="attend_back",
    )(qkv, qkv, qkv, d_attended, lse)

def gelu_parts(v):
    e = jnp.exp(-0.5 * v * v)
    t = 1.0 / (1.0 + (0.3275911 * 0.5 ** 0.5) * jnp.abs(v))
    poly = t * (0.127414796 + t * (-0.142248368 + t * (0.7107068705 + t * (-0.7265760135 + t * 0.5307027145))))
    tail = poly * e
    phi = jnp.where(v < 0, tail, 1.0 - tail)
    return v * phi, phi + v * (e * (2.0 * math.pi) ** -0.5)

def flat(ref):
    w = ref[...]
    return w.reshape(-1, w.shape[-1])

def joined_spec(joined, block):
    n, _, rows, d = joined.shape
    per = d // block
    return pl.BlockSpec((n, 1, rows, block), lambda i: (0, 1 + i // per, 0, i % per))

def mlp_in_body(n_ref, w_ref, b_ref, act_ref, slope_ref):
    v = dot(n_ref[...], flat(w_ref)) + b_ref[...]
    act, slope = gelu_parts(v)
    act_ref[...] = act.astype(bf16)
    slope_ref[...] = slope.astype(bf16)

def mlp_in(normed, w, bias, block=512):
    t, d = normed.shape
    ff = bias.shape[-1]
    out = pl.BlockSpec((t, block), lambda i: (0, i))
    shape = jax.ShapeDtypeStruct((t, ff), bf16)
    return pl.pallas_call(
        mlp_in_body, grid=(ff // block,),
        in_specs=[pl.BlockSpec((t, d), lambda i: (0, 0)), joined_spec(w, block), pl.BlockSpec((1, block), lambda i: (0, i))],
        out_specs=[out, out], out_shape=[shape, shape],
        compiler_params=pltpu.CompilerParams(vmem_limit_bytes=48 << 20),
        cost_estimate=FREE,
        name="mlp_in",
    )(normed, w, bias.reshape(1, -1))

def mlp_back_body(dy_ref, slope_ref, w1_ref, w2_ref, dpre_ref, db_ref, dn_ref):
    g = dot(dy_ref[...], w2_ref[...], NT) * slope_ref[...].astype(f32)
    low = g.astype(bf16)
    dpre_ref[...] = low
    db_ref[...] = jnp.sum(low.astype(f32), axis=0, keepdims=True)
    dn = dot(low, flat(w1_ref), NT)
    @pl.when(pl.program_id(0) == 0)
    def _(): dn_ref[...] = dn
    @pl.when(pl.program_id(0) > 0)
    def _(): dn_ref[...] += dn

def mlp_back(dy, slope, w1, w2, block=512):
    t, d = dy.shape
    ff = w2.shape[0]
    whole = pl.BlockSpec((t, d), lambda i: (0, 0))
    part = pl.BlockSpec((t, block), lambda i: (0, i))
    return pl.pallas_call(
        mlp_back_body, grid=(ff // block,),
        in_specs=[whole, part, joined_spec(w1, block), pl.BlockSpec((block, d), lambda i: (i, 0))],
        out_specs=[part, pl.BlockSpec((1, block), lambda i: (0, i)), whole],
        out_shape=[jax.ShapeDtypeStruct((t, ff), bf16), jax.ShapeDtypeStruct((1, ff), f32), jax.ShapeDtypeStruct((t, d), f32)],
        compiler_params=pltpu.CompilerParams(vmem_limit_bytes=48 << 20),
        cost_estimate=FREE,
        name="mlp_back",
    )(dy, slope, w1, w2)

def side_steps(x, side):
    n = x.shape[0]
    b = lax.rem(lax.broadcasted_iota(jnp.int32, x.shape, 0), side)
    before = jnp.where(b == 0, 0.0, pltpu.roll(x, 1, 0))
    after = jnp.where(b == side - 1, 0.0, pltpu.roll(x, n - 1, 0))
    return before, after

def up(x, by):
    return jnp.concatenate([jnp.zeros((by, x.shape[1]), x.dtype), x[:-by]], 0)

def down(x, by):
    return jnp.concatenate([x[by:], jnp.zeros((by, x.shape[1]), x.dtype)], 0)

def adapter_body(n_pieces, side, pos_ref, *refs):
    pieces, (w_ref, table_ref, dy_ref, proj_ref, spat_ref, rows_ref, dg_ref, dys_ref) = refs[:n_pieces], refs[n_pieces:]
    x = table_ref[BIAS_PROJ : BIAS_PROJ + 1]
    for k in range(n_pieces):
        x = x + dot(pieces[k][...], w_ref[lax.rem(pos_ref[0] - k + n_pieces, n_pieces)])
    proj_ref[...] = x
    before, after = side_steps(x, side)
    w = table_ref[DEPTH : DEPTH + 9]
    y = [before * w[3 * s:3 * s + 1] + x * w[3 * s + 1:3 * s + 2] + after * w[3 * s + 2:3 * s + 3] for s in range(3)]
    spatial = up(y[0], side) + y[1] + down(y[2], side) + table_ref[BIAS_DEPTH : BIAS_DEPTH + 1]
    spat_ref[...] = spatial
    rows_ref[...] = jnp.sum(spatial, axis=0, keepdims=True)
    dy = dy_ref[...].astype(f32)
    dg_ref[...] = jnp.sum(dy * spatial, axis=0, keepdims=True)
    dys_ref[...] = jnp.sum(dy, axis=0, keepdims=True)

def adapter(pos, pieces, w_proj, table, dy, side=PS, block=256):
    t, d = dy.shape
    n, width = len(pieces), pieces[0].shape[1]
    whole = pl.BlockSpec((t, width), lambda i: (0, 0))
    part = pl.BlockSpec((t, block), lambda i: (0, i))
    row = pl.BlockSpec((1, block), lambda i: (0, i))
    big, line = jax.ShapeDtypeStruct((t, d), f32), jax.ShapeDtypeStruct((1, d), f32)
    return pl.pallas_call(
        functools.partial(adapter_body, n, side), grid=(d // block,),
        in_specs=[pl.BlockSpec(memory_space=pltpu.SMEM)] + [whole] * n + [pl.BlockSpec((n, width, block), lambda i: (0, 0, i)), pl.BlockSpec((table.shape[0], block), lambda i: (0, i)), part],
        out_specs=[part, part, row, row, row], out_shape=[big, big, line, line, line],
        compiler_params=pltpu.CompilerParams(vmem_limit_bytes=48 << 20),
        cost_estimate=FREE,
        name="adapter",
    )(pos.reshape(1).astype(jnp.int32), *pieces, w_proj.reshape(n, width, d), table, dy)

def adapter_back_body(side, dy_ref, proj_ref, gate_ref, dr_ref, table_ref, dp_ref, dwd_ref, dbd_ref, dbp_ref):
    ds = dy_ref[...].astype(f32) * gate_ref[...] + dr_ref[...]
    dbd_ref[...] = jnp.sum(ds, axis=0, keepdims=True)
    before, after = side_steps(ds, side)
    w = table_ref[DEPTH : DEPTH + 9]
    y = [after * w[3 * s:3 * s + 1] + ds * w[3 * s + 1:3 * s + 2] + before * w[3 * s + 2:3 * s + 3] for s in range(3)]
    low = (down(y[0], side) + y[1] + up(y[2], side)).astype(bf16)
    dp_ref[...] = low
    dbp_ref[...] = jnp.sum(low.astype(f32), axis=0, keepdims=True)
    x = proj_ref[...]
    x_before, x_after = side_steps(x, side)
    for t, c in enumerate((x_before, x, x_after)):
        dwd_ref[t:t + 1] = jnp.sum(ds[side:] * c[:-side], axis=0, keepdims=True)
        dwd_ref[3 + t:4 + t] = jnp.sum(ds * c, axis=0, keepdims=True)
        dwd_ref[6 + t:7 + t] = jnp.sum(ds[:-side] * c[side:], axis=0, keepdims=True)

def adapter_back(dy, projected, gate, d_rows, table, side=PS, block=256):
    t, d = dy.shape
    part = pl.BlockSpec((t, block), lambda i: (0, i))
    row = pl.BlockSpec((1, block), lambda i: (0, i))
    nine = pl.BlockSpec((9, block), lambda i: (0, i))
    line = jax.ShapeDtypeStruct((1, d), f32)
    return pl.pallas_call(
        functools.partial(adapter_back_body, side), grid=(d // block,),
        in_specs=[part, part, row, row, pl.BlockSpec((table.shape[0], block), lambda i: (0, i))], out_specs=[part, nine, row, row],
        out_shape=[jax.ShapeDtypeStruct((t, d), bf16), jax.ShapeDtypeStruct((9, d), f32), line, line],
        compiler_params=pltpu.CompilerParams(vmem_limit_bytes=48 << 20),
        cost_estimate=FREE,
        name="adapter_back",
    )(dy, projected, gate, d_rows, table)


def rows_call(body, name, t, steps, ins, outs, sums):
    b = t // steps

    def spec(shape, by_rows):
        if by_rows:
            return pl.BlockSpec((b, shape[1]), lambda i: (i, 0))
        if len(shape) == 4:
            return pl.BlockSpec((shape[0], 1) + shape[2:], lambda i: (0, 0, 0, 0))
        return pl.BlockSpec(shape, lambda i: (0, 0))

    out_specs = [pl.BlockSpec((b, w), lambda i: (i, 0)) for w, _ in outs]
    shapes = [jax.ShapeDtypeStruct((t, w), dt) for w, dt in outs]
    if sums:
        out_specs.append(pl.BlockSpec(sums, lambda i: (0, 0)))
        shapes.append(jax.ShapeDtypeStruct(sums, f32))
    return pl.pallas_call(
        body,
        grid=(steps,),
        in_specs=[spec(a.shape, by_rows) for a, by_rows in ins],
        out_specs=out_specs,
        out_shape=shapes,
        compiler_params=pltpu.CompilerParams(vmem_limit_bytes=48 << 20),
        cost_estimate=FREE,
        name=name,
    )(*[a for a, _ in ins])


def add_sums(ref, values):
    total = jnp.concatenate([jnp.sum(v, axis=0, keepdims=True) for v in values], 0)

    @pl.when(pl.program_id(0) == 0)
    def _():
        ref[...] = total

    @pl.when(pl.program_id(0) > 0)
    def _():
        ref[...] += total


def norm_parts(x):
    centred = x - jnp.mean(x, axis=-1, keepdims=True)
    rstd = lax.rsqrt(jnp.mean(centred * centred, axis=-1, keepdims=True) + norm_eps)
    return centred * rstd, rstd


def norm_back(d_normed, x, gain):
    xhat, rstd = norm_parts(x)
    u = d_normed * gain
    shift = jnp.mean(u, axis=-1, keepdims=True)
    slope = jnp.mean(u * xhat, axis=-1, keepdims=True)
    return (u - shift - xhat * slope) * rstd, d_normed * xhat


def attn_out_norm(attended, w, x, table):
    def body(a_ref, w_ref, x_ref, t_ref, first_ref, n_ref):
        first = x_ref[...].astype(f32) + dot(a_ref[...], flat(w_ref)) + t_ref[BIAS_OUT : BIAS_OUT + 1]
        first_ref[...] = first
        xhat, _ = norm_parts(first)
        n_ref[...] = (
            xhat * t_ref[LN2_GAIN : LN2_GAIN + 1] + t_ref[LN2_BIAS : LN2_BIAS + 1]
        ).astype(bf16)

    t, d = x.shape
    ins = [(attended, True), (w, False), (x, True), (table, False)]
    return rows_call(body, "attn_out", t, 4, ins, [(d, f32), (d, bf16)], None)


def norm_two_back(d_normed2, first_sum, dy, table, w):
    def body(dn_ref, x_ref, dy_ref, t_ref, w_ref, first_ref, branch_ref, att_ref, sum_ref):
        dn = dn_ref[...]
        dx, scaled = norm_back(dn, x_ref[...], t_ref[LN2_GAIN : LN2_GAIN + 1])
        first = dy_ref[...].astype(f32) + dx
        low = first.astype(bf16)
        first_ref[...] = first
        branch_ref[...] = low
        att_ref[...] = dot(low, flat(w_ref), NT).astype(bf16)
        add_sums(sum_ref, (scaled, dn, low.astype(f32)))

    t, d = dy.shape
    ins = [(d_normed2, True), (first_sum, True), (dy, True), (table, False), (w, False)]
    return rows_call(body, "norm_two", t, 4, ins, [(d, f32), (d, bf16), (d, bf16)], (3, d))


def norm_one_back(parts, w, x, d_first, table):
    def body(q_ref, k_ref, v_ref, w_ref, x_ref, first_ref, t_ref, out_ref, sum_ref):
        d = x_ref.shape[1]
        q, k, v = q_ref[...], k_ref[...], v_ref[...]
        dn = dot(q, w_ref[:, :d], NT) + dot(k, w_ref[:, d : 2 * d], NT) + dot(v, w_ref[:, 2 * d :], NT)
        dx, scaled = norm_back(dn, x_ref[...].astype(f32), t_ref[LN1_GAIN : LN1_GAIN + 1])
        out_ref[...] = (first_ref[...] + dx).astype(bf16)
        add_sums(sum_ref, (scaled, dn, q.astype(f32), v.astype(f32)))

    t, d = x.shape
    ins = [(p, True) for p in parts] + [(w, False), (x, True), (d_first, True), (table, False)]
    return rows_call(body, "norm_one", t, 4, ins, [(d, bf16)], (4, d))


def columns_call(body, name, block, ins, width, dtype):
    t = ins[0][0].shape[0]

    def spec(shape, by_columns):
        if by_columns:
            return pl.BlockSpec((shape[0], block), lambda i: (0, i))
        return pl.BlockSpec(shape, lambda i: (0, 0))

    return pl.pallas_call(
        body,
        grid=(width // block,),
        in_specs=[spec(a.shape, by) for a, by in ins],
        out_specs=pl.BlockSpec((t, block), lambda i: (0, i)),
        out_shape=jax.ShapeDtypeStruct((t, width), dtype),
        compiler_params=pltpu.CompilerParams(vmem_limit_bytes=48 << 20),
        cost_estimate=FREE,
        name=name,
    )(*[a for a, _ in ins])


def project(normed, w, bias):
    def body(n_ref, w_ref, b_ref, out_ref):
        out_ref[...] = (dot(n_ref[...], w_ref[...]) + b_ref[...]).astype(bf16)

    ins = [(normed, False), (w, True), (bias, True)]
    return columns_call(body, "project", 512, ins, w.shape[1], bf16)


def layer_output(activation, w, first_sum, table, gate, spatial):
    def body(a_ref, w_ref, x_ref, t_ref, g_ref, s_ref, out_ref):
        total = x_ref[...] + dot(a_ref[...], w_ref[...]) + t_ref[BIAS_FC2 : BIAS_FC2 + 1]
        out_ref[...] = (total + g_ref[...] * s_ref[...]).astype(bf16)

    ins = [(activation, False), (w, True), (first_sum, True), (table, True), (gate, True), (spatial, True)]
    return columns_call(body, "layer_output", 256, ins, w.shape[1], bf16)


def dot3(x, w, dims=NN):
    a = x.astype(bf16)
    rest = x - a.astype(f32)
    b = rest.astype(bf16)
    c = (rest - b.astype(f32)).astype(bf16)
    return dot(a, w, dims) + dot(b, w, dims) + dot(c, w, dims)


def gate_body(n_near, tokens, d, *refs):
    near_refs, refs = refs[:n_near], refs[n_near:]
    win_ref, wout_ref, gate_ref, drows_ref, pack_ref, sum_ref = refs
    near = [ref[i : i + 1] for ref in near_refs for i in range(ref.shape[0])]
    n_near = len(near)
    own = near[0][:, 2 * d :]
    match = [(near[i][:, 2 * d :] == own).astype(f32) for i in range(n_near)]
    count = functools.reduce(lambda a, b: a + b, match)[:, :1] * tokens
    rows = d_gates = None
    for i in range(n_near):
        weight = match[i][:, :1]
        row, d_gate = weight * near[i][:, :d], weight * near[i][:, d : 2 * d]
        rows = row if i == 0 else rows + row
        d_gates = d_gate if i == 0 else d_gates + d_gate
    second = lax.broadcasted_iota(jnp.int32, (8, d), 0) == 1
    mean = jnp.broadcast_to(rows / count, (8, d))
    d_gate = jnp.where(second, jnp.broadcast_to(d_gates, (8, d)), jnp.broadcast_to(near[0][:, d : 2 * d], (8, d)))
    win, wout = win_ref[...], wout_ref[...]
    act, slope = gelu_parts(dot3(mean, win))
    gate = jnp.tanh(dot3(act, wout, NT))
    d_pre = d_gate * (1.0 - gate * gate)
    d_hidden = dot3(d_pre, wout) * slope
    d_mean = dot3(d_hidden, win, NT)
    gate_ref[...] = gate[:1]
    drows_ref[...] = d_mean[1:2] / count
    sum_ref[...] = jnp.zeros((1, 128), f32) + jnp.sum(gate[:1])
    at = 0
    for v, order in ((mean, (0, 0, 1)), (d_pre, (0, 0, 1)), (d_hidden, (0, 1, 0)), (act, (0, 1, 0))):
        line = jnp.broadcast_to(v[:1], v.shape)
        high = line.astype(bf16)
        low = (line - high.astype(f32)).astype(bf16)
        place = lax.broadcasted_iota(jnp.int32, v.shape, 0)
        kind = jnp.where(place == 1, order[1], jnp.where(place == 2, order[2], 0))
        pick = jnp.where(kind == 1, low.astype(f32), high.astype(f32))
        pack_ref[:, at : at + v.shape[1]] = jnp.where(place < 3, pick, 0.0).astype(bf16)
        at += v.shape[1]


def gate_step(near, gates, d, hidden, tokens):
    n = len(near)

    def line(k):
        return jax.ShapeDtypeStruct((1, k), f32)

    def at(k):
        return pl.BlockSpec((1, k), lambda j: (0, 0))

    k = 2 * d + 2 * hidden
    return pl.pallas_call(
        functools.partial(gate_body, n, tokens, d),
        grid=(1,),
        in_specs=[pl.BlockSpec(v.shape, lambda j: (0, 0)) for v in near]
        + [pl.BlockSpec((d, hidden), lambda j, b=b: (0, b)) for b in range(2)],
        out_specs=[at(d), at(d), pl.BlockSpec((8, k), lambda j: (0, 0)), at(128)],
        out_shape=[line(d), line(d), jax.ShapeDtypeStruct((8, k), bf16), line(128)],
        compiler_params=pltpu.CompilerParams(vmem_limit_bytes=32 << 20),
        cost_estimate=FREE,
        name="gate",
    )(*near, gates, gates)


def pool_table(coarse_side, fine_side):
    coarse, fine = np.arange(coarse_side)[:, None], np.arange(fine_side)[None]
    start = coarse * fine_side // coarse_side
    end = ((coarse + 1) * fine_side + coarse_side - 1) // coarse_side
    single = np.where((fine >= start) & (fine < end), 1.0, 0.0) / (end - start)
    return np.kron(single, single)


def token_sum(values):
    return jnp.sum(values.astype(f32), axis=0)


def shards(
    tokens,
    features,
    sample_of,
    cotangent,
    ln1_gain,
    ln1_bias,
    w_qkv,
    bias_qv,
    w_attn_out,
    bias_attn_out,
    ln2_gain,
    ln2_bias,
    w_fc1,
    bias_fc1,
    w_fc2,
    bias_fc2,
    w_proj,
    bias_proj,
    w_depth,
    bias_depth,
    w_gate_in,
    w_gate_out,
):
    grid = Grid()
    rows = ln1_gain.shape[0]
    total = grid.total
    x, dy = tokens[0], cotangent[0]
    count, d = x.shape
    hidden = w_gate_in.shape[1]

    vectors = [ln1_gain, ln1_bias, bias_attn_out, ln2_gain, ln2_bias, bias_fc2, bias_proj, bias_depth]
    a_small = GatherSmall(
        grid, jnp.concatenate(vectors + [w_depth.reshape(-1), bias_qv, bias_fc1])
    )
    gate_out_rows = dot(jnp.eye(rows, dtype=bf16), w_gate_out, NT).astype(bf16)
    gates = jnp.concatenate([w_gate_in, gate_out_rows], 1)
    gate_out_rows = dot(jnp.eye(rows, dtype=bf16), w_gate_out, NT).astype(bf16)
    gates = jnp.concatenate([w_gate_in, gate_out_rows], 1)
    full_qkv = lax.all_gather(w_qkv, AXES, axis=0, tiled=True)
    joined = lax.all_gather(
        jnp.concatenate([w_attn_out] + [w_fc1[:, i : i + d] for i in range(0, w_fc1.shape[1], d)], 0),
        AXES,
    )
    joined = joined.reshape(total, -1, rows, d)
    if rows % 16:
        joined = joined.transpose(1, 0, 2, 3).reshape(1, -1, d, d)
    mixed_shard = jnp.concatenate([gates, w_proj], 0)
    a_qkv, a_fc2 = Gather(grid, (w_qkv,)), Gather(grid, (w_fc2,))

    n_ch = lax.axis_size("ch")
    ch = lax.axis_index("ch")
    n_img, own_ch = features.shape[0], features.shape[1]
    core = grid.pos["c"]

    def along_ch(v, by):
        img = lax.axis_size("img")
        pairs = [
            (i * n_ch + j, i * n_ch + (j + by) % n_ch) for i in range(img) for j in range(n_ch)
        ]
        return lax.ppermute(v, AXES, pairs)

    def peer(v):
        return grid.send(v, "c", 1)

    def peer_half(v):
        h = v.shape[1] // 2
        return grid.send(lax.dynamic_slice(v, (0, (1 - core) * h), (v.shape[0], h)), "c", 1)

    def step(active, *values):
        states, values = lax.optimization_barrier(([a.state() for a in active], values))
        for a, state in zip(active, states):
            a.set_state(state)
        return values

    a_qkv.along_z()
    for _ in range(3):
        a_small.next()
    pool = jnp.asarray(pool_table(PS, FS), bf16)
    pooled_own = dot(pool, features.reshape(n_img * own_ch, -1), NT).astype(bf16)
    a_qkv.pack_first()
    a_small.v, pooled_own = step((a_qkv,), a_small.v, pooled_own)

    a_qkv.first()
    a_qkv.pack_second()
    while a_small.next():
        pass
    every, pooled_own = step((a_qkv, a_fc2), a_small.v, pooled_own)

    a_qkv.second()
    a_fc2.along_z()
    a_fc2.pack_first()
    every = every.astype(f32)
    table = every[:, : LINES * rows].reshape(total, LINES, rows)
    table = table.transpose(1, 0, 2).reshape(LINES, d)
    at = LINES * rows
    full_bias_qv = every[:, at : at + 2 * rows].reshape(-1)
    full_bias_fc1 = every[:, at + 2 * rows :].reshape(1, -1)
    bias_qkv = jnp.concatenate([full_bias_qv[:d], jnp.zeros((d,), f32), full_bias_qv[d:]])[None]
    x32 = x.astype(f32)
    normed1 = layer_norm(x32, table[LN1_GAIN], table[LN1_BIAS]).astype(bf16)
    cuts = []
    for k in range(n_ch):
        to = lax.rem(ch + k, n_ch)
        cuts.append(lax.dynamic_slice(pooled_own, (0, to * own_ch), (count, own_ch)))
    normed1, table, full_bias_fc1, bias_qkv, cuts = step(
        (a_qkv, a_fc2), normed1, table, full_bias_fc1, bias_qkv, cuts
    )

    a_qkv.early()
    a_qkv.cross()
    dy_far = peer_half(dy)
    normed1, cuts, dy_far = step((a_qkv, a_fc2), normed1, cuts, dy_far)

    def pooled_piece(k):
        return along_ch(cuts[k], k) if k else cuts[k]

    a_fc2.first()
    early = n_ch // 2 + 1
    pieces = [pooled_piece(k) for k in range(early)]
    (full_qkv,) = a_qkv.whole()
    qkv = project(normed1, full_qkv, bias_qkv)
    attended, log_total = attend(qkv)
    a_fc2.s0, a_fc2.r1, attended = lax.optimization_barrier((a_fc2.s0, a_fc2.r1, attended))
    a_fc2.pack_second()
    attended, log_total, pieces, cuts, full_qkv, mixed_shard = step(
        (a_fc2,), attended, log_total, pieces, cuts, full_qkv, mixed_shard
    )

    mixed_w = lax.all_gather(mixed_shard, AXES)
    a_fc2.second()
    a_fc2.early()
    attended_far = peer(attended)
    first_sum, normed2 = attn_out_norm(attended, joined, x, table)
    activation, slope = mlp_in(normed2, joined, full_bias_fc1)
    activation, slope, normed2, first_sum, cuts, attended_far = step(
        (a_fc2,), activation, slope, normed2, first_sum, cuts, attended_far
    )

    activation_far = peer(activation)
    pieces = pieces + [pooled_piece(k) for k in range(early, n_ch)]
    pooled = jnp.zeros((count, n_ch * own_ch), bf16)
    for k in range(n_ch):
        from_ch = lax.rem(ch - k + n_ch, n_ch)
        pooled = lax.dynamic_update_slice(pooled, pieces[k], (0, from_ch * own_ch))
    activation_far, normed2, slope, attended, pieces, pooled = step(
        (a_fc2,), activation_far, normed2, slope, attended, pieces, pooled
    )

    a_fc2.cross()
    normed2_far = peer(normed2)
    ff = activation.shape[1]
    s_one = Scatter(
        grid,
        [(activation, activation_far, dy, dy_far, 0, None, 0, ff, d // 2, 0, 0)],
        2 * ff // total,
        d // 4,
    )
    a_fc2.c2, s_one.away = lax.optimization_barrier((a_fc2.c2, s_one.away))
    (full_fc2,) = a_fc2.whole()
    slope, attended, pieces, full_fc2, normed2_far = step(
        (s_one,), slope, attended, pieces, full_fc2, normed2_far
    )

    s_one.first()
    d_pre, d_bias_fc1, d_normed2 = mlp_back(dy, slope, joined, full_fc2)
    d_first, d_branch, d_attended, sums_two = norm_two_back(
        d_normed2, first_sum, dy, table, joined
    )
    s_one.got, d_attended = lax.optimization_barrier((s_one.got, d_attended))
    s_one.fold_second()
    d_attended, d_first, d_branch, d_pre, full_fc2, attended, pieces = step(
        (s_one,), d_attended, d_first, d_branch, d_pre, full_fc2, attended, pieces
    )

    s_one.second()
    d_pre_far, d_branch_far = peer_half(d_pre), peer_half(d_branch)
    full_gates = mixed_w[:, :rows].reshape(d, 2 * hidden)
    full_proj = mixed_w[:, rows:].reshape(-1, d)
    projected, spatial, row_sums, d_gate, dy_sum = adapter(ch, pieces, full_proj, table, dy)
    ids_plus = sample_of.astype(f32) + 1.0
    carried = jnp.concatenate(
        [row_sums, d_gate, jnp.broadcast_to(ids_plus[:, None], (1, 128))], 1
    )
    s_one.more, carried = lax.optimization_barrier((s_one.more, carried))
    s_one.fold_z()
    d_attended, d_branch, d_pre, d_pre_far, d_branch_far, carried, full_gates, full_proj = step(
        (s_one,), d_attended, d_branch, d_pre, d_pre_far, d_branch_far, carried, full_gates, full_proj
    )

    near = neighbours(grid, carried)
    s_two = Scatter(
        grid,
        [
            (normed2, normed2_far, d_pre, d_pre_far, 0, None, 0, d, ff // 2, 0, 0),
            (attended, attended_far, d_branch, d_branch_far, 0, None, 0, d, d // 2, 0, ff // 4),
        ],
        2 * rows,
        (ff + d) // 4,
    )
    d_attended, normed1, near = step((s_one, s_two), d_attended, normed1, near)

    s_two.first()
    s_one.along_z()
    d_query, d_key, d_value = attend_back(qkv, d_attended, log_total)
    gate, d_rows, pack, gate_sum = gate_step(near, full_gates, d, hidden, count)
    d_projected, d_depth, d_bias_depth, d_bias_proj = adapter_back(
        dy, projected, gate, d_rows, table
    )
    s_two.got, d_query, d_projected = lax.optimization_barrier((s_two.got, d_query, d_projected))
    s_two.fold_second()
    d_query, d_key, d_value, normed1, pack, d_projected, gate, pooled = step(
        (s_one, s_two), d_query, d_key, d_value, normed1, pack, d_projected, gate, pooled
    )

    d_mixed = jnp.concatenate([d_query, d_key, d_value], -1)
    d_mixed_far, normed1_far, pooled_far = peer_half(d_mixed), peer(normed1), peer(pooled)
    pack_far, d_projected_far = peer(pack), peer_half(d_projected)
    d_pooled = dot(d_projected, full_proj, NT).astype(bf16)
    d_mixed, d_mixed_far, normed1_far, pooled_far, pack_far, d_projected_far, d_pooled = step(
        (s_two,),
        d_mixed,
        d_mixed_far,
        normed1_far,
        pooled_far,
        pack_far,
        d_projected_far,
        d_pooled,
    )

    s_two.second()
    lines = jnp.concatenate([sums_two[2:], sums_two[:2], dy_sum, d_bias_proj, d_bias_depth, d_depth], 0)
    lines = lines.reshape(LINES - 2, total, rows).transpose(1, 0, 2).reshape(total, -1)
    small = jnp.concatenate(
        [lines, d_bias_fc1.reshape(total, -1), jnp.broadcast_to(gate_sum, (total, 128))], 1
    )
    later = n_ch // 2
    back = []
    for k in range(n_ch):
        to = lax.rem(ch + k, n_ch)
        piece = lax.dynamic_slice(d_pooled, (0, to * own_ch), (count, own_ch))
        back.append(along_ch(piece, k) if k not in (0, later) else piece)
    wide, low = 3 * d // 4, hidden // 4
    half = d // (hidden // 2)
    s_three = Scatter(
        grid,
        [
            (normed1, normed1_far, d_mixed, d_mixed_far, 0, None, 0, d, 3 * d // 2, 0, 0),
            (pack, pack_far, pack, pack_far, 2 * half, 2 * half, 0, d, hidden // 2, 0, wide),
            (
                pack,
                pack_far,
                pack,
                pack_far,
                2 * half + 2,
                2 * half + 2,
                grid.n["z"],
                d,
                hidden // 2,
                0,
                wide + low,
            ),
            (
                pooled,
                pooled_far,
                d_projected,
                d_projected_far,
                0,
                None,
                0,
                pooled.shape[1],
                d // 2,
                0,
                wide + 2 * low,
            ),
        ],
        2 * rows,
        wide + 2 * low + pooled.shape[1] // 4,
    )
    s_two.more, s_three.away = lax.optimization_barrier((s_two.more, s_three.away))
    s_two.fold_z()
    d_query, d_key, d_value, activation, back, small = step(
        (s_one, s_two, s_three), d_query, d_key, d_value, activation, back, small
    )

    s_three.first()
    s_two.along_z()
    grad_tokens, sums_one = norm_one_back(
        (d_query, d_key, d_value), full_qkv, x, d_first, table
    )
    layer_out = layer_output(activation, full_fc2, first_sum, table, gate, spatial)
    s_three.got, layer_out, grad_tokens = lax.optimization_barrier(
        (s_three.got, layer_out, grad_tokens)
    )
    s_three.fold_second()
    layer_out, grad_tokens, sums_one, small, back = step(
        (s_one, s_two, s_three), layer_out, grad_tokens, sums_one, small, back
    )

    s_three.second()
    ones = sums_one[:2].reshape(2, total, rows).transpose(1, 0, 2).reshape(total, -1)
    d_bias_qv = sums_one[2:].reshape(total, -1)
    s_small = ScatterSmall(grid, jnp.concatenate([ones, small, d_bias_qv], 1))
    s_one.last()
    s_two.last()
    s_small.next()
    s_small.next()
    s_three.fold_z()
    s_small.v, back = step((s_one, s_two, s_three), s_small.v, back)

    s_three.along_z()
    back[later] = along_ch(back[later], later)
    while s_small.left:
        s_small.next()
    (g_fc2,) = s_one.results()
    g_fc1, g_attn_out = s_two.results()
    s_small.v, back, g_fc2, g_fc1 = step((s_three,), s_small.v, back, g_fc2, g_fc1)

    d_local = jnp.zeros((n_img, count, own_ch), bf16)
    for k in range(n_ch):
        from_ch = lax.rem(ch - k + n_ch, n_ch)
        d_local = lax.dynamic_update_slice(d_local, back[k][None], (from_ch, 0, 0))
    grad_features = jnp.einsum("kpc,pf->kcf", d_local, pool, preferred_element_type=f32).astype(bf16)
    s_three.last()
    summed = s_small.v[0]
    gate_mean = summed[-2 * rows - 1] / (total * d)
    g_qkv, g_gate_in, g_gate_out, g_proj = s_three.results()

    def owned(i):
        return summed[i * rows : (i + 1) * rows]

    return (
        layer_out[None],
        grad_tokens[None],
        grad_features,
        owned(LN1_GAIN),
        owned(LN1_BIAS),
        g_qkv,
        summed[-2 * rows :],
        g_attn_out,
        owned(BIAS_OUT),
        owned(LN2_GAIN),
        owned(LN2_BIAS),
        g_fc1,
        summed[at : at + 4 * rows],
        g_fc2,
        owned(BIAS_FC2),
        g_proj,
        owned(BIAS_PROJ),
        summed[DEPTH * rows : at].reshape(9, rows),
        owned(BIAS_DEPTH),
        g_gate_in,
        g_gate_out.T,
        gate_mean,
    )


def solution(mesh):
    return jax.shard_map(
        shards,
        mesh=mesh,
        in_specs=(
            P(("img", "ch"), None, None),
            P("img", "ch", None),
            P(("img", "ch")),
            P(("img", "ch"), None, None),
            P(("img", "ch")),
            P(("img", "ch")),
            P(("img", "ch"), None),
            P(("img", "ch")),
            P(("img", "ch"), None),
            P(("img", "ch")),
            P(("img", "ch")),
            P(("img", "ch")),
            P(("img", "ch"), None),
            P(("img", "ch")),
            P(("img", "ch"), None),
            P(("img", "ch")),
            P(("img", "ch"), None),
            P(("img", "ch")),
            P(None, ("img", "ch")),
            P(("img", "ch")),
            P(("img", "ch"), None),
            P(None, ("img", "ch")),
        ),
        out_specs=(
            P(("img", "ch"), None, None),
            P(("img", "ch"), None, None),
            P("img", "ch", None),
            P(("img", "ch")),
            P(("img", "ch")),
            P(("img", "ch"), None),
            P(("img", "ch")),
            P(("img", "ch"), None),
            P(("img", "ch")),
            P(("img", "ch")),
            P(("img", "ch")),
            P(("img", "ch"), None),
            P(("img", "ch")),
            P(("img", "ch"), None),
            P(("img", "ch")),
            P(("img", "ch"), None),
            P(("img", "ch")),
            P(None, ("img", "ch")),
            P(("img", "ch")),
            P(("img", "ch"), None),
            P(None, ("img", "ch")),
            P(),
        ),
        check_vma=False,
    )
```
